128 devices in a mesh: row: 8 (over x, core), col: 16 (over y, z).
Axes of the slice: x: 4, y: 4, z: 4, core: 2. Of those that a mesh axis runs over, the one named last changes fastest.
Arguments:
- blocks_a: bfloat16 [64, 256, 138, 138], P('row', 'col'), may hold values from -6 to 6
- pattern_a: int32 [64, 256], P('row', 'col'), may hold values 0 or 1
- blocks_b: bfloat16 [256, 16, 138, 138], P('col'), may hold values from -0.0625 to 0.0625
- filter_mask: int32 [64, 16], P('row', 'col'), may hold values 0 or 1
- task_brick: int32 [64, 16], P('row', 'col'), may hold values from 0 to 127
- basis_rows: bfloat16 [64, 138, 16384], P('row'), may hold values from -0.5 to 0.5
- basis_cols: bfloat16 [16, 138, 16384], P('col'), may hold values from -0.5 to 0.5
- kernel: float32 [1024, 2048], P(('row', 'col')), may hold values from 0.1 to 10
Outputs:
- density: bfloat16 [64, 16, 138, 138], P('row', 'col')
- potential: float32 [1024, 2048], P('row', 'col')
The draws below stay inside these ranges and needn't reach their ends.
Inputs may be any that keep to these rules, and one draw needn't show every extreme that they name: `pattern_a`: 1 marks a block that is kept. `filter_mask`: 1 marks a product block that is kept. `task_brick`: brick number as in the reference program.
All inputs are finite; a program needn't handle non-finite values.
Results may differ from the reference program's by a relative error of at most 0.0028.
Values may be sent and summed in bfloat16 or wider, within the bound.
No kernel may reach another device: no remote copies, remote signals or barrier semaphores. Data moves between devices by JAX's collectives and lax.ppermute only.
A program may use at most 576 MiB of HBM per device.

```python
import math
import jax
import jax.numpy as jnp
import numpy as np
from jax import lax

BS = 138
BY = 128
BX = 128
NI = 64
NK = 256
NJ = 16
GRID_Y = 1024
GRID_X = 2048
N_ROW = 8
N_COL = 16


def with_ends(array, own_key, smallest, high):
    longest = array.shape.index(max(array.shape))
    spots = []
    for shift in (0, 1):
        where = [jax.random.randint(jax.random.fold_in(own_key, axis), (), 0, length) for axis, length in enumerate(array.shape)]
        where[longest] = (where[longest] + shift) % array.shape[longest]
        spots.append(tuple(where))
    return array.at[spots[0]].set(smallest).at[spots[1]].set(high)


def with_spikes(entries, own_key, source, target, shards_of, factor):
    owner, partner = [(jnp.arange(entries.shape[axis_at]) // (entries.shape[axis_at] // shards_of)).reshape([-1 if axis == axis_at else 1 for axis in range(entries.ndim)]) for axis_at in (source, target)]
    chosen = jax.random.permutation(own_key, shards_of)[partner]
    strong = (owner == chosen) | (owner == (partner + shards_of // 2) % shards_of)
    return jnp.where(strong, factor * entries, entries)


def block_levels(stream_key, shape, shards, smallest, largest):
    def one(dim, shards_of):
        steps = jax.random.uniform(jax.random.fold_in(jax.random.fold_in(stream_key, 6), dim), (shards_of,), jnp.float32, smallest / len(shards), largest / len(shards))
        return jnp.repeat(jnp.exp(steps), shape[dim] // shards_of).reshape((-1,) + (1,) * (len(shape) - dim - 1))

    gain = one(*shards[0])
    for cut in shards[1:]:
        gain = gain * one(*cut)
    return gain


def rank_table(amount, skew):
    loads = [(1 << 20) // math.isqrt(grade ** skew) + 1 for grade in range(1, amount + 1)]
    width = 1 + sum(loads) // (1 << 30)
    return np.cumsum(np.array([max(1, weight // width) for weight in loads]))


def ranked(own_key, extent, amount, lean):
    table = rank_table(amount, lean)
    ticket = jax.random.randint(jax.random.fold_in(own_key, 1), extent, 0, int(table[amount - 1]))
    grade = jnp.searchsorted(jnp.asarray(table, jnp.int32), ticket, side="right")
    return jax.random.permutation(jax.random.fold_in(own_key, 2), amount)[grade].astype(jnp.int32)


def gaussian(key, dims, deviation, most, pieces=(), kind=jnp.bfloat16):
    array = jax.random.normal(key, dims, jnp.float32) * deviation
    if len(pieces) > 0:
        array = block_levels(key, dims, pieces, -0.22, 0.18) * array
    return jnp.clip(array, min=-most, max=most).astype(kind)


def heavy_noise(stream_key, extent, scale, reach, cuts, heavy, kind=jnp.bfloat16):
    array = scale * jax.random.normal(stream_key, extent, jnp.float32)
    if cuts:
        array = array * block_levels(stream_key, extent, cuts, -0.22, 0.18)
    return jnp.clip(with_spikes(array, jax.random.fold_in(stream_key, 3), *heavy), -reach, reach).astype(kind)


def setup_inputs(seed: int = 0) -> dict:
    key_list = jax.random.split(jax.random.key(seed), 9)
    return {
        "blocks_a": gaussian(key_list[0], (NI, NK, BS, BS), 1.0, 6.0, ((0, 8), (1, 16))),
        "pattern_a": with_ends((jax.random.randint(key_list[1], (NI, NK), 0, 2) < 1).astype(jnp.int32), jax.random.fold_in(key_list[1], 1), 0, 1),
        "blocks_b": heavy_noise(key_list[2], (NK, NJ, BS, BS), (BS * NK // 2) ** -0.5, 0.0625, ((0, 16),), (0, 1, 16, 2.0)),
        "filter_mask": with_ends((jax.random.randint(key_list[3], (NI, NJ), 0, 4) < 3).astype(jnp.int32), jax.random.fold_in(key_list[3], 1), 0, 1),
        "task_brick": with_ends(ranked(key_list[4], (NI, NJ), N_ROW * N_COL, 2), jax.random.fold_in(key_list[4], 3), 0, (N_ROW * N_COL) - 1).astype(jnp.int32),
        "basis_rows": gaussian(key_list[5], (NI, BS, BY * BX), BS ** -0.5, 0.5, ((0, 8),)),
        "basis_cols": gaussian(key_list[6], (NJ, BS, BY * BX), BS ** -0.5, 0.5, ((0, 16),)),
        "kernel": jnp.clip(jnp.exp(math.log(10.0) - 4.6051702 * jax.random.uniform(key_list[7], (GRID_Y, GRID_X), jnp.float32) ** block_levels(key_list[7], (GRID_Y, GRID_X), ((0, 128),), -0.2, 0.2)), 0.1, 10.0),
    }


def reference(blocks_a, pattern_a, blocks_b, filter_mask, task_brick, basis_rows, basis_cols, kernel):
    masked = blocks_a * pattern_a[:, :, None, None].astype(jnp.bfloat16)
    right_factor = blocks_b.astype(jnp.float32)

    def block_row(row_blocks):
        return jnp.einsum("kab,kjbc->jac", row_blocks.astype(jnp.float32), right_factor)

    product = lax.map(block_row, masked)
    density = (product * filter_mask[:, :, None, None].astype(jnp.float32)).astype(jnp.bfloat16)
    column_basis = basis_cols.astype(jnp.float32)

    def collocate(paired):
        row_density, row_basis = paired
        inner = jnp.einsum("jab,jbg->jag", row_density.astype(jnp.float32), column_basis)
        return jnp.sum(inner * row_basis.astype(jnp.float32)[None], axis=1)

    contribution = lax.map(collocate, (density, basis_rows))
    devices = N_ROW * N_COL
    owners = task_brick.reshape(-1)
    onehot = (owners[None, :] == jnp.arange(devices, dtype=jnp.int32)[:, None]).astype(jnp.float32)
    bricks = jnp.dot(onehot, contribution.reshape(NI * NJ, BY * BX), precision=lax.Precision.HIGHEST)
    grid = bricks.reshape(N_ROW, N_COL, BY, BX).transpose(0, 2, 1, 3).reshape(N_ROW * BY, N_COL * BX)
    spectrum = jnp.fft.fft(grid, axis=1)
    potential = jnp.real(jnp.fft.ifft(kernel * spectrum, axis=1)).astype(jnp.float32)
    return density, potential
```

```python
import functools
import math

import jax
import jax.numpy as jnp
import numpy as np
from jax import lax
from jax.experimental import pallas as pl
from jax.experimental.pallas import tpu as pltpu
from jax.sharding import PartitionSpec as P

BS = 138
PAD = 144
MIB = 1 << 20
HIGH = lax.Precision.HIGHEST


def collocate_kernel(count, density, cols, rows, out, stacked):
    @pl.when(pl.program_id(0) == 0)
    def _():
        for i in range(count):
            stacked[i * PAD : i * PAD + BS, :] = density[i]

    for t in range(4):
        lanes = slice(t * 256, (t + 1) * 256)
        inner = jnp.dot(stacked[...], cols[0, :, lanes], preferred_element_type=jnp.float32)
        for i in range(count):
            part = inner[i * PAD : i * PAD + BS] * rows[i, :, lanes].astype(jnp.float32)
            line = jnp.sum(part, axis=0, keepdims=True)
            out[0, i, 2 * t : 2 * t + 1, :] = line[:, :128]
            out[0, i, 2 * t + 1 : 2 * t + 2, :] = line[:, 128:]


def collocate(density, basis_cols, basis_rows):
    count = density.shape[0]
    return pl.pallas_call(
        functools.partial(collocate_kernel, count),
        grid=(16,),
        in_specs=[
            pl.BlockSpec((count, BS, BS), lambda g: (0, 0, 0)),
            pl.BlockSpec((1, BS, 1024), lambda g: (0, 0, g)),
            pl.BlockSpec((count, BS, 1024), lambda g: (0, 0, g)),
        ],
        out_specs=pl.BlockSpec((1, count, 8, 128), lambda g: (g, 0, 0, 0)),
        out_shape=jax.ShapeDtypeStruct((16, count, 8, 128), jnp.float32),
        scratch_shapes=[pltpu.VMEM((count * PAD, BS), jnp.bfloat16)],
        compiler_params=pltpu.CompilerParams(vmem_limit_bytes=40 * MIB),
        cost_estimate=pl.CostEstimate(
            flops=2 * count * BS * BS * 16384, bytes_accessed=(count + 1) * PAD * 16384 * 2, transcendentals=0
        ),
        name="collocate",
    )(density, basis_cols, basis_rows)


def bricks_kernel(owners, points, out):
    ids = lax.broadcasted_iota(jnp.int32, (128, 128), 0)
    onehot = (owners[...] == ids).astype(jnp.float32)
    for y in range(8):
        out[:, y, :] = jnp.dot(onehot, points[:, y, :], precision=HIGH, preferred_element_type=jnp.float32)


def sum_bricks(owners, points):
    return pl.pallas_call(
        bricks_kernel,
        out_shape=jax.ShapeDtypeStruct((128, 8, 128), jnp.float32),
        compiler_params=pltpu.CompilerParams(vmem_limit_bytes=16 * MIB),
        cost_estimate=pl.CostEstimate(flops=2 * 128 * 128 * 1024, bytes_accessed=MIB, transcendentals=0),
        name="sum_bricks",
    )(owners, points)


def tables():
    a = np.arange(16)
    outer = 2.0 * math.pi * (np.outer(a, a) % 16) / 16
    eye = np.eye(8)
    ck, sk = np.kron(np.cos(outer), eye), np.kron(np.sin(outer), eye)
    b = np.arange(128)
    inner = 2.0 * math.pi * (np.outer(b, b) % 128) / 128
    c, s = np.cos(inner), np.sin(inner)
    twist = 2.0 * math.pi * np.outer(np.repeat(a, 8), b) / 2048
    first = np.concatenate([ck, -sk], 0)
    second = np.block([[c, -s], [s, c]])
    third = np.block([[c, s], [-s, c]])
    last = np.concatenate([ck, -sk], 1) / 2048
    return [np.asarray(t, np.float32) for t in (first, second, third, last, np.cos(twist), np.sin(twist))]


def filter_kernel(own, in1, in2, in3, kern, first, second, third, last, tc, ts, out):
    def dot(p, q):
        return jnp.dot(p, q, precision=HIGH, preferred_element_type=jnp.float32)

    grid = (own[...] + in1[...]) + (in2[...] + in3[...])
    section = dot(first[...], grid)
    re, im = section[:128], section[128:]
    c, s = tc[...], ts[...]
    spec = dot(jnp.concatenate([re * c + im * s, im * c - re * s], axis=1), second[...])
    k = kern[...]
    back = dot(spec * jnp.concatenate([k, k], axis=1), third[...])
    re, im = back[:, :128], back[:, 128:]
    turned = jnp.concatenate([re * c - im * s, im * c + re * s], axis=0)
    out[...] = dot(last[...], turned)


def filter_rows(pieces, kern):
    return pl.pallas_call(
        filter_kernel,
        out_shape=jax.ShapeDtypeStruct((128, 128), jnp.float32),
        compiler_params=pltpu.CompilerParams(vmem_limit_bytes=16 * MIB),
        cost_estimate=pl.CostEstimate(flops=1 << 26, bytes_accessed=MIB, transcendentals=0),
        name="filter_rows",
    )(*pieces, kern, *tables())


def scatter_rows(partial):
    place = lax.axis_index("row")
    x, core = place // 2, place % 2
    halves = partial.reshape(4, 2, 16, 8, 128)
    away = lax.dynamic_index_in_dim(halves, 1 - core, 1, keepdims=False)
    mine = lax.dynamic_index_in_dim(halves, core, 1, keepdims=False)
    mine = mine + lax.ppermute(away, "row", [(r, r ^ 1) for r in range(8)])
    pieces = [lax.dynamic_index_in_dim(mine, x, 0, keepdims=False)]
    for d in (1, 2, 3):
        part = lax.dynamic_index_in_dim(mine, (x + d) % 4, 0, keepdims=False)
        pieces.append(lax.ppermute(part, "row", [(r, (r + 2 * d) % 8) for r in range(8)]))
    return [p.reshape(128, 128) for p in pieces]


def product(blocks_a, pattern_a, blocks_b):
    masked = blocks_a * pattern_a[:, :, None, None].astype(jnp.bfloat16)
    left = jnp.transpose(masked, (0, 2, 1, 3)).reshape(8 * BS, 16 * BS)
    right = jnp.transpose(blocks_b, (0, 2, 1, 3)).reshape(16 * BS, 16 * BS)
    result = jnp.dot(left, right, preferred_element_type=jnp.float32)
    result = jnp.transpose(result.reshape(8, BS, 16, BS), (2, 0, 1, 3))
    return lax.psum_scatter(result, "col", scatter_dimension=0, tiled=True)[0]


def shards(blocks_a, pattern_a, blocks_b, filter_mask, task_brick, basis_rows, basis_cols, kernel):
    owners = lax.all_gather(task_brick.reshape(8), "col", axis=0, tiled=True).reshape(1, 128)
    kern = jnp.transpose(kernel.reshape(8, 128, 16), (2, 0, 1)).reshape(128, 128)
    summed = product(blocks_a, pattern_a, blocks_b)
    density = (summed * filter_mask.reshape(8, 1, 1).astype(jnp.float32)).astype(jnp.bfloat16)
    points = collocate(density, basis_cols, basis_rows)
    points = lax.all_to_all(points, "col", split_axis=0, concat_axis=0, tiled=True)
    pieces = scatter_rows(sum_bricks(owners, points.reshape(128, 8, 128)))
    filtered = filter_rows(pieces, kern).reshape(16, 8, 128)
    potential = lax.all_to_all(filtered, "col", split_axis=0, concat_axis=0, tiled=True)
    return density[:, None], potential.reshape(128, 128)


def solution(mesh):
    return jax.shard_map(
        shards,
        mesh=mesh,
        in_specs=(
            P("row", "col", None, None),
            P("row", "col"),
            P("col", None, None, None),
            P("row", "col"),
            P("row", "col"),
            P("row", None, None),
            P("col", None, None),
            P(("row", "col"), None),
        ),
        out_specs=(P("row", "col", None, None), P("row", "col")),
        check_vma=False,
    )
```

```python
import functools
import math

import jax
import jax.numpy as jnp
import numpy as np
from jax import lax
from jax.experimental import pallas as pl
from jax.experimental.pallas import tpu as pltpu
from jax.sharding import PartitionSpec as P

BS = 138
PAD = 144
MIB = 1 << 20
HIGH = lax.Precision.HIGHEST
WIDE = 2304


def pack_kernel(pattern, blocks, out):
    first = pl.program_id(0)
    lane = lax.broadcasted_iota(jnp.int32, (BS, 128), 1)
    out[128:PAD, :] = jnp.zeros((PAD - 128, WIDE), jnp.bfloat16)
    for half in range(2):
        rest = jnp.zeros((BS, 128), jnp.float32)
        for n in range(8):
            k = half * 8 + n
            keep = pattern[first, k].astype(jnp.float32)
            block = blocks[0, k]
            out[0:BS, k * 128 : k * 128 + 128] = (block[:, :128].astype(jnp.float32) * keep).astype(jnp.bfloat16)
            tail = jnp.concatenate([block[:, 128:].astype(jnp.float32), jnp.zeros((BS, 118), jnp.float32)], axis=1)
            if n:
                tail = pltpu.roll(tail, 16 * n, 1)
            rest = jnp.where(lane // 16 == n, tail * keep, rest)
        out[0:BS, 2048 + half * 128 : 2176 + half * 128] = rest.astype(jnp.bfloat16)


def pack_rows(pattern, blocks_a, start):
    return pl.pallas_call(
        pack_kernel,
        grid_spec=pltpu.PrefetchScalarGridSpec(
            num_scalar_prefetch=1,
            grid=(4,),
            in_specs=[pl.BlockSpec((1, 16, BS, BS), lambda i, p: (i + start, 0, 0, 0))],
            out_specs=pl.BlockSpec((PAD, WIDE), lambda i, p: (i, 0)),
        ),
        out_shape=jax.ShapeDtypeStruct((4 * PAD, WIDE), jnp.bfloat16),
        compiler_params=pltpu.CompilerParams(vmem_limit_bytes=16 * MIB),
        cost_estimate=pl.CostEstimate(flops=1 << 24, bytes_accessed=8 * MIB, transcendentals=0),
        name="pack_rows",
    )(pattern[start : start + 4], blocks_a)


def fold(wide):
    lane = lax.broadcasted_iota(jnp.int32, (48, 128), 1)
    tail = wide[:, 128:]
    if tail.shape[1] < 128:
        tail = jnp.concatenate([tail, jnp.zeros((tail.shape[0], 128 - tail.shape[1]), jnp.float32)], axis=1)
    rest = jnp.zeros((48, 128), jnp.float32)
    for g in range(12):
        piece = tail[48 * g : 48 * g + 48]
        if g:
            piece = pltpu.roll(piece, 10 * g, 1)
        rest = jnp.where((lane >= 10 * g) & (lane < 10 * g + 10), piece, rest)
    return wide[:, :128], rest


def encode(out, main, rest):
    most = jnp.maximum(jnp.max(jnp.abs(main)), jnp.max(jnp.abs(rest)))
    most = jnp.full((1, 128), most, jnp.float32)
    power = jnp.floor(jnp.log2(jnp.maximum(most, 1e-30))) + 1.0
    gain = 32000.0 * jnp.exp2(-power)
    lane = lax.broadcasted_iota(jnp.int32, (48, 128), 1)
    out[0:576, :] = jnp.round(main * gain).astype(jnp.int32).astype(jnp.int16)
    coded = jnp.where(lane >= 120, jnp.broadcast_to(power, (48, 128)), jnp.round(rest * gain))
    out[576:624, :] = coded.astype(jnp.int32).astype(jnp.int16)


def decode(ref):
    lane = lax.broadcasted_iota(jnp.int32, (48, 128), 1)
    rest = ref[576:624, :].astype(jnp.int32).astype(jnp.float32)
    power = jnp.max(jnp.where(lane >= 120, rest, -1000.0))
    gain = jnp.exp2(jnp.full((1, 128), power, jnp.float32)) * (1.0 / 32000.0)
    return ref[0:576, :].astype(jnp.int32).astype(jnp.float32) * gain, rest * gain


def product_kernel(coded, which, left, right, out, stacked):
    @pl.when(pl.program_id(0) == 0)
    def _():
        stacked[2048:WIDE, :] = jnp.zeros((256, BS), jnp.bfloat16)

    for k in range(16):
        stacked[k * 128 : k * 128 + 128, :] = right[k, 0, 0:128, :]
        stacked[2048 + 16 * k : 2058 + 16 * k, :] = right[k, 0, 128:BS, :]
    main, rest = fold(jnp.dot(left[...], stacked[...], preferred_element_type=jnp.float32))
    if coded:
        encode(out.at[0], main, rest)
    else:
        out[0, 0:576, :] = main
        out[0, 576:624, :] = rest


def product_group(which, left, blocks_b, coded):
    return pl.pallas_call(
        functools.partial(product_kernel, coded),
        grid_spec=pltpu.PrefetchScalarGridSpec(
            num_scalar_prefetch=1,
            grid=(4,),
            in_specs=[
                pl.BlockSpec((4 * PAD, WIDE), lambda n, w: (0, 0)),
                pl.BlockSpec((16, 1, BS, BS), lambda n, w: (0, w[n], 0, 0)),
            ],
            out_specs=pl.BlockSpec((1, 624, 128), lambda n, w: (n, 0, 0)),
            scratch_shapes=[pltpu.VMEM((WIDE, BS), jnp.bfloat16)],
        ),
        out_shape=jax.ShapeDtypeStruct((4, 624, 128), jnp.int16 if coded else jnp.float32),
        compiler_params=pltpu.CompilerParams(vmem_limit_bytes=24 * MIB),
        cost_estimate=pl.CostEstimate(flops=8 * 576 * WIDE * 256, bytes_accessed=8 * MIB, transcendentals=0),
        name="product_coded" if coded else "product_own",
    )(which, left, blocks_b)


def merge_kernel(own, in1, in2, in3, mine, out1, out2, out3):
    step = pl.program_id(0)
    main, rest = own[0, 0:576, :], own[0, 576:624, :]
    for part in (in1, in2, in3):
        more, extra = decode(part.at[0])
        main, rest = main + more, rest + extra

    @pl.when(step == 0)
    def _():
        mine[0:576, :] = main
        mine[576:624, :] = rest

    for n, out in enumerate((out1, out2, out3)):

        @pl.when(step == n + 1)
        def _(out=out):
            encode(out, main, rest)


def merge(own, parts):
    unit = pl.BlockSpec((1, 624, 128), lambda n: (n, 0, 0))
    whole = pl.BlockSpec((624, 128), lambda n: (0, 0))
    return pl.pallas_call(
        merge_kernel,
        grid=(4,),
        in_specs=[unit] * 4,
        out_specs=[whole] * 4,
        out_shape=[jax.ShapeDtypeStruct((624, 128), t) for t in (jnp.float32,) + (jnp.int16,) * 3],
        compiler_params=pltpu.CompilerParams(vmem_limit_bytes=16 * MIB),
        cost_estimate=pl.CostEstimate(flops=1 << 22, bytes_accessed=4 * MIB, transcendentals=0),
        name="merge",
    )(own, *parts)


def turn(dy, dz):
    return [(4 * y + z, (y + dy) % 4 * 4 + (z + dz) % 4) for y in range(4) for z in range(4)]


def send(array, axis, d):
    return lax.ppermute(array, "col", turn(d, 0) if axis == 0 else turn(0, d))


def exchange_products(blocks_a, pattern, blocks_b):
    place = lax.axis_index("col")
    y, z = place // 4, place % 4
    steps = jnp.arange(4, dtype=jnp.int32)
    firsts = []
    for half in range(2):
        left = pack_rows(pattern, blocks_a, 4 * half)

        def group(d, half=half):
            if half == 0:
                return (y + d) % 4 * 4 + (z + steps) % 4
            return (y + steps) % 4 * 4 + (z + d) % 4

        parts = [send(product_group(group(d), left, blocks_b, True), half, d) for d in (2, 1, 3)]
        firsts.append((product_group(group(0), left, blocks_b, False), parts))
    sums = []
    for half in range(2):
        own, parts = firsts[half]
        mine, *outs = merge(own, parts)
        sums.append((mine, [send(outs[d - 1], 1 - half, d) for d in (2, 1, 3)]))
    return sums


def collocate_kernel(mask, own, in1, in2, in3, cols, rows, density, out, stacked, right):
    @pl.when(pl.program_id(0) == 0)
    def _():
        lane = lax.broadcasted_iota(jnp.int32, (48, 128), 1)
        main, rest = own[0:576, :], own[576:624, :]
        for part in (in1, in2, in3):
            more, extra = decode(part)
            main, rest = main + more, rest + extra
        tails = []
        for g in range(12):
            piece = pltpu.roll(rest, 128 - 10 * g, 1) if g else rest
            tails.append(jnp.where(lane < 10, piece, 0.0))
        tail = jnp.concatenate(tails, axis=0)
        for i in range(4):
            keep = mask[i].astype(jnp.float32)
            near = (main[i * PAD : i * PAD + PAD] * keep).astype(jnp.bfloat16)
            far = (tail[i * PAD : i * PAD + PAD] * keep).astype(jnp.bfloat16)
            stacked[i * PAD : i * PAD + PAD, 0:128] = near
            stacked[i * PAD : i * PAD + PAD, 128:256] = far
            density[i, :, 0:128] = near[:BS]
            density[i, :, 128:BS] = far[:BS, 0 : BS - 128]
        right[128:256, :] = jnp.zeros((128, 1024), jnp.bfloat16)

    right[0:BS, :] = cols[0]
    for t in range(4):
        lanes = slice(t * 256, (t + 1) * 256)
        inner = jnp.dot(stacked[...], right[:, lanes], preferred_element_type=jnp.float32)
        for i in range(4):
            part = inner[i * PAD : i * PAD + BS] * rows[i, :, lanes].astype(jnp.float32)
            line = jnp.sum(part, axis=0, keepdims=True)
            out[0, i, 2 * t : 2 * t + 1, :] = line[:, :128]
            out[0, i, 2 * t + 1 : 2 * t + 2, :] = line[:, 128:]


def collocate(mask, own, parts, basis_cols, basis_rows, half):
    unit = pl.BlockSpec((624, 128), lambda g, m: (0, 0))
    return pl.pallas_call(
        collocate_kernel,
        grid_spec=pltpu.PrefetchScalarGridSpec(
            num_scalar_prefetch=1,
            grid=(16,),
            in_specs=[unit] * 4
            + [
                pl.BlockSpec((1, BS, 1024), lambda g, m: (0, 0, g)),
                pl.BlockSpec((4, BS, 1024), lambda g, m: (half, 0, g)),
            ],
            out_specs=[
                pl.BlockSpec((4, BS, BS), lambda g, m: (0, 0, 0)),
                pl.BlockSpec((1, 4, 8, 128), lambda g, m: (g, 0, 0, 0)),
            ],
            scratch_shapes=[pltpu.VMEM((4 * PAD, 256), jnp.bfloat16), pltpu.VMEM((256, 1024), jnp.bfloat16)],
        ),
        out_shape=[
            jax.ShapeDtypeStruct((4, BS, BS), jnp.bfloat16),
            jax.ShapeDtypeStruct((16, 4, 8, 128), jnp.float32),
        ],
        compiler_params=pltpu.CompilerParams(vmem_limit_bytes=24 * MIB),
        cost_estimate=pl.CostEstimate(
            flops=8 * BS * 256 * 16384, bytes_accessed=5 * PAD * 16384 * 2, transcendentals=0
        ),
        name="collocate",
    )(mask, own, *parts, basis_cols, basis_rows)


def bricks_kernel(points, out):
    owners = jnp.sum(points[:, 8, 0, :], axis=0, keepdims=True).astype(jnp.int32)
    ids = lax.broadcasted_iota(jnp.int32, (128, 128), 0)
    onehot = (owners == ids).astype(jnp.float32)
    for y in range(8):
        held = points[:, 0:8, y, :].reshape(128, 128)
        out[:, y, :] = jnp.dot(onehot, held, precision=HIGH, preferred_element_type=jnp.float32)


def sum_bricks(points):
    return pl.pallas_call(
        bricks_kernel,
        out_shape=jax.ShapeDtypeStruct((128, 8, 128), jnp.float32),
        compiler_params=pltpu.CompilerParams(vmem_limit_bytes=16 * MIB),
        cost_estimate=pl.CostEstimate(flops=2 * 128 * 128 * 1024, bytes_accessed=MIB, transcendentals=0),
        name="sum_bricks",
    )(points)


def shards(blocks_a, pattern_a, blocks_b, filter_mask, task_brick, basis_rows, basis_cols, kernel):
    kern = jnp.transpose(kernel.reshape(8, 128, 16), (2, 0, 1)).reshape(128, 128)
    lane = jnp.arange(128, dtype=jnp.int32)
    owners = jnp.where(lane // 8 == lax.axis_index("col"), jnp.tile(task_brick.reshape(8), 16), 0)
    owners = jnp.broadcast_to(owners.astype(jnp.float32), (16, 1, 8, 128))
    mask = filter_mask.reshape(8)
    sums = exchange_products(blocks_a, pattern_a, blocks_b)
    density, points = [], []
    for half in range(2):
        own, parts = sums[half]
        kept, given = collocate(mask[4 * half : 4 * half + 4], own, parts, basis_cols, basis_rows, half)
        density.append(kept)
        points.append(given)
    points = lax.all_to_all(
        jnp.concatenate(points + [owners], axis=1), "col", split_axis=0, concat_axis=0, tiled=True
    )
    pieces = scatter_rows(sum_bricks(points))
    filtered = filter_rows(pieces, kern).reshape(16, 8, 128)
    potential = lax.all_to_all(filtered, "col", split_axis=0, concat_axis=0, tiled=True)
    return jnp.concatenate(density, axis=0)[:, None], potential.reshape(128, 128)


def tables():
    a = np.arange(16)
    outer = 2.0 * math.pi * (np.outer(a, a) % 16) / 16
    eye = np.eye(8)
    ck, sk = np.kron(np.cos(outer), eye), np.kron(np.sin(outer), eye)
    b = np.arange(128)
    inner = 2.0 * math.pi * (np.outer(b, b) % 128) / 128
    c, s = np.cos(inner), np.sin(inner)
    twist = 2.0 * math.pi * np.outer(np.repeat(a, 8), b) / 2048
    first = np.concatenate([ck, -sk], 0)
    second = np.block([[c, -s], [s, c]])
    third = np.block([[c, s], [-s, c]])
    last = np.concatenate([ck, -sk], 1) / 2048
    return [np.asarray(t, np.float32) for t in (first, second, third, last, np.cos(twist), np.sin(twist))]


def filter_kernel(own, in1, in2, in3, kern, first, second, third, last, tc, ts, out):
    def dot(p, q):
        return jnp.dot(p, q, precision=HIGH, preferred_element_type=jnp.float32)

    grid = (own[...] + in1[...]) + (in2[...] + in3[...])
    section = dot(first[...], grid)
    re, im = section[:128], section[128:]
    c, s = tc[...], ts[...]
    spec = dot(jnp.concatenate([re * c + im * s, im * c - re * s], axis=1), second[...])
    k = kern[...]
    back = dot(spec * jnp.concatenate([k, k], axis=1), third[...])
    re, im = back[:, :128], back[:, 128:]
    turned = jnp.concatenate([re * c - im * s, im * c + re * s], axis=0)
    out[...] = dot(last[...], turned)


def filter_rows(pieces, kern):
    return pl.pallas_call(
        filter_kernel,
        out_shape=jax.ShapeDtypeStruct((128, 128), jnp.float32),
        compiler_params=pltpu.CompilerParams(vmem_limit_bytes=16 * MIB),
        cost_estimate=pl.CostEstimate(flops=1 << 26, bytes_accessed=MIB, transcendentals=0),
        name="filter_rows",
    )(*pieces, kern, *tables())


def scatter_rows(partial):
    place = lax.axis_index("row")
    x, core = place // 2, place % 2
    halves = partial.reshape(4, 2, 16, 8, 128)
    away = lax.dynamic_index_in_dim(halves, 1 - core, 1, keepdims=False)
    mine = lax.dynamic_index_in_dim(halves, core, 1, keepdims=False)
    mine = mine + lax.ppermute(away, "row", [(r, r ^ 1) for r in range(8)])
    pieces = [lax.dynamic_index_in_dim(mine, x, 0, keepdims=False)]
    for d in (1, 2, 3):
        part = lax.dynamic_index_in_dim(mine, (x + d) % 4, 0, keepdims=False)
        pieces.append(lax.ppermute(part, "row", [(r, (r + 2 * d) % 8) for r in range(8)]))
    return [p.reshape(128, 128) for p in pieces]


def solution(mesh):
    return jax.shard_map(
        shards,
        mesh=mesh,
        in_specs=(
            P("row", "col", None, None),
            P("row", "col"),
            P("col", None, None, None),
            P("row", "col"),
            P("row", "col"),
            P("row", None, None),
            P("col", None, None),
            P(("row", "col"), None),
        ),
        out_specs=(P("row", "col", None, None), P("row", "col")),
        check_vma=False,
    )
```

```python
import functools
import math

import jax
import jax.numpy as jnp
import numpy as np
from jax import lax
from jax.experimental import pallas as pl
from jax.experimental.pallas import tpu as pltpu
from jax.sharding import PartitionSpec as P

BS = 138
MIB = 1 << 20
HIGH = lax.Precision.HIGHEST
F32 = jnp.float32
BF16 = jnp.bfloat16
I16 = jnp.int16
WIDE = 2304
NEAR = 2048
ROWS = (560, 544)
CUT = (0, 560)
TOP = 288
FOLD = 80


def widen(tail):
    return jnp.concatenate([tail.astype(F32), jnp.zeros(tail.shape[:-1] + (128 - tail.shape[-1],), F32)], axis=-1)


def place_tails(tails, out, rows):
    lane = lax.broadcasted_iota(jnp.int32, (16, 128), 1) // 16
    for half in range(2):
        rest = jnp.zeros((16, 128), F32)
        for n in range(8):
            tail = tails[half * 8 + n]
            rest = jnp.where(lane == n, pltpu.roll(tail, 16 * n, 1) if n else tail, rest)
        out(half, rest.astype(BF16))


def pack_left_kernel(mask, blocks, out):
    def step(p, carry):
        pair = jnp.transpose(blocks[:, pl.ds(2 * p, 2)], (1, 0, 2, 3)).reshape(16, 16, BS)
        wide = jnp.swapaxes(pair, 0, 1)
        rows = pl.ds(pl.multiple_of(16 * p, 16), 16)
        tails = []
        for k in range(16):
            out[rows, k * 128 : k * 128 + 128] = wide[k, :, :128] * mask[k]
            tails.append(widen(wide[k, :, 128:] * mask[k, :, : BS - 128]))

        def put(half, value):
            out[rows, NEAR + 128 * half : NEAR + 128 * half + 128] = value

        place_tails(tails, put, rows)
        return carry

    lax.fori_loop(0, 23, step, 0)


def pack_left(mask, blocks):
    return pl.pallas_call(
        pack_left_kernel,
        grid=(3,),
        in_specs=[
            pl.BlockSpec((16, 16, 128), lambda g: (0, 0, 0)),
            pl.BlockSpec((8, 46, 16, BS), lambda g: (0, g, 0, 0)),
        ],
        out_specs=pl.BlockSpec((368, WIDE), lambda g: (g, 0)),
        out_shape=jax.ShapeDtypeStruct((1104, WIDE), BF16),
        compiler_params=pltpu.CompilerParams(vmem_limit_bytes=40 * MIB),
        cost_estimate=pl.CostEstimate(flops=1 << 24, bytes_accessed=14 * MIB, transcendentals=0),
        name="pack_left",
    )(mask, blocks)


def pack_right_kernel(blocks, near, far, rest, rest_far):
    def step(k, carry):
        for c in range(0, 144, 16):
            if c < 128:
                rows = pl.ds(pl.multiple_of(128 * k + c, 16), 16)
                square, to, tail_to = blocks[k, c : c + 16], near, rest
            else:
                rows = pl.ds(pl.multiple_of(16 * k, 16), 16)
                square = jnp.concatenate([blocks[k, 128:BS], jnp.zeros((144 - BS, 16, BS), BF16)], axis=0)
                to, tail_to = far, rest_far
            turned = jnp.swapaxes(square, 0, 1)
            to[:, rows, :] = turned[:, :, :128]

            def put(half, value, rows=rows, tail_to=tail_to):
                tail_to[rows, 128 * half : 128 * half + 128] = value

            place_tails([widen(turned[j, :, 128:]) for j in range(16)], put, rows)
        return carry

    lax.fori_loop(0, 4, step, 0)


def pack_right(blocks):
    return pl.pallas_call(
        pack_right_kernel,
        grid=(4,),
        in_specs=[pl.BlockSpec((4, BS, 16, BS), lambda g: (g, 0, 0, 0))],
        out_specs=[
            pl.BlockSpec((16, 512, 128), lambda g: (0, g, 0)),
            pl.BlockSpec((16, 64, 128), lambda g: (0, g, 0)),
            pl.BlockSpec((512, 256), lambda g: (g, 0)),
            pl.BlockSpec((64, 256), lambda g: (g, 0)),
        ],
        out_shape=[
            jax.ShapeDtypeStruct((16, NEAR, 128), BF16),
            jax.ShapeDtypeStruct((16, 256, 128), BF16),
            jax.ShapeDtypeStruct((NEAR, 256), BF16),
            jax.ShapeDtypeStruct((256, 256), BF16),
        ],
        compiler_params=pltpu.CompilerParams(vmem_limit_bytes=36 * MIB),
        cost_estimate=pl.CostEstimate(flops=1 << 24, bytes_accessed=30 * MIB, transcendentals=0),
        name="pack_right",
    )(blocks)


def dot_parts(left, half, near, far):
    rows = slice(CUT[half], CUT[half] + ROWS[half])
    return jnp.dot(left[rows, :NEAR], near, preferred_element_type=F32) + jnp.dot(
        left[rows, NEAR:], far, preferred_element_type=F32
    )


def tails_kernel(half, left, rest, rest_far, out):
    out[...] = dot_parts(left, half, rest[...], rest_far[...])


def product_tails(half, left, rest, rest_far):
    return pl.pallas_call(
        functools.partial(tails_kernel, half),
        out_shape=jax.ShapeDtypeStruct((ROWS[half], 256), F32),
        compiler_params=pltpu.CompilerParams(vmem_limit_bytes=24 * MIB),
        cost_estimate=pl.CostEstimate(flops=2 * 560 * WIDE * 256, bytes_accessed=4 * MIB, transcendentals=0),
        name="product_tails",
    )(left, rest, rest_far)


def lanes(rows):
    return lax.broadcasted_iota(jnp.int32, (rows, 128), 1)


def scale_of(most):
    power = jnp.floor(jnp.log2(jnp.maximum(jnp.full((1, 128), most, F32), 1e-30))) + 1.0
    return power, 32000.0 * jnp.exp2(-power)


def gain_of(coded):
    power = jnp.max(jnp.where(lanes(16) % 16 == 15, coded[0:16], -1000.0))
    return jnp.exp2(jnp.full((1, 128), power, F32)) * (1.0 / 32000.0)


def code(value, gain):
    return jnp.round(value * gain).astype(jnp.int32).astype(I16)


def code_tail(value, gain, power):
    coded = jnp.where(lanes(value.shape[0]) % 16 == 15, jnp.broadcast_to(power, value.shape), jnp.round(value * gain))
    return coded.astype(jnp.int32).astype(I16)


def plain(value):
    return value.astype(jnp.int32).astype(F32)


def product_kernel(half, coded, which, left, near, far, tails, out, held):
    rows = ROWS[half]
    for pair in range(2):
        j0, j1 = which[2 * pair], which[2 * pair + 1]
        both = dot_parts(
            left,
            half,
            jnp.concatenate([near[j0], near[j1]], axis=1),
            jnp.concatenate([far[j0], far[j1]], axis=1),
        )
        held[2 * pair] = both[:, :128]
        held[2 * pair + 1] = both[:, 128:]
    group = which[4]
    slot = lanes(rows) // 16
    if half == 0:
        tile = jnp.where(group >= 2, tails[:, 128:], tails[:, :128])
        tail = pltpu.roll(tile, 64 * (group % 2), 1)
    else:
        tail = jnp.zeros((rows, 128), F32)
        for y in range(4):
            tile = tails[:, 128 * (y // 2) : 128 * (y // 2) + 128]
            shift = (16 * y - 64 * (y % 2) - 16 * group + 128) % 128
            tail = jnp.where(slot == y, pltpu.roll(tile, shift, 1), tail)
    low = jnp.concatenate([tail[TOP:], jnp.zeros((2 * TOP - rows, 128), F32)], axis=0)
    folded = jnp.where(lanes(TOP) < 64, tail[:TOP], pltpu.roll(low, 64, 1))
    if coded:
        power, gain = scale_of(jnp.maximum(jnp.max(jnp.abs(held[...])), jnp.max(jnp.abs(folded))))
        for n in range(4):
            out[n * rows : (n + 1) * rows, :] = code(held[n], gain)
        out[4 * rows : 4 * rows + TOP, :] = code_tail(folded, gain, power)
    else:
        for n in range(4):
            out[n * rows : (n + 1) * rows, :] = held[n]
        out[4 * rows : 4 * rows + TOP, :] = folded


def product_group(half, coded, which, left, near, far, tails):
    rows = ROWS[half]
    vmem = pl.BlockSpec(memory_space=pltpu.VMEM)
    return pl.pallas_call(
        functools.partial(product_kernel, half, coded),
        in_specs=[pl.BlockSpec(memory_space=pltpu.SMEM)] + [vmem] * 4,
        out_specs=vmem,
        out_shape=jax.ShapeDtypeStruct((4 * rows + TOP, 128), I16 if coded else F32),
        scratch_shapes=[pltpu.VMEM((4, rows, 128), F32)],
        compiler_params=pltpu.CompilerParams(vmem_limit_bytes=40 * MIB),
        cost_estimate=pl.CostEstimate(flops=2 * 560 * WIDE * 512, bytes_accessed=8 * MIB, transcendentals=0),
        name="product_coded" if coded else "product_own",
    )(which, left, near, far, tails)


def merge_kernel(half, place, own, in1, in2, in3, mine, out1, out2, out3, held):
    rows = ROWS[half]
    parts = (in1, in2, in3)
    tails = [plain(p[4 * rows : 4 * rows + TOP, :]) for p in parts]
    gains = [gain_of(t) for t in tails]
    for n in range(4):
        here = slice(n * rows, (n + 1) * rows)
        total = own[here, :]
        for p, g in zip(parts, gains):
            total = total + plain(p[here, :]) * g
        held[n] = total
    folded = own[4 * rows : 4 * rows + TOP, :]
    for t, g in zip(tails, gains):
        folded = folded + t * g
    last = jnp.concatenate([folded[3 * FOLD :], jnp.zeros((4 * FOLD - TOP, 128), F32)], axis=0)
    pieces = [folded[0:FOLD], folded[FOLD : 2 * FOLD], folded[2 * FOLD : 3 * FOLD], last]
    slot = lanes(FOLD) // 16 % 4
    for d, out in enumerate((mine, out1, out2, out3)):
        s = (place[0] + d) % 4
        tail = jnp.zeros((FOLD, 128), F32)
        for q in range(4):
            tail = jnp.where(slot == q, pltpu.roll(pieces[q], 16 * ((q - s + 8) % 8), 1), tail)
        main = held[s]
        if d == 0:
            out[0:rows, :] = main
            out[rows : rows + FOLD, :] = tail
        else:
            tail = jnp.where(lanes(FOLD) % 16 < 10, tail, 0.0)
            power, gain = scale_of(jnp.maximum(jnp.max(jnp.abs(main)), jnp.max(jnp.abs(tail))))
            out[0:rows, :] = code(main, gain)
            out[rows : rows + FOLD, :] = code_tail(tail, gain, power)


def merge(half, place, own, parts):
    vmem = pl.BlockSpec(memory_space=pltpu.VMEM)
    return pl.pallas_call(
        functools.partial(merge_kernel, half),
        in_specs=[pl.BlockSpec(memory_space=pltpu.SMEM)] + [vmem] * 4,
        out_specs=[vmem] * 4,
        out_shape=[jax.ShapeDtypeStruct((ROWS[half] + FOLD, 128), t) for t in (F32, I16, I16, I16)],
        scratch_shapes=[pltpu.VMEM((4, ROWS[half], 128), F32)],
        compiler_params=pltpu.CompilerParams(vmem_limit_bytes=24 * MIB),
        cost_estimate=pl.CostEstimate(flops=1 << 22, bytes_accessed=4 * MIB, transcendentals=0),
        name="merge",
    )(place, own, *parts)


def turn(dy, dz):
    return [(4 * y + z, (y + dy) % 4 * 4 + (z + dz) % 4) for y in range(4) for z in range(4)]


def send(array, axis, d):
    return lax.ppermute(array, "col", turn(d, 0) if axis == 0 else turn(0, d))


def exchange_products(blocks_a, pattern, blocks_b):
    place = lax.axis_index("col")
    spot = (place // 4, place % 4)
    steps = jnp.arange(4, dtype=jnp.int32)
    mask = jnp.broadcast_to(jnp.tile(pattern.T, (1, 2))[:, :, None], (16, 16, 128)).astype(BF16)
    left = pack_left(mask, jnp.transpose(blocks_a, (0, 2, 1, 3)))
    near, far, rest, rest_far = pack_right(jnp.transpose(blocks_b, (0, 2, 1, 3)))
    tails = [product_tails(half, left, rest, rest_far) for half in range(2)]

    def group(half, d):
        g = (spot[half] + d) % 4
        which = 4 * g + steps if half == 0 else 4 * steps + g
        which = jnp.concatenate([which, g[None]]).astype(jnp.int32)
        return product_group(half, d != 0, which, left, near, far, tails[half])

    parts = ([], [])
    for d in (2, 1, 3):
        for half in range(2):
            parts[half].append(send(group(half, d), half, d))
    owns = [group(half, 0) for half in range(2)]
    sums = []
    for half in range(2):
        mine, *outs = merge(half, spot[1 - half].reshape(1), owns[half], parts[half])
        sums.append((mine, [send(outs[d - 1], 1 - half, d) for d in (2, 1, 3)]))
    return sums


def collocate_kernel(half, keep, ids, own, in1, in2, in3, cols, rows, *rest):
    if half == 0:
        density, out, stacked, right = rest
        before = None
    else:
        before, density, out, stacked, right = rest
    count = ROWS[half]

    @pl.when(pl.program_id(0) == 0)
    def _():
        main, fold = own[0:count, :], own[count : count + FOLD, :]
        for part in (in1, in2, in3):
            extra = plain(part[count : count + FOLD, :])
            gain = gain_of(extra)
            main, fold = main + plain(part[0:count, :]) * gain, fold + extra * gain
        tails = []
        for base, total in ((0, TOP), (4, count - TOP)):
            for q in range(4):
                piece = fold[0 : min(FOLD, total - q * FOLD)]
                shift = (128 - 16 * (q + base)) % 128
                tails.append(pltpu.roll(piece, shift, 1) if shift else piece)
        tail = jnp.where(lanes(count) < BS - 128, jnp.concatenate(tails, axis=0), 0.0)
        kept = keep[...][None]
        main = (main.reshape(count // 8, 8, 128) * kept).reshape(count, 128).astype(BF16)
        tail = (tail.reshape(count // 8, 8, 128) * kept).reshape(count, 128).astype(BF16)
        stacked[:, 0:128] = main
        stacked[:, 128:256] = tail
        density[:, :, 0:128] = main.reshape(count // 8, 8, 128)
        density[:, :, 128:BS] = tail.reshape(count // 8, 8, 128)[:, :, : BS - 128]
        right[128:256, :] = jnp.zeros((128, 1024), BF16)

    right[0:BS, :] = cols[0]
    for t in range(4):
        here = slice(t * 256, (t + 1) * 256)
        inner = jnp.dot(stacked[...], right[:, here], preferred_element_type=F32).reshape(count // 8, 8, 256)
        total = jnp.sum(inner * rows[:, :, here].astype(F32), axis=0)
        if half == 1:
            total = total + before[0, :, here]
        out[0, :, here] = total
    if half == 1:
        out[0, :, 1024:1152] = ids[...]


def collocate(half, keep, ids, own, parts, basis_cols, basis_rows, before):
    count = ROWS[half]
    unit = pl.BlockSpec((count + FOLD, 128), lambda g: (0, 0))
    small = pl.BlockSpec((8, 128), lambda g: (0, 0))
    wide = 1152 if half else 1024
    many = count // 8
    return pl.pallas_call(
        functools.partial(collocate_kernel, half),
        grid=(16,),
        in_specs=[small, small]
        + [unit] * 4
        + [
            pl.BlockSpec((1, BS, 1024), lambda g: (0, 0, g)),
            pl.BlockSpec(
                (pl.Element(many), pl.Element(8), pl.Element(1024)), lambda g: (CUT[half] // 8, 0, g * 1024)
            ),
        ]
        + [pl.BlockSpec((1, 8, 1024), lambda g: (g, 0, 0))] * half,
        out_specs=[
            pl.BlockSpec((many, 8, BS), lambda g: (0, 0, 0)),
            pl.BlockSpec((1, 8, wide), lambda g: (g, 0, 0)),
        ],
        scratch_shapes=[pltpu.VMEM((count, 256), BF16), pltpu.VMEM((256, 1024), BF16)],
        out_shape=[
            jax.ShapeDtypeStruct((many, 8, BS), BF16),
            jax.ShapeDtypeStruct((16, 8, wide), F32),
        ],
        compiler_params=pltpu.CompilerParams(vmem_limit_bytes=40 * MIB),
        cost_estimate=pl.CostEstimate(
            flops=2 * count * 256 * 16384, bytes_accessed=(count + 144) * 16384 * 2, transcendentals=0
        ),
        name="collocate",
    )(keep, ids, own, *parts, basis_cols, basis_rows, *before)


def bricks_kernel(points, out):
    owners = jnp.sum(points[:, :, 1024:1152].reshape(128, 128), axis=0, keepdims=True).astype(jnp.int32)
    onehot = (owners == lax.broadcasted_iota(jnp.int32, (128, 128), 0)).astype(F32)
    held = points[:, :, 0:1024].reshape(128, 1024)
    out[...] = jnp.dot(onehot, held, precision=HIGH, preferred_element_type=F32)


def sum_bricks(points):
    return pl.pallas_call(
        bricks_kernel,
        out_shape=jax.ShapeDtypeStruct((128, 1024), F32),
        compiler_params=pltpu.CompilerParams(vmem_limit_bytes=16 * MIB),
        cost_estimate=pl.CostEstimate(flops=2 * 128 * 128 * 1024, bytes_accessed=MIB, transcendentals=0),
        name="sum_bricks",
    )(points)


def tables():
    a = np.arange(16)
    outer = 2.0 * math.pi * (np.outer(a, a) % 16) / 16
    eye = np.eye(8)
    ck, sk = np.kron(eye, np.cos(outer)), np.kron(eye, np.sin(outer))
    b = np.arange(128)
    inner = 2.0 * math.pi * (np.outer(b, b) % 128) / 128
    c, s = np.cos(inner), np.sin(inner)
    twist = 2.0 * math.pi * np.outer(np.tile(a, 8), b) / 2048
    first = np.concatenate([ck, -sk], 0)
    second = np.block([[c, -s], [s, c]])
    third = np.block([[c, s], [-s, c]])
    last = np.concatenate([ck, -sk], 1) / 2048
    return [np.asarray(t, np.float32) for t in (first, second, third, last, np.cos(twist), np.sin(twist))]


def filter_kernel(own, in1, in2, in3, kern, first, second, third, last, tc, ts, out):
    def dot(p, q):
        return jnp.dot(p, q, precision=HIGH, preferred_element_type=F32)

    grid = (own[...] + in1[...]) + (in2[...] + in3[...])
    grid = jnp.concatenate([grid[:, y * 128 : y * 128 + 128] for y in range(8)], axis=0)
    section = dot(first[...], grid)
    re, im = section[:128], section[128:]
    c, s = tc[...], ts[...]
    spec = dot(jnp.concatenate([re * c + im * s, im * c - re * s], axis=1), second[...])
    k = kern[...]
    back = dot(spec * jnp.concatenate([k, k], axis=1), third[...])
    re, im = back[:, :128], back[:, 128:]
    turned = jnp.concatenate([re * c - im * s, im * c + re * s], axis=0)
    result = dot(last[...], turned)
    for y in range(8):
        out[:, y, :] = result[y * 16 : y * 16 + 16]


def filter_rows(pieces, kern):
    return pl.pallas_call(
        filter_kernel,
        out_shape=jax.ShapeDtypeStruct((16, 8, 128), F32),
        compiler_params=pltpu.CompilerParams(vmem_limit_bytes=16 * MIB),
        cost_estimate=pl.CostEstimate(flops=1 << 26, bytes_accessed=MIB, transcendentals=0),
        name="filter_rows",
    )(*pieces, kern, *tables())


def scatter_rows(partial):
    place = lax.axis_index("row")
    x, core = place // 2, place % 2
    halves = partial.reshape(4, 2, 16, 1024)
    away = lax.dynamic_index_in_dim(halves, 1 - core, 1, keepdims=False)
    mine = lax.dynamic_index_in_dim(halves, core, 1, keepdims=False)
    mine = mine + lax.ppermute(away, "row", [(r, r ^ 1) for r in range(8)])
    pieces = [lax.dynamic_index_in_dim(mine, x, 0, keepdims=False)]
    for d in (1, 2, 3):
        part = lax.dynamic_index_in_dim(mine, (x + d) % 4, 0, keepdims=False)
        pieces.append(lax.ppermute(part, "row", [(r, (r + 2 * d) % 8) for r in range(8)]))
    return pieces


def shards(blocks_a, pattern_a, blocks_b, filter_mask, task_brick, basis_rows, basis_cols, kernel):
    kern = jnp.transpose(kernel.reshape(8, 128, 16), (0, 2, 1)).reshape(128, 128)
    lane = jnp.arange(128, dtype=jnp.int32)
    owners = jnp.where(lane // 8 == lax.axis_index("col"), jnp.tile(task_brick.reshape(8), 16), 0)
    ids = jnp.concatenate([owners.astype(F32)[None], jnp.zeros((7, 128), F32)], axis=0)
    keep = jnp.broadcast_to(filter_mask.reshape(8, 1).astype(F32), (8, 128))
    by_point = jnp.transpose(basis_rows, (1, 0, 2))
    sums = exchange_products(blocks_a, pattern_a, blocks_b)
    densities, before = [], []
    for half in range(2):
        own, parts = sums[half]
        density, points = collocate(half, keep, ids, own, parts, basis_cols, by_point, before)
        densities.append(density)
        before = [points]
    points = lax.all_to_all(points, "col", split_axis=0, concat_axis=0, tiled=True)
    pieces = scatter_rows(sum_bricks(points))
    filtered = filter_rows(pieces, kern)
    potential = lax.all_to_all(filtered, "col", split_axis=0, concat_axis=0, tiled=True)
    density = jnp.transpose(jnp.concatenate(densities, axis=0), (1, 0, 2))
    return density[:, None], potential.reshape(128, 128)


def solution(mesh):
    return jax.shard_map(
        shards,
        mesh=mesh,
        in_specs=(
            P("row", "col", None, None),
            P("row", "col"),
            P("col", None, None, None),
            P("row", "col"),
            P("row", "col"),
            P("row", None, None),
            P("col", None, None),
            P(("row", "col"), None),
        ),
        out_specs=(P("row", "col", None, None), P("row", "col")),
        check_vma=False,
    )
```

```python
import functools
import math

import jax
import jax.numpy as jnp
import numpy as np
from jax import lax
from jax.experimental import pallas as pl
from jax.experimental.pallas import tpu as pltpu
from jax.sharding import PartitionSpec as P

BS = 138
MIB = 1 << 20
HIGH = lax.Precision.HIGHEST
F32 = jnp.float32
BF16 = jnp.bfloat16
I16 = jnp.int16
WIDE = 2304
SPAN = 1152
ROWS = (560, 544)
CUT = (0, 560)
TOP = 288
FOLD = 80
POINTS = 2048


def widen(tail):
    return jnp.concatenate([tail.astype(F32), jnp.zeros(tail.shape[:-1] + (128 - tail.shape[-1],), F32)], axis=-1)


def place_tails(tails, out, rows):
    lane = lax.broadcasted_iota(jnp.int32, (16, 128), 1) // 16
    for half in range(2):
        rest = jnp.zeros((16, 128), F32)
        for n in range(8):
            tail = tails[half * 8 + n]
            rest = jnp.where(lane == n, pltpu.roll(tail, 16 * n, 1) if n else tail, rest)
        out(half, rest.astype(BF16))


def pack_left_kernel(mask, blocks, out):
    def step(p, carry):
        pair = jnp.transpose(blocks[:, pl.ds(2 * p, 2)], (1, 0, 2, 3)).reshape(16, 16, BS)
        wide = jnp.swapaxes(pair, 0, 1)
        rows = pl.ds(pl.multiple_of(16 * p, 16), 16)
        tails = []
        for k in range(16):
            at = SPAN * (k // 8) + 128 * (k % 8)
            out[rows, at : at + 128] = wide[k, :, :128] * mask[k]
            tails.append(widen(wide[k, :, 128:] * mask[k, :, : BS - 128]))

        def put(half, value):
            out[rows, SPAN * half + 1024 : SPAN * half + 1152] = value

        place_tails(tails, put, rows)
        return carry

    lax.fori_loop(0, 23, step, 0)


def pack_left(mask, blocks):
    return pl.pallas_call(
        pack_left_kernel,
        grid=(3,),
        in_specs=[
            pl.BlockSpec((16, 16, 128), lambda g: (0, 0, 0)),
            pl.BlockSpec((8, 46, 16, BS), lambda g: (0, g, 0, 0)),
        ],
        out_specs=pl.BlockSpec((368, WIDE), lambda g: (g, 0)),
        out_shape=jax.ShapeDtypeStruct((1104, WIDE), BF16),
        compiler_params=pltpu.CompilerParams(vmem_limit_bytes=40 * MIB),
        cost_estimate=pl.CostEstimate(flops=1 << 24, bytes_accessed=14 * MIB, transcendentals=0),
        name="pack_left",
    )(mask, blocks)


def pack_right_kernel(blocks, near, rest):
    base = pl.program_id(0) % 2 * 4

    def step(n, carry):
        k = base + n
        for c in range(0, 144, 16):
            if c < 128:
                rows = pl.ds(pl.multiple_of(128 * k + c, 16), 16)
                square = blocks[n, c : c + 16]
            else:
                rows = pl.ds(pl.multiple_of(1024 + 16 * k, 16), 16)
                square = jnp.concatenate([blocks[n, 128:BS], jnp.zeros((144 - BS, 16, BS), BF16)], axis=0)
            turned = jnp.swapaxes(square, 0, 1)
            near[:, rows, :] = turned[:, :, :128]

            def put(half, value, rows=rows):
                rest[rows, 128 * half : 128 * half + 128] = value

            place_tails([widen(turned[j, :, 128:]) for j in range(16)], put, rows)
        return carry

    lax.fori_loop(0, 4, step, 0)


def pack_right(blocks):
    return pl.pallas_call(
        pack_right_kernel,
        grid=(4,),
        in_specs=[pl.BlockSpec((4, BS, 16, BS), lambda g: (g, 0, 0, 0))],
        out_specs=[
            pl.BlockSpec((16, SPAN, 128), lambda g: (0, g // 2, 0)),
            pl.BlockSpec((SPAN, 256), lambda g: (g // 2, 0)),
        ],
        out_shape=[
            jax.ShapeDtypeStruct((16, WIDE, 128), BF16),
            jax.ShapeDtypeStruct((WIDE, 256), BF16),
        ],
        compiler_params=pltpu.CompilerParams(vmem_limit_bytes=28 * MIB),
        cost_estimate=pl.CostEstimate(flops=1 << 24, bytes_accessed=30 * MIB, transcendentals=0),
        name="pack_right",
    )(blocks)


def tails_kernel(left, rest, swap, out0, out1):
    out0[...] = jnp.dot(left[: ROWS[0]], rest[...], preferred_element_type=F32)
    turned = jnp.dot(rest[...], swap[...], preferred_element_type=F32).astype(BF16)
    out1[...] = jnp.dot(left[CUT[1] :], turned, preferred_element_type=F32)


def product_tails(left, rest):
    lane = np.arange(256)
    swap = np.zeros((256, 256), np.float32)
    swap[lane, lane // 16 % 4 * 64 + lane // 64 * 16 + lane % 16] = 1.0
    return pl.pallas_call(
        tails_kernel,
        out_shape=[jax.ShapeDtypeStruct((r, 256), F32) for r in ROWS],
        compiler_params=pltpu.CompilerParams(vmem_limit_bytes=16 * MIB),
        cost_estimate=pl.CostEstimate(flops=4 * 560 * WIDE * 256, bytes_accessed=4 * MIB, transcendentals=0),
        name="product_tails",
    )(left, rest, jnp.asarray(swap, BF16))


def lanes(rows):
    return lax.broadcasted_iota(jnp.int32, (rows, 128), 1)


def scale_of(most):
    power = jnp.floor(jnp.log2(jnp.maximum(jnp.full((1, 128), most, F32), 1e-30))) + 1.0
    return power, 32000.0 * jnp.exp2(-power)


def gain_of(coded):
    power = jnp.max(jnp.where(lanes(16) % 16 == 15, coded[0:16], -1000.0))
    return jnp.exp2(jnp.full((1, 128), power, F32)) * (1.0 / 32000.0)


def code(value, gain):
    return jnp.round(value * gain).astype(jnp.int32).astype(I16)


def code_tail(value, gain, power):
    coded = jnp.where(lanes(value.shape[0]) % 16 == 15, jnp.broadcast_to(power, value.shape), jnp.round(value * gain))
    return coded.astype(jnp.int32).astype(I16)


def plain(value):
    return value.astype(jnp.int32).astype(F32)


def product_kernel(half, coded, which, left, near, tails, out, held):
    rows = ROWS[half]
    for pair in range(2):
        both = jnp.dot(
            left[CUT[half] : CUT[half] + rows],
            jnp.concatenate([near[which[2 * pair]], near[which[2 * pair + 1]]], axis=1),
            preferred_element_type=F32,
        )
        if coded:
            held[2 * pair] = both[:, :128]
            held[2 * pair + 1] = both[:, 128:]
        else:
            out[2 * pair * rows : (2 * pair + 1) * rows, :] = both[:, :128]
            out[(2 * pair + 1) * rows : (2 * pair + 2) * rows, :] = both[:, 128:]
    group = which[4]
    tail = jnp.where(group >= 2, tails[:, 128:], tails[:, :128])
    high, low = tail[:TOP], jnp.concatenate([tail[TOP:], jnp.zeros((2 * TOP - rows, 128), F32)], axis=0)
    odd = group % 2 == 1
    folded = jnp.where(
        lanes(TOP) < 64,
        jnp.where(odd, pltpu.roll(high, 64, 1), high),
        jnp.where(odd, low, pltpu.roll(low, 64, 1)),
    )
    if coded:
        power, gain = scale_of(jnp.maximum(jnp.max(jnp.abs(held[...])), jnp.max(jnp.abs(folded))))
        for n in range(4):
            out[n * rows : (n + 1) * rows, :] = code(held[n], gain)
        out[4 * rows : 4 * rows + TOP, :] = code_tail(folded, gain, power)
    else:
        out[4 * rows : 4 * rows + TOP, :] = folded


def product_group(half, coded, which, left, near, tails):
    rows = ROWS[half]
    vmem = pl.BlockSpec(memory_space=pltpu.VMEM)
    return pl.pallas_call(
        functools.partial(product_kernel, half, coded),
        in_specs=[pl.BlockSpec(memory_space=pltpu.SMEM)] + [vmem] * 3,
        out_specs=vmem,
        out_shape=jax.ShapeDtypeStruct((4 * rows + TOP, 128), I16 if coded else F32),
        scratch_shapes=[pltpu.VMEM((4, rows, 128), F32)],
        compiler_params=pltpu.CompilerParams(vmem_limit_bytes=20 * MIB),
        cost_estimate=pl.CostEstimate(flops=2 * 560 * WIDE * 512, bytes_accessed=8 * MIB, transcendentals=0),
        name="product_coded" if coded else "product_own",
    )(which, left, near, tails)


def merge_kernel(half, place, own, in1, in2, in3, mine, out1, out2, out3, held):
    rows = ROWS[half]
    parts = (in1, in2, in3)
    tails = [plain(p[4 * rows : 4 * rows + TOP, :]) for p in parts]
    gains = [gain_of(t) for t in tails]
    for n in range(4):
        here = slice(n * rows, (n + 1) * rows)
        total = own[here, :]
        for p, g in zip(parts, gains):
            total = total + plain(p[here, :]) * g
        held[n] = total
    folded = own[4 * rows : 4 * rows + TOP, :]
    for t, g in zip(tails, gains):
        folded = folded + t * g
    last = jnp.concatenate([folded[3 * FOLD :], jnp.zeros((4 * FOLD - TOP, 128), F32)], axis=0)
    pieces = [folded[0:FOLD], folded[FOLD : 2 * FOLD], folded[2 * FOLD : 3 * FOLD], last]
    slot = lanes(FOLD) // 16 % 4
    for s in range(4):

        @pl.when(place[0] == s)
        def _(s=s):
            for d, out in enumerate((mine, out1, out2, out3)):
                here = (s + d) % 4
                tail = jnp.zeros((FOLD, 128), F32)
                for q in range(4):
                    tail = jnp.where(slot == q, pltpu.roll(pieces[q], 16 * ((q - here) % 8), 1) if (q - here) % 8 else pieces[q], tail)
                main = held[here]
                if d == 0:
                    out[0:rows, :] = main
                    out[rows : rows + FOLD, :] = tail
                else:
                    tail = jnp.where(lanes(FOLD) % 16 < 10, tail, 0.0)
                    power, gain = scale_of(jnp.maximum(jnp.max(jnp.abs(main)), jnp.max(jnp.abs(tail))))
                    out[0:rows, :] = code(main, gain)
                    out[rows : rows + FOLD, :] = code_tail(tail, gain, power)


def merge(half, place, own, parts):
    vmem = pl.BlockSpec(memory_space=pltpu.VMEM)
    return pl.pallas_call(
        functools.partial(merge_kernel, half),
        in_specs=[pl.BlockSpec(memory_space=pltpu.SMEM)] + [vmem] * 4,
        out_specs=[vmem] * 4,
        out_shape=[jax.ShapeDtypeStruct((ROWS[half] + FOLD, 128), t) for t in (F32, I16, I16, I16)],
        scratch_shapes=[pltpu.VMEM((4, ROWS[half], 128), F32)],
        compiler_params=pltpu.CompilerParams(vmem_limit_bytes=24 * MIB),
        cost_estimate=pl.CostEstimate(flops=1 << 22, bytes_accessed=4 * MIB, transcendentals=0),
        name="merge",
    )(place, own, *parts)


def turn(dy, dz):
    return [(4 * y + z, (y + dy) % 4 * 4 + (z + dz) % 4) for y in range(4) for z in range(4)]


def send(array, axis, d):
    return lax.ppermute(array, "col", turn(d, 0) if axis == 0 else turn(0, d))


def exchange_products(blocks_a, pattern, blocks_b):
    place = lax.axis_index("col")
    spot = (place // 4, place % 4)
    steps = jnp.arange(4, dtype=jnp.int32)
    mask = jnp.broadcast_to(jnp.tile(pattern.T, (1, 2))[:, :, None], (16, 16, 128)).astype(BF16)
    left = pack_left(mask, jnp.transpose(blocks_a, (0, 2, 1, 3)))
    near, rest = pack_right(jnp.transpose(blocks_b, (0, 2, 1, 3)))
    tails = product_tails(left, rest)

    def group(half, d):
        g = (spot[half] + d) % 4
        which = 4 * g + steps if half == 0 else 4 * steps + g
        which = jnp.concatenate([which, g[None]]).astype(jnp.int32)
        return product_group(half, d != 0, which, left, near, tails[half])

    parts = ([], [])
    for d in (2, 1, 3):
        for half in range(2):
            parts[half].append(send(group(half, d), half, d))
    owns = [group(half, 0) for half in range(2)]
    sums = []
    for half in range(2):
        mine, *outs = merge(half, spot[1 - half].reshape(1), owns[half], parts[half])
        sums.append((mine, [send(outs[d - 1], 1 - half, d) for d in (2, 1, 3)]))
    return sums


def collocate_kernel(half, keep, ids, own, in1, in2, in3, cols, rows, *rest):
    if half == 0:
        density, out, stacked, right = rest
        before = None
    else:
        before, density, out, stacked, right = rest
    count = ROWS[half]

    @pl.when(pl.program_id(0) == 0)
    def _():
        main, fold = own[0:count, :], own[count : count + FOLD, :]
        for part in (in1, in2, in3):
            extra = plain(part[count : count + FOLD, :])
            gain = gain_of(extra)
            main, fold = main + plain(part[0:count, :]) * gain, fold + extra * gain
        tails = []
        for base, total in ((0, TOP), (4, count - TOP)):
            for q in range(4):
                piece = fold[0 : min(FOLD, total - q * FOLD)]
                shift = (128 - 16 * (q + base)) % 128
                tails.append(pltpu.roll(piece, shift, 1) if shift else piece)
        tail = jnp.where(lanes(count) < BS - 128, jnp.concatenate(tails, axis=0), 0.0)
        kept = keep[...][None]
        main = (main.reshape(count // 8, 8, 128) * kept).reshape(count, 128).astype(BF16)
        tail = (tail.reshape(count // 8, 8, 128) * kept).reshape(count, 128).astype(BF16)
        stacked[:, 0:128] = main
        stacked[:, 128:256] = tail
        density[:, :, 0:128] = main.reshape(count // 8, 8, 128)
        density[:, :, 128:BS] = tail.reshape(count // 8, 8, 128)[:, :, : BS - 128]
        right[128:256, :] = jnp.zeros((128, POINTS), BF16)

    right[0:BS, :] = cols[0]
    for t in range(POINTS // 256):
        here = slice(t * 256, (t + 1) * 256)
        inner = jnp.dot(stacked[...], right[:, here], preferred_element_type=F32).reshape(count // 8, 8, 256)
        total = jnp.sum(inner * rows[:, :, here].astype(F32), axis=0)
        within = slice(t % 4 * 256, t % 4 * 256 + 256)
        if half == 1:
            total = total + before[t // 4, :, within]
        out[t // 4, :, within] = total
    if half == 1:
        for n in range(POINTS // 1024):
            out[n, :, 1024:1152] = ids[...]


def collocate(half, keep, ids, own, parts, basis_cols, basis_rows, before):
    count = ROWS[half]
    unit = pl.BlockSpec((count + FOLD, 128), lambda g: (0, 0))
    small = pl.BlockSpec((8, 128), lambda g: (0, 0))
    wide = 1152 if half else 1024
    many = count // 8
    return pl.pallas_call(
        functools.partial(collocate_kernel, half),
        grid=(16384 // POINTS,),
        in_specs=[small, small]
        + [unit] * 4
        + [
            pl.BlockSpec((1, BS, POINTS), lambda g: (0, 0, g)),
            pl.BlockSpec(
                (pl.Element(many), pl.Element(8), pl.Element(POINTS)), lambda g: (CUT[half] // 8, 0, g * POINTS)
            ),
        ]
        + [pl.BlockSpec((POINTS // 1024, 8, 1024), lambda g: (g, 0, 0))] * half,
        out_specs=[
            pl.BlockSpec((many, 8, BS), lambda g: (0, 0, 0)),
            pl.BlockSpec((POINTS // 1024, 8, wide), lambda g: (g, 0, 0)),
        ],
        scratch_shapes=[pltpu.VMEM((count, 256), BF16), pltpu.VMEM((256, POINTS), BF16)],
        out_shape=[
            jax.ShapeDtypeStruct((many, 8, BS), BF16),
            jax.ShapeDtypeStruct((16, 8, wide), F32),
        ],
        compiler_params=pltpu.CompilerParams(vmem_limit_bytes=40 * MIB),
        cost_estimate=pl.CostEstimate(
            flops=2 * count * 256 * 16384, bytes_accessed=(count + 144) * 16384 * 2, transcendentals=0
        ),
        name="collocate",
    )(keep, ids, own, *parts, basis_cols, basis_rows, *before)


def bricks_kernel(points, out):
    owners = jnp.sum(points[:, :, 1024:1152].reshape(128, 128), axis=0, keepdims=True).astype(jnp.int32)
    onehot = (owners == lax.broadcasted_iota(jnp.int32, (128, 128), 0)).astype(F32)
    held = points[:, :, 0:1024].reshape(128, 1024)
    out[...] = jnp.dot(onehot, held, precision=HIGH, preferred_element_type=F32)


def sum_bricks(points):
    return pl.pallas_call(
        bricks_kernel,
        out_shape=jax.ShapeDtypeStruct((128, 1024), F32),
        compiler_params=pltpu.CompilerParams(vmem_limit_bytes=16 * MIB),
        cost_estimate=pl.CostEstimate(flops=2 * 128 * 128 * 1024, bytes_accessed=MIB, transcendentals=0),
        name="sum_bricks",
    )(points)


def tables():
    a = np.arange(16)
    outer = 2.0 * math.pi * (np.outer(a, a) % 16) / 16
    eye = np.eye(8)
    ck, sk = np.kron(eye, np.cos(outer)), np.kron(eye, np.sin(outer))
    b = np.arange(128)
    inner = 2.0 * math.pi * (np.outer(b, b) % 128) / 128
    c, s = np.cos(inner), np.sin(inner)
    twist = 2.0 * math.pi * np.outer(np.tile(a, 8), b) / 2048
    first = np.concatenate([ck, -sk], 0)
    second = np.block([[c, -s], [s, c]])
    third = np.block([[c, s], [-s, c]])
    last = np.concatenate([ck, -sk], 1) / 2048
    return [np.asarray(t, np.float32) for t in (first, second, third, last, np.cos(twist), np.sin(twist))]


def filter_kernel(own, in1, in2, in3, kern, first, second, third, last, tc, ts, out):
    def dot(p, q):
        return jnp.dot(p, q, precision=HIGH, preferred_element_type=F32)

    grid = (own[...] + in1[...]) + (in2[...] + in3[...])
    grid = jnp.concatenate([grid[:, y * 128 : y * 128 + 128] for y in range(8)], axis=0)
    section = dot(first[...], grid)
    re, im = section[:128], section[128:]
    c, s = tc[...], ts[...]
    spec = dot(jnp.concatenate([re * c + im * s, im * c - re * s], axis=1), second[...])
    k = kern[...]
    back = dot(spec * jnp.concatenate([k, k], axis=1), third[...])
    re, im = back[:, :128], back[:, 128:]
    turned = jnp.concatenate([re * c - im * s, im * c + re * s], axis=0)
    result = dot(last[...], turned)
    for y in range(8):
        out[:, y, :] = result[y * 16 : y * 16 + 16]


def filter_rows(pieces, kern):
    return pl.pallas_call(
        filter_kernel,
        out_shape=jax.ShapeDtypeStruct((16, 8, 128), F32),
        compiler_params=pltpu.CompilerParams(vmem_limit_bytes=16 * MIB),
        cost_estimate=pl.CostEstimate(flops=1 << 26, bytes_accessed=MIB, transcendentals=0),
        name="filter_rows",
    )(*pieces, kern, *tables())


def scatter_rows(partial):
    place = lax.axis_index("row")
    x, core = place // 2, place % 2
    halves = partial.reshape(4, 2, 16, 1024)
    away = lax.dynamic_index_in_dim(halves, 1 - core, 1, keepdims=False)
    mine = lax.dynamic_index_in_dim(halves, core, 1, keepdims=False)
    mine = mine + lax.ppermute(away, "row", [(r, r ^ 1) for r in range(8)])
    pieces = [lax.dynamic_index_in_dim(mine, x, 0, keepdims=False)]
    for d in (1, 2, 3):
        part = lax.dynamic_index_in_dim(mine, (x + d) % 4, 0, keepdims=False)
        pieces.append(lax.ppermute(part, "row", [(r, (r + 2 * d) % 8) for r in range(8)]))
    return pieces


def shards(blocks_a, pattern_a, blocks_b, filter_mask, task_brick, basis_rows, basis_cols, kernel):
    kern = jnp.transpose(kernel.reshape(8, 128, 16), (0, 2, 1)).reshape(128, 128)
    lane = jnp.arange(128, dtype=jnp.int32)
    owners = jnp.where(lane // 8 == lax.axis_index("col"), jnp.tile(task_brick.reshape(8), 16), 0)
    ids = jnp.concatenate([owners.astype(F32)[None], jnp.zeros((7, 128), F32)], axis=0)
    keep = jnp.broadcast_to(filter_mask.reshape(8, 1).astype(F32), (8, 128))
    by_point = jnp.transpose(basis_rows, (1, 0, 2))
    sums = exchange_products(blocks_a, pattern_a, blocks_b)
    densities, before = [], []
    for half in range(2):
        own, parts = sums[half]
        density, points = collocate(half, keep, ids, own, parts, basis_cols, by_point, before)
        densities.append(density)
        before = [points]
    points = lax.all_to_all(points, "col", split_axis=0, concat_axis=0, tiled=True)
    pieces = scatter_rows(sum_bricks(points))
    filtered = filter_rows(pieces, kern)
    potential = lax.all_to_all(filtered, "col", split_axis=0, concat_axis=0, tiled=True)
    density = jnp.transpose(jnp.concatenate(densities, axis=0), (1, 0, 2))
    return density[:, None], potential.reshape(128, 128)


def solution(mesh):
    return jax.shard_map(
        shards,
        mesh=mesh,
        in_specs=(
            P("row", "col", None, None),
            P("row", "col"),
            P("col", None, None, None),
            P("row", "col"),
            P("row", "col"),
            P("row", None, None),
            P("col", None, None),
            P(("row", "col"), None),
        ),
        out_specs=(P("row", "col", None, None), P("row", "col")),
        check_vma=False,
    )
```

```python
import functools
import math

import jax
import jax.numpy as jnp
import numpy as np
from jax import lax
from jax.experimental import pallas as pl
from jax.experimental.pallas import tpu as pltpu
from jax.sharding import PartitionSpec as P

BS = 138
MIB = 1 << 20
HIGH = lax.Precision.HIGHEST
F32 = jnp.float32
BF16 = jnp.bfloat16
I16 = jnp.int16
WIDE = 2304
SPAN = 1152
ROWS = (560, 544)
CUT = (0, 560)
TOP = 288
FOLD = 80
POINTS = 2048


def widen(tail):
    return jnp.concatenate([tail.astype(F32), jnp.zeros(tail.shape[:-1] + (128 - tail.shape[-1],), F32)], axis=-1)


def place_tails(tails, out, rows):
    lane = lax.broadcasted_iota(jnp.int32, (16, 128), 1) // 16
    for half in range(2):
        rest = jnp.zeros((16, 128), F32)
        for n in range(8):
            tail = tails[half * 8 + n]
            rest = jnp.where(lane == n, pltpu.roll(tail, 16 * n, 1) if n else tail, rest)
        out(half, rest.astype(BF16))


def pack_left_kernel(mask, blocks, out):
    def step(p, carry):
        pair = jnp.transpose(blocks[:, pl.ds(2 * p, 2)], (1, 0, 2, 3)).reshape(16, 16, BS)
        wide = jnp.swapaxes(pair, 0, 1)
        rows = pl.ds(pl.multiple_of(16 * p, 16), 16)
        tails = []
        for k in range(16):
            at = SPAN * (k // 8) + 128 * (k % 8)
            out[rows, at : at + 128] = wide[k, :, :128] * mask[k]
            tails.append(widen(wide[k, :, 128:] * mask[k, :, : BS - 128]))

        def put(half, value):
            out[rows, SPAN * half + 1024 : SPAN * half + 1152] = value

        place_tails(tails, put, rows)
        return carry

    lax.fori_loop(0, 23, step, 0)


def pack_left(mask, blocks):
    return pl.pallas_call(
        pack_left_kernel,
        grid=(3,),
        in_specs=[
            pl.BlockSpec((16, 16, 128), lambda g: (0, 0, 0)),
            pl.BlockSpec((8, 46, 16, BS), lambda g: (0, g, 0, 0)),
        ],
        out_specs=pl.BlockSpec((368, WIDE), lambda g: (g, 0)),
        out_shape=jax.ShapeDtypeStruct((1104, WIDE), BF16),
        compiler_params=pltpu.CompilerParams(vmem_limit_bytes=14 * MIB),
        cost_estimate=pl.CostEstimate(flops=1 << 24, bytes_accessed=14 * MIB, transcendentals=0),
        name="pack_left",
    )(mask, blocks)


def pack_right_kernel(blocks, near, rest):
    base = pl.program_id(0) % 2 * 4

    def step(n, carry):
        k = base + n
        for c in range(0, 144, 16):
            if c < 128:
                rows = pl.ds(pl.multiple_of(128 * k + c, 16), 16)
                square = blocks[n, c : c + 16]
            else:
                rows = pl.ds(pl.multiple_of(1024 + 16 * k, 16), 16)
                square = jnp.concatenate([blocks[n, 128:BS], jnp.zeros((144 - BS, 16, BS), BF16)], axis=0)
            turned = jnp.swapaxes(square, 0, 1)
            near[:, rows, :] = turned[:, :, :128]

            def put(half, value, rows=rows):
                rest[rows, 128 * half : 128 * half + 128] = value

            place_tails([widen(turned[j, :, 128:]) for j in range(16)], put, rows)
        return carry

    lax.fori_loop(0, 4, step, 0)


def pack_right(blocks):
    return pl.pallas_call(
        pack_right_kernel,
        grid=(4,),
        in_specs=[pl.BlockSpec((4, BS, 16, BS), lambda g: (g, 0, 0, 0))],
        out_specs=[
            pl.BlockSpec((16, SPAN, 128), lambda g: (0, g // 2, 0)),
            pl.BlockSpec((SPAN, 256), lambda g: (g // 2, 0)),
        ],
        out_shape=[
            jax.ShapeDtypeStruct((16, WIDE, 128), BF16),
            jax.ShapeDtypeStruct((WIDE, 256), BF16),
        ],
        compiler_params=pltpu.CompilerParams(vmem_limit_bytes=24 * MIB),
        cost_estimate=pl.CostEstimate(flops=1 << 24, bytes_accessed=30 * MIB, transcendentals=0),
        name="pack_right",
    )(blocks)


def tails_kernel(left, rest, swap, out0, out1):
    out0[...] = jnp.dot(left[: ROWS[0]], rest[...], preferred_element_type=F32)
    turned = jnp.dot(rest[...], swap[...], preferred_element_type=F32).astype(BF16)
    out1[...] = jnp.dot(left[CUT[1] :], turned, preferred_element_type=F32)


def product_tails(left, rest):
    lane = np.arange(256)
    swap = np.zeros((256, 256), np.float32)
    swap[lane, lane // 16 % 4 * 64 + lane // 64 * 16 + lane % 16] = 1.0
    return pl.pallas_call(
        tails_kernel,
        out_shape=[jax.ShapeDtypeStruct((r, 256), F32) for r in ROWS],
        compiler_params=pltpu.CompilerParams(vmem_limit_bytes=10 * MIB),
        cost_estimate=pl.CostEstimate(flops=4 * 560 * WIDE * 256, bytes_accessed=4 * MIB, transcendentals=0),
        name="product_tails",
    )(left, rest, jnp.asarray(swap, BF16))


def lanes(rows):
    return lax.broadcasted_iota(jnp.int32, (rows, 128), 1)


def scale_of(most):
    power = jnp.floor(jnp.log2(jnp.maximum(jnp.full((1, 128), most, F32), 1e-30))) + 1.0
    return power, 32000.0 * jnp.exp2(-power)


def gain_of(coded):
    power = jnp.max(jnp.where(lanes(16) % 16 == 15, coded[0:16], -1000.0))
    return jnp.exp2(jnp.full((1, 128), power, F32)) * (1.0 / 32000.0)


def code(value, gain):
    return jnp.round(value * gain).astype(jnp.int32).astype(I16)


def code_tail(value, gain, power):
    coded = jnp.where(lanes(value.shape[0]) % 16 == 15, jnp.broadcast_to(power, value.shape), jnp.round(value * gain))
    return coded.astype(jnp.int32).astype(I16)


def plain(value):
    return value.astype(jnp.int32).astype(F32)


def product_kernel(half, d, spot, left, near, tails, out, held):
    rows = ROWS[half]
    coded = d != 0
    group = (spot[half] + d) % 4
    which = [4 * group + n if half == 0 else 4 * n + group for n in range(4)]
    for pair in range(2):
        both = jnp.dot(
            left[CUT[half] : CUT[half] + rows],
            jnp.concatenate([near[which[2 * pair]], near[which[2 * pair + 1]]], axis=1),
            preferred_element_type=F32,
        )
        if coded:
            held[2 * pair] = both[:, :128]
            held[2 * pair + 1] = both[:, 128:]
        else:
            out[2 * pair * rows : (2 * pair + 1) * rows, :] = both[:, :128]
            out[(2 * pair + 1) * rows : (2 * pair + 2) * rows, :] = both[:, 128:]
    tail = jnp.where(group >= 2, tails[:, 128:], tails[:, :128])
    high, low = tail[:TOP], jnp.concatenate([tail[TOP:], jnp.zeros((2 * TOP - rows, 128), F32)], axis=0)
    odd = group % 2 == 1
    folded = jnp.where(
        lanes(TOP) < 64,
        jnp.where(odd, pltpu.roll(high, 64, 1), high),
        jnp.where(odd, low, pltpu.roll(low, 64, 1)),
    )
    if coded:
        power, gain = scale_of(jnp.maximum(jnp.max(jnp.abs(held[...])), jnp.max(jnp.abs(folded))))
        for n in range(4):
            out[n * rows : (n + 1) * rows, :] = code(held[n], gain)
        out[4 * rows : 4 * rows + TOP, :] = code_tail(folded, gain, power)
    else:
        out[4 * rows : 4 * rows + TOP, :] = folded


def product_group(half, d, spot, left, near, tails):
    rows = ROWS[half]
    coded = d != 0
    vmem = pl.BlockSpec(memory_space=pltpu.VMEM)
    return pl.pallas_call(
        functools.partial(product_kernel, half, d),
        in_specs=[pl.BlockSpec(memory_space=pltpu.SMEM)] + [vmem] * 3,
        out_specs=vmem,
        out_shape=jax.ShapeDtypeStruct((4 * rows + TOP, 128), I16 if coded else F32),
        scratch_shapes=[pltpu.VMEM((4, rows, 128), F32)],
        compiler_params=pltpu.CompilerParams(vmem_limit_bytes=10 * MIB),
        cost_estimate=pl.CostEstimate(flops=2 * 560 * WIDE * 512, bytes_accessed=8 * MIB, transcendentals=0),
        name="product_coded" if coded else "product_own",
    )(spot, left, near, tails)


def merge_kernel(half, place, own, in1, in2, in3, mine, out1, out2, out3, held):
    rows = ROWS[half]
    parts = (in1, in2, in3)
    tails = [plain(p[4 * rows : 4 * rows + TOP, :]) for p in parts]
    gains = [gain_of(t) for t in tails]
    for n in range(4):
        here = slice(n * rows, (n + 1) * rows)
        total = own[here, :]
        for p, g in zip(parts, gains):
            total = total + plain(p[here, :]) * g
        held[n] = total
    folded = own[4 * rows : 4 * rows + TOP, :]
    for t, g in zip(tails, gains):
        folded = folded + t * g
    last = jnp.concatenate([folded[3 * FOLD :], jnp.zeros((4 * FOLD - TOP, 128), F32)], axis=0)
    pieces = [folded[0:FOLD], folded[FOLD : 2 * FOLD], folded[2 * FOLD : 3 * FOLD], last]
    slot = lanes(FOLD) // 16 % 4
    for s in range(4):

        @pl.when(place[1 - half] == s)
        def _(s=s):
            for d, out in enumerate((mine, out1, out2, out3)):
                here = (s + d) % 4
                tail = jnp.zeros((FOLD, 128), F32)
                for q in range(4):
                    tail = jnp.where(slot == q, pltpu.roll(pieces[q], 16 * ((q - here) % 8), 1) if (q - here) % 8 else pieces[q], tail)
                main = held[here]
                if d == 0:
                    out[0:rows, :] = main
                    out[rows : rows + FOLD, :] = tail
                else:
                    tail = jnp.where(lanes(FOLD) % 16 < 10, tail, 0.0)
                    power, gain = scale_of(jnp.maximum(jnp.max(jnp.abs(main)), jnp.max(jnp.abs(tail))))
                    out[0:rows, :] = code(main, gain)
                    out[rows : rows + FOLD, :] = code_tail(tail, gain, power)


def merge(half, place, own, parts):
    vmem = pl.BlockSpec(memory_space=pltpu.VMEM)
    return pl.pallas_call(
        functools.partial(merge_kernel, half),
        in_specs=[pl.BlockSpec(memory_space=pltpu.SMEM)] + [vmem] * 4,
        out_specs=[vmem] * 4,
        out_shape=[jax.ShapeDtypeStruct((ROWS[half] + FOLD, 128), t) for t in (F32, I16, I16, I16)],
        scratch_shapes=[pltpu.VMEM((4, ROWS[half], 128), F32)],
        compiler_params=pltpu.CompilerParams(vmem_limit_bytes=8 * MIB),
        cost_estimate=pl.CostEstimate(flops=1 << 22, bytes_accessed=4 * MIB, transcendentals=0),
        name="merge",
    )(place, own, *parts)


def turn(dy, dz):
    return [(4 * y + z, (y + dy) % 4 * 4 + (z + dz) % 4) for y in range(4) for z in range(4)]


def send(array, axis, d):
    return lax.ppermute(array, "col", turn(d, 0) if axis == 0 else turn(0, d))


def exchange_products(blocks_a, pattern, blocks_b):
    place = lax.axis_index("col").astype(jnp.int32)
    spot = jnp.stack([place // 4, place % 4])
    mask = jnp.broadcast_to(jnp.tile(pattern.T, (1, 2))[:, :, None], (16, 16, 128)).astype(BF16)
    left = pack_left(mask, jnp.transpose(blocks_a, (0, 2, 1, 3)))
    near, rest = pack_right(jnp.transpose(blocks_b, (0, 2, 1, 3)))
    tails = product_tails(left, rest)

    def group(half, d):
        return product_group(half, d, spot, left, near, tails[half])

    parts = ([], [])
    for d in (2, 1, 3):
        for half in range(2):
            parts[half].append(send(group(half, d), half, d))
    owns = [group(half, 0) for half in range(2)]
    sums = []
    for half in range(2):
        mine, *outs = merge(half, spot, owns[half], parts[half])
        sums.append((mine, [send(outs[d - 1], 1 - half, d) for d in (2, 1, 3)]))
    return sums


def collocate_kernel(half, keep, ids, own, in1, in2, in3, cols, rows, *rest):
    if half == 0:
        density, out, stacked, right = rest
        before = None
    else:
        before, density, out, stacked, right = rest
    count = ROWS[half]

    @pl.when(pl.program_id(0) == 0)
    def _():
        main, fold = own[0:count, :], own[count : count + FOLD, :]
        for part in (in1, in2, in3):
            extra = plain(part[count : count + FOLD, :])
            gain = gain_of(extra)
            main, fold = main + plain(part[0:count, :]) * gain, fold + extra * gain
        tails = []
        for base, total in ((0, TOP), (4, count - TOP)):
            for q in range(4):
                piece = fold[0 : min(FOLD, total - q * FOLD)]
                shift = (128 - 16 * (q + base)) % 128
                tails.append(pltpu.roll(piece, shift, 1) if shift else piece)
        tail = jnp.where(lanes(count) < BS - 128, jnp.concatenate(tails, axis=0), 0.0)
        kept = keep[...][None]
        main = (main.reshape(count // 8, 8, 128) * kept).reshape(count, 128).astype(BF16)
        tail = (tail.reshape(count // 8, 8, 128) * kept).reshape(count, 128).astype(BF16)
        stacked[:, 0:128] = main
        stacked[:, 128:256] = tail
        density[:, :, 0:128] = main.reshape(count // 8, 8, 128)
        density[:, :, 128:BS] = tail.reshape(count // 8, 8, 128)[:, :, : BS - 128]
        right[128:256, :] = jnp.zeros((128, POINTS), BF16)

    right[0:BS, :] = cols[0]
    for t in range(POINTS // 256):
        here = slice(t * 256, (t + 1) * 256)
        inner = jnp.dot(stacked[...], right[:, here], preferred_element_type=F32).reshape(count // 8, 8, 256)
        total = jnp.sum(inner * rows[:, :, here].astype(F32), axis=0)
        within = slice(t % 4 * 256, t % 4 * 256 + 256)
        if half == 1:
            total = total + before[t // 4, :, within]
        out[t // 4, :, within] = total
    if half == 1:
        for n in range(POINTS // 1024):
            out[n, :, 1024:1152] = ids[...]


def collocate(half, keep, ids, own, parts, basis_cols, basis_rows, before):
    count = ROWS[half]
    unit = pl.BlockSpec((count + FOLD, 128), lambda g: (0, 0))
    small = pl.BlockSpec((8, 128), lambda g: (0, 0))
    wide = 1152 if half else 1024
    many = count // 8
    return pl.pallas_call(
        functools.partial(collocate_kernel, half),
        grid=(16384 // POINTS,),
        in_specs=[small, small]
        + [unit] * 4
        + [
            pl.BlockSpec((1, BS, POINTS), lambda g: (0, 0, g)),
            pl.BlockSpec(
                (pl.Element(many), pl.Element(8), pl.Element(POINTS)), lambda g: (CUT[half] // 8, 0, g * POINTS)
            ),
        ]
        + [pl.BlockSpec((POINTS // 1024, 8, 1024), lambda g: (g, 0, 0))] * half,
        out_specs=[
            pl.BlockSpec((many, 8, BS), lambda g: (0, 0, 0)),
            pl.BlockSpec((POINTS // 1024, 8, wide), lambda g: (g, 0, 0)),
        ],
        scratch_shapes=[pltpu.VMEM((count, 256), BF16), pltpu.VMEM((256, POINTS), BF16)],
        out_shape=[
            jax.ShapeDtypeStruct((many, 8, BS), BF16),
            jax.ShapeDtypeStruct((16, 8, wide), F32),
        ],
        compiler_params=pltpu.CompilerParams(vmem_limit_bytes=16 * MIB),
        cost_estimate=pl.CostEstimate(
            flops=2 * count * 256 * 16384, bytes_accessed=(count + 144) * 16384 * 2, transcendentals=0
        ),
        name="collocate",
    )(keep, ids, own, *parts, basis_cols, basis_rows, *before)


def bricks_kernel(points, out):
    owners = jnp.sum(points[:, :, 1024:1152].reshape(128, 128), axis=0, keepdims=True).astype(jnp.int32)
    onehot = (owners == lax.broadcasted_iota(jnp.int32, (128, 128), 0)).astype(F32)
    held = points[:, :, 0:1024].reshape(128, 1024)
    out[...] = jnp.dot(onehot, held, precision=HIGH, preferred_element_type=F32)


def sum_bricks(points):
    return pl.pallas_call(
        bricks_kernel,
        out_shape=jax.ShapeDtypeStruct((128, 1024), F32),
        compiler_params=pltpu.CompilerParams(vmem_limit_bytes=8 * MIB),
        cost_estimate=pl.CostEstimate(flops=2 * 128 * 128 * 1024, bytes_accessed=MIB, transcendentals=0),
        name="sum_bricks",
    )(points)


def tables():
    a = np.arange(16)
    outer = 2.0 * math.pi * (np.outer(a, a) % 16) / 16
    eye = np.eye(8)
    ck, sk = np.kron(eye, np.cos(outer)), np.kron(eye, np.sin(outer))
    b = np.arange(128)
    inner = 2.0 * math.pi * (np.outer(b, b) % 128) / 128
    c, s = np.cos(inner), np.sin(inner)
    twist = 2.0 * math.pi * np.outer(np.tile(a, 8), b) / 2048
    first = np.concatenate([ck, -sk], 0)
    second = np.block([[c, -s], [s, c]])
    third = np.block([[c, s], [-s, c]])
    last = np.concatenate([ck, -sk], 1) / 2048
    return [np.asarray(t, np.float32) for t in (first, second, third, last, np.cos(twist), np.sin(twist))]


def filter_kernel(own, in1, in2, in3, kern, first, second, third, last, tc, ts, out):
    def dot(p, q):
        return jnp.dot(p, q, precision=HIGH, preferred_element_type=F32)

    grid = (own[...] + in1[...]) + (in2[...] + in3[...])
    grid = jnp.concatenate([grid[:, y * 128 : y * 128 + 128] for y in range(8)], axis=0)
    section = dot(first[...], grid)
    re, im = section[:128], section[128:]
    c, s = tc[...], ts[...]
    spec = dot(jnp.concatenate([re * c + im * s, im * c - re * s], axis=1), second[...])
    k = kern[...]
    back = dot(spec * jnp.concatenate([k, k], axis=1), third[...])
    re, im = back[:, :128], back[:, 128:]
    turned = jnp.concatenate([re * c - im * s, im * c + re * s], axis=0)
    result = dot(last[...], turned)
    for y in range(8):
        out[:, y, :] = result[y * 16 : y * 16 + 16]


def filter_rows(pieces, kern):
    return pl.pallas_call(
        filter_kernel,
        out_shape=jax.ShapeDtypeStruct((16, 8, 128), F32),
        compiler_params=pltpu.CompilerParams(vmem_limit_bytes=8 * MIB),
        cost_estimate=pl.CostEstimate(flops=1 << 26, bytes_accessed=MIB, transcendentals=0),
        name="filter_rows",
    )(*pieces, kern, *tables())


def scatter_rows(partial):
    place = lax.axis_index("row")
    x, core = place // 2, place % 2
    halves = partial.reshape(4, 2, 16, 1024)
    away = lax.dynamic_index_in_dim(halves, 1 - core, 1, keepdims=False)
    mine = lax.dynamic_index_in_dim(halves, core, 1, keepdims=False)
    mine = mine + lax.ppermute(away, "row", [(r, r ^ 1) for r in range(8)])
    pieces = [lax.dynamic_index_in_dim(mine, x, 0, keepdims=False)]
    for d in (1, 2, 3):
        part = lax.dynamic_index_in_dim(mine, (x + d) % 4, 0, keepdims=False)
        pieces.append(lax.ppermute(part, "row", [(r, (r + 2 * d) % 8) for r in range(8)]))
    return pieces


def shards(blocks_a, pattern_a, blocks_b, filter_mask, task_brick, basis_rows, basis_cols, kernel):
    kern = jnp.transpose(kernel.reshape(8, 128, 16), (0, 2, 1)).reshape(128, 128)
    lane = jnp.arange(128, dtype=jnp.int32)
    owners = jnp.where(lane // 8 == lax.axis_index("col"), jnp.tile(task_brick.reshape(8), 16), 0)
    ids = jnp.concatenate([owners.astype(F32)[None], jnp.zeros((7, 128), F32)], axis=0)
    keep = jnp.broadcast_to(filter_mask.reshape(8, 1).astype(F32), (8, 128))
    by_point = jnp.transpose(basis_rows, (1, 0, 2))
    sums = exchange_products(blocks_a, pattern_a, blocks_b)
    densities, before = [], []
    for half in range(2):
        own, parts = sums[half]
        density, points = collocate(half, keep, ids, own, parts, basis_cols, by_point, before)
        densities.append(density)
        before = [points]
    points = lax.all_to_all(points, "col", split_axis=0, concat_axis=0, tiled=True)
    pieces = scatter_rows(sum_bricks(points))
    filtered = filter_rows(pieces, kern)
    potential = lax.all_to_all(filtered, "col", split_axis=0, concat_axis=0, tiled=True)
    density = jnp.transpose(jnp.concatenate(densities, axis=0), (1, 0, 2))
    return density[:, None], potential.reshape(128, 128)


def solution(mesh):
    return jax.shard_map(
        shards,
        mesh=mesh,
        in_specs=(
            P("row", "col", None, None),
            P("row", "col"),
            P("col", None, None, None),
            P("row", "col"),
            P("row", "col"),
            P("row", None, None),
            P("col", None, None),
            P(("row", "col"), None),
        ),
        out_specs=(P("row", "col", None, None), P("row", "col")),
        check_vma=False,
    )
```

```python
import functools
import math

import jax
import jax.numpy as jnp
import numpy as np
from jax import lax
from jax.experimental import pallas as pl
from jax.experimental.pallas import tpu as pltpu
from jax.sharding import PartitionSpec as P

BS = 138
MIB = 1 << 20
HIGH = lax.Precision.HIGHEST
F32 = jnp.float32
BF16 = jnp.bfloat16
I16 = jnp.int16
WIDE = 2304
SPAN = 1152
ROWS = (560, 544)
CUT = (0, 560)
TOP = 288
FOLD = 80
POINTS = 2048


def widen(tail):
    return jnp.concatenate([tail.astype(F32), jnp.zeros(tail.shape[:-1] + (128 - tail.shape[-1],), F32)], axis=-1)


def place_tails(tails, out, rows):
    lane = lax.broadcasted_iota(jnp.int32, (16, 128), 1) // 16
    for half in range(2):
        rest = jnp.zeros((16, 128), F32)
        for n in range(8):
            tail = tails[half * 8 + n]
            rest = jnp.where(lane == n, pltpu.roll(tail, 16 * n, 1) if n else tail, rest)
        out(half, rest.astype(BF16))


def pack_left_kernel(pairs, mask, blocks, after, out):
    def step(p, carry):
        pair = jnp.transpose(blocks[:, pl.ds(2 * p, 2)], (1, 0, 2, 3)).reshape(16, 16, BS)
        wide = jnp.swapaxes(pair, 0, 1)
        rows = pl.ds(pl.multiple_of(16 * p, 16), 16)
        tails = []
        for k in range(16):
            at = SPAN * (k // 8) + 128 * (k % 8)
            out[rows, at : at + 128] = wide[k, :, :128] * mask[k]
            tails.append(widen(wide[k, :, 128:] * mask[k, :, : BS - 128]))

        def put(half, value):
            out[rows, SPAN * half + 1024 : SPAN * half + 1152] = value

        place_tails(tails, put, rows)
        return carry

    lax.fori_loop(0, pairs, step, 0)


def pack_left(half, mask, blocks, after):
    count = (14, 34)[half]
    return pl.pallas_call(
        functools.partial(pack_left_kernel, count // 2),
        grid=(ROWS[half] // 8 // count,),
        in_specs=[
            pl.BlockSpec((16, 16, 128), lambda g: (0, 0, 0)),
            pl.BlockSpec(
                (pl.Element(8), pl.Element(count), pl.Element(16), pl.Element(BS)),
                lambda g: (0, CUT[half] // 8 + count * g, 0, 0),
            ),
            pl.BlockSpec(memory_space=pl.ANY),
        ],
        out_specs=pl.BlockSpec((count * 8, WIDE), lambda g: (g, 0)),
        out_shape=jax.ShapeDtypeStruct((ROWS[half], WIDE), BF16),
        compiler_params=pltpu.CompilerParams(vmem_limit_bytes=32 * MIB),
        cost_estimate=pl.CostEstimate(flops=1 << 24, bytes_accessed=7 * MIB, transcendentals=0),
        name="pack_left",
    )(mask, blocks, after)


def pack_right_kernel(blocks, near):
    base = pl.program_id(0) % 4 * 2

    def step(n, carry):
        k = base + n
        for c in range(0, 144, 16):
            if c < 128:
                rows = pl.ds(pl.multiple_of(128 * k + c, 16), 16)
                square = blocks[n, c : c + 16]
            else:
                rows = pl.ds(pl.multiple_of(1024 + 16 * k, 16), 16)
                square = jnp.concatenate([blocks[n, 128:BS], jnp.zeros((144 - BS, 16, BS), BF16)], axis=0)
            near[:, rows, :] = jnp.swapaxes(square, 0, 1)
        return carry

    lax.fori_loop(0, 2, step, 0)


def pack_right(blocks):
    return pl.pallas_call(
        pack_right_kernel,
        grid=(8,),
        in_specs=[pl.BlockSpec((2, BS, 16, BS), lambda g: (g, 0, 0, 0))],
        out_specs=pl.BlockSpec((16, SPAN, BS), lambda g: (0, g // 4, 0)),
        out_shape=jax.ShapeDtypeStruct((16, WIDE, BS), BF16),
        compiler_params=pltpu.CompilerParams(vmem_limit_bytes=36 * MIB),
        cost_estimate=pl.CostEstimate(flops=1 << 24, bytes_accessed=38 * MIB, transcendentals=0),
        name="pack_right",
    )(blocks)


def lanes(rows):
    return lax.broadcasted_iota(jnp.int32, (rows, 128), 1)


def scale_of(most):
    power = jnp.floor(jnp.log2(jnp.maximum(jnp.full((1, 128), most, F32), 1e-30))) + 1.0
    return power, 32000.0 * jnp.exp2(-power)


def gain_of(coded):
    power = jnp.max(jnp.where(lanes(16) % 16 == 15, coded[0:16], -1000.0))
    return jnp.exp2(jnp.full((1, 128), power, F32)) * (1.0 / 32000.0)


def code(value, gain):
    return jnp.round(value * gain).astype(jnp.int32).astype(I16)


def code_tail(value, gain, power):
    coded = jnp.where(lanes(value.shape[0]) % 16 == 15, jnp.broadcast_to(power, value.shape), jnp.round(value * gain))
    return coded.astype(jnp.int32).astype(I16)


def plain(value):
    return value.astype(jnp.int32).astype(F32)


def product_kernel(half, d, spot, left, near, after, out, held):
    rows = ROWS[half]
    coded = d != 0
    group = (spot[half] + d) % 4
    slot = lanes(rows) // 16
    tail = jnp.zeros((rows, 128), F32)
    for n in range(4):
        both = jnp.dot(left[...], near[4 * group + n if half == 0 else 4 * n + group], preferred_element_type=F32)
        if coded:
            held[n] = both[:, :128]
        else:
            out[n * rows : (n + 1) * rows, :] = both[:, :128]
        piece = widen(both[:, 128:])
        tail = jnp.where(slot == n, pltpu.roll(piece, 16 * n, 1) if n else piece, tail)
    high, low = tail[:TOP], jnp.concatenate([tail[TOP:], jnp.zeros((2 * TOP - rows, 128), F32)], axis=0)
    folded = jnp.where(lanes(TOP) < 64, high, pltpu.roll(low, 64, 1))
    if coded:
        power, gain = scale_of(jnp.maximum(jnp.max(jnp.abs(held[...])), jnp.max(jnp.abs(folded))))
        for n in range(4):
            out[n * rows : (n + 1) * rows, :] = code(held[n], gain)
        out[4 * rows : 4 * rows + TOP, :] = code_tail(folded, gain, power)
    else:
        out[4 * rows : 4 * rows + TOP, :] = folded


def product_group(half, d, spot, left, near, after):
    rows = ROWS[half]
    coded = d != 0
    vmem = pl.BlockSpec(memory_space=pltpu.VMEM)
    return pl.pallas_call(
        functools.partial(product_kernel, half, d),
        in_specs=[pl.BlockSpec(memory_space=pltpu.SMEM), vmem, vmem, pl.BlockSpec(memory_space=pl.ANY)],
        out_specs=vmem,
        out_shape=jax.ShapeDtypeStruct((4 * rows + TOP, 128), I16 if coded else F32),
        scratch_shapes=[pltpu.VMEM((4, rows, 128), F32)],
        compiler_params=pltpu.CompilerParams(vmem_limit_bytes=12 * MIB),
        cost_estimate=pl.CostEstimate(flops=2 * 560 * WIDE * 1024, bytes_accessed=8 * MIB, transcendentals=0),
        name="product_coded" if coded else "product_own",
    )(spot, left, near, after)


def merge_kernel(half, place, own, in1, in2, in3, after, mine, out1, out2, out3, held):
    rows = ROWS[half]
    parts = (in1, in2, in3)
    tails = [plain(p[4 * rows : 4 * rows + TOP, :]) for p in parts]
    gains = [gain_of(t) for t in tails]
    for n in range(4):
        here = slice(n * rows, (n + 1) * rows)
        total = own[here, :]
        for p, g in zip(parts, gains):
            total = total + plain(p[here, :]) * g
        held[n] = total
    folded = own[4 * rows : 4 * rows + TOP, :]
    for t, g in zip(tails, gains):
        folded = folded + t * g
    last = jnp.concatenate([folded[3 * FOLD :], jnp.zeros((4 * FOLD - TOP, 128), F32)], axis=0)
    pieces = [folded[0:FOLD], folded[FOLD : 2 * FOLD], folded[2 * FOLD : 3 * FOLD], last]
    slot = lanes(FOLD) // 16 % 4
    for s in range(4):

        @pl.when(place[1 - half] == s)
        def _(s=s):
            for d, out in enumerate((mine, out1, out2, out3)):
                here = (s + d) % 4
                tail = jnp.zeros((FOLD, 128), F32)
                for q in range(4):
                    tail = jnp.where(slot == q, pltpu.roll(pieces[q], 16 * ((q - here) % 8), 1) if (q - here) % 8 else pieces[q], tail)
                main = held[here]
                if d == 0:
                    out[0:rows, :] = main
                    out[rows : rows + FOLD, :] = tail
                else:
                    tail = jnp.where(lanes(FOLD) % 16 < 10, tail, 0.0)
                    power, gain = scale_of(jnp.maximum(jnp.max(jnp.abs(main)), jnp.max(jnp.abs(tail))))
                    out[0:rows, :] = code(main, gain)
                    out[rows : rows + FOLD, :] = code_tail(tail, gain, power)


def merge(half, place, own, parts, after):
    vmem = pl.BlockSpec(memory_space=pltpu.VMEM)
    return pl.pallas_call(
        functools.partial(merge_kernel, half),
        in_specs=[pl.BlockSpec(memory_space=pltpu.SMEM)] + [vmem] * 4 + [pl.BlockSpec(memory_space=pl.ANY)],
        out_specs=[vmem] * 4,
        out_shape=[jax.ShapeDtypeStruct((ROWS[half] + FOLD, 128), t) for t in (F32, I16, I16, I16)],
        scratch_shapes=[pltpu.VMEM((4, ROWS[half], 128), F32)],
        compiler_params=pltpu.CompilerParams(vmem_limit_bytes=8 * MIB),
        cost_estimate=pl.CostEstimate(flops=1 << 22, bytes_accessed=4 * MIB, transcendentals=0),
        name="merge",
    )(place, own, *parts, after)


def turn(dy, dz):
    return [(4 * y + z, (y + dy) % 4 * 4 + (z + dz) % 4) for y in range(4) for z in range(4)]


def send(array, axis, d):
    return lax.ppermute(array, "col", turn(d, 0) if axis == 0 else turn(0, d))


def exchange_products(blocks_a, pattern, blocks_b):
    place = lax.axis_index("col").astype(jnp.int32)
    spot = jnp.stack([place // 4, place % 4])
    mask = jnp.broadcast_to(jnp.tile(pattern.T, (1, 2))[:, :, None], (16, 16, 128)).astype(BF16)
    blocks_a = jnp.transpose(blocks_a, (0, 2, 1, 3))
    near = pack_right(jnp.transpose(blocks_b, (0, 2, 1, 3)))
    after = near
    parts, owns = ([], []), []
    lefts = []
    for half in range(2):
        left = pack_left(half, mask, blocks_a, after)
        lefts.append(left)
        after = left
        for d in (2, 1, 3):
            after = product_group(half, d, spot, left, near, after)
            parts[half].append(send(after, half, d))
    for half in range(2):
        after = product_group(half, 0, spot, lefts[half], near, after)
        owns.append(after)

    def finish(half, after):
        mine, *outs = merge(half, spot, owns[half], parts[half], after)
        return mine, [send(outs[d - 1], 1 - half, d) for d in (2, 1, 3)]

    return finish, after


def collocate_kernel(half, keep, ids, own, in1, in2, in3, cols, rows, *rest):
    if half == 0:
        density, out, stacked, right = rest
        before = None
    else:
        before, density, out, stacked, right = rest
    count = ROWS[half]

    @pl.when(pl.program_id(0) == 0)
    def _():
        main, fold = own[0:count, :], own[count : count + FOLD, :]
        for part in (in1, in2, in3):
            extra = plain(part[count : count + FOLD, :])
            gain = gain_of(extra)
            main, fold = main + plain(part[0:count, :]) * gain, fold + extra * gain
        tails = []
        for base, total in ((0, TOP), (4, count - TOP)):
            for q in range(4):
                piece = fold[0 : min(FOLD, total - q * FOLD)]
                shift = (128 - 16 * (q + base)) % 128
                tails.append(pltpu.roll(piece, shift, 1) if shift else piece)
        tail = jnp.where(lanes(count) < BS - 128, jnp.concatenate(tails, axis=0), 0.0)
        kept = keep[...][None]
        main = (main.reshape(count // 8, 8, 128) * kept).reshape(count, 128).astype(BF16)
        tail = (tail.reshape(count // 8, 8, 128) * kept).reshape(count, 128).astype(BF16)
        stacked[:, 0:128] = main
        stacked[:, 128:256] = tail
        density[:, :, 0:128] = main.reshape(count // 8, 8, 128)
        density[:, :, 128:BS] = tail.reshape(count // 8, 8, 128)[:, :, : BS - 128]
        right[128:256, :] = jnp.zeros((128, POINTS), BF16)

    right[0:BS, :] = cols[0]
    for t in range(POINTS // 256):
        here = slice(t * 256, (t + 1) * 256)
        inner = jnp.dot(stacked[...], right[:, here], preferred_element_type=F32).reshape(count // 8, 8, 256)
        total = jnp.sum(inner * rows[:, :, here].astype(F32), axis=0)
        within = slice(t % 4 * 256, t % 4 * 256 + 256)
        if half == 1:
            total = total + before[t // 4, :, within]
        out[t // 4, :, within] = total
    if half == 1:
        for n in range(POINTS // 1024):
            out[n, :, 1024:1152] = ids[...]


def collocate(half, keep, ids, own, parts, basis_cols, basis_rows, before):
    count = ROWS[half]
    unit = pl.BlockSpec((count + FOLD, 128), lambda g: (0, 0))
    small = pl.BlockSpec((8, 128), lambda g: (0, 0))
    wide = 1152 if half else 1024
    many = count // 8
    return pl.pallas_call(
        functools.partial(collocate_kernel, half),
        grid=(16384 // POINTS,),
        in_specs=[small, small]
        + [unit] * 4
        + [
            pl.BlockSpec((1, BS, POINTS), lambda g: (0, 0, g)),
            pl.BlockSpec(
                (pl.Element(many), pl.Element(8), pl.Element(POINTS)), lambda g: (CUT[half] // 8, 0, g * POINTS)
            ),
        ]
        + [pl.BlockSpec((POINTS // 1024, 8, 1024), lambda g: (g, 0, 0))] * half,
        out_specs=[
            pl.BlockSpec((many, 8, BS), lambda g: (0, 0, 0)),
            pl.BlockSpec((POINTS // 1024, 8, wide), lambda g: (g, 0, 0)),
        ],
        scratch_shapes=[pltpu.VMEM((count, 256), BF16), pltpu.VMEM((256, POINTS), BF16)],
        out_shape=[
            jax.ShapeDtypeStruct((many, 8, BS), BF16),
            jax.ShapeDtypeStruct((16, 8, wide), F32),
        ],
        compiler_params=pltpu.CompilerParams(vmem_limit_bytes=16 * MIB),
        cost_estimate=pl.CostEstimate(
            flops=2 * count * 256 * 16384, bytes_accessed=(count + 144) * 16384 * 2, transcendentals=0
        ),
        name="collocate",
    )(keep, ids, own, *parts, basis_cols, basis_rows, *before)


def bricks_kernel(points, out):
    owners = jnp.sum(points[:, :, 1024:1152].reshape(128, 128), axis=0, keepdims=True).astype(jnp.int32)
    onehot = (owners == lax.broadcasted_iota(jnp.int32, (128, 128), 0)).astype(F32)
    held = points[:, :, 0:1024].reshape(128, 1024)
    out[...] = jnp.dot(onehot, held, precision=HIGH, preferred_element_type=F32)


def sum_bricks(points):
    return pl.pallas_call(
        bricks_kernel,
        out_shape=jax.ShapeDtypeStruct((128, 1024), F32),
        compiler_params=pltpu.CompilerParams(vmem_limit_bytes=8 * MIB),
        cost_estimate=pl.CostEstimate(flops=2 * 128 * 128 * 1024, bytes_accessed=MIB, transcendentals=0),
        name="sum_bricks",
    )(points)


def tables():
    a = np.arange(16)
    outer = 2.0 * math.pi * (np.outer(a, a) % 16) / 16
    eye = np.eye(8)
    ck, sk = np.kron(eye, np.cos(outer)), np.kron(eye, np.sin(outer))
    b = np.arange(128)
    inner = 2.0 * math.pi * (np.outer(b, b) % 128) / 128
    c, s = np.cos(inner), np.sin(inner)
    twist = 2.0 * math.pi * np.outer(np.tile(a, 8), b) / 2048
    first = np.concatenate([ck, -sk], 0)
    second = np.block([[c, -s], [s, c]])
    third = np.block([[c, s], [-s, c]])
    last = np.concatenate([ck, -sk], 1) / 2048
    return [np.asarray(t, np.float32) for t in (first, second, third, last, np.cos(twist), np.sin(twist))]


def filter_kernel(own, in1, in2, in3, kern, first, second, third, last, tc, ts, out):
    def dot(p, q):
        return jnp.dot(p, q, precision=HIGH, preferred_element_type=F32)

    grid = (own[...] + in1[...]) + (in2[...] + in3[...])
    grid = jnp.concatenate([grid[:, y * 128 : y * 128 + 128] for y in range(8)], axis=0)
    section = dot(first[...], grid)
    re, im = section[:128], section[128:]
    c, s = tc[...], ts[...]
    spec = dot(jnp.concatenate([re * c + im * s, im * c - re * s], axis=1), second[...])
    k = kern[...]
    back = dot(spec * jnp.concatenate([k, k], axis=1), third[...])
    re, im = back[:, :128], back[:, 128:]
    turned = jnp.concatenate([re * c - im * s, im * c + re * s], axis=0)
    result = dot(last[...], turned)
    for y in range(8):
        out[:, y, :] = result[y * 16 : y * 16 + 16]


def filter_rows(pieces, kern):
    return pl.pallas_call(
        filter_kernel,
        out_shape=jax.ShapeDtypeStruct((16, 8, 128), F32),
        compiler_params=pltpu.CompilerParams(vmem_limit_bytes=8 * MIB),
        cost_estimate=pl.CostEstimate(flops=1 << 26, bytes_accessed=MIB, transcendentals=0),
        name="filter_rows",
    )(*pieces, kern, *tables())


def scatter_rows(partial):
    place = lax.axis_index("row")
    x, core = place // 2, place % 2
    halves = partial.reshape(4, 2, 16, 1024)
    away = lax.dynamic_index_in_dim(halves, 1 - core, 1, keepdims=False)
    mine = lax.dynamic_index_in_dim(halves, core, 1, keepdims=False)
    mine = mine + lax.ppermute(away, "row", [(r, r ^ 1) for r in range(8)])
    pieces = [lax.dynamic_index_in_dim(mine, x, 0, keepdims=False)]
    for d in (1, 2, 3):
        part = lax.dynamic_index_in_dim(mine, (x + d) % 4, 0, keepdims=False)
        pieces.append(lax.ppermute(part, "row", [(r, (r + 2 * d) % 8) for r in range(8)]))
    return pieces


def shards(blocks_a, pattern_a, blocks_b, filter_mask, task_brick, basis_rows, basis_cols, kernel):
    kern = jnp.transpose(kernel.reshape(8, 128, 16), (0, 2, 1)).reshape(128, 128)
    lane = jnp.arange(128, dtype=jnp.int32)
    owners = jnp.where(lane // 8 == lax.axis_index("col"), jnp.tile(task_brick.reshape(8), 16), 0)
    ids = jnp.concatenate([owners.astype(F32)[None], jnp.zeros((7, 128), F32)], axis=0)
    keep = jnp.broadcast_to(filter_mask.reshape(8, 1).astype(F32), (8, 128))
    by_point = jnp.transpose(basis_rows, (1, 0, 2))
    finish, after = exchange_products(blocks_a, pattern_a, blocks_b)
    densities, before, sums = [], [], []
    for half in range(2):
        sums.append(finish(half, after))
        after = sums[-1][0]
    for half in range(2):
        own, parts = sums[half]
        density, points = collocate(half, keep, ids, own, parts, basis_cols, by_point, before)
        densities.append(density)
        before = [points]
    points = lax.all_to_all(points, "col", split_axis=0, concat_axis=0, tiled=True)
    pieces = scatter_rows(sum_bricks(points))
    filtered = filter_rows(pieces, kern)
    potential = lax.all_to_all(filtered, "col", split_axis=0, concat_axis=0, tiled=True)
    density = jnp.transpose(jnp.concatenate(densities, axis=0), (1, 0, 2))
    return density[:, None], potential.reshape(128, 128)


def solution(mesh):
    return jax.shard_map(
        shards,
        mesh=mesh,
        in_specs=(
            P("row", "col", None, None),
            P("row", "col"),
            P("col", None, None, None),
            P("row", "col"),
            P("row", "col"),
            P("row", None, None),
            P("col", None, None),
            P(("row", "col"), None),
        ),
        out_specs=(P("row", "col", None, None), P("row", "col")),
        check_vma=False,
    )
```

```python
import functools
import math

import jax
import jax.numpy as jnp
import numpy as np
from jax import lax
from jax.experimental import pallas as pl
from jax.experimental.pallas import tpu as pltpu
from jax.sharding import PartitionSpec as P

BS = 138
MIB = 1 << 20
HIGH = lax.Precision.HIGHEST
F32 = jnp.float32
BF16 = jnp.bfloat16
I16 = jnp.int16
WIDE = 2304
SPAN = 1152
ROWS = (560, 544)
CUT = (0, 560)
TOP = 288
FOLD = 80
POINTS = 2048


def in_hbm(array):
    return pltpu.with_memory_space_constraint(array, pltpu.HBM)


def widen(tail):
    return jnp.concatenate([tail.astype(F32), jnp.zeros(tail.shape[:-1] + (128 - tail.shape[-1],), F32)], axis=-1)


def place_tails(tails, out, rows):
    lane = lax.broadcasted_iota(jnp.int32, (16, 128), 1) // 16
    for half in range(2):
        rest = jnp.zeros((16, 128), F32)
        for n in range(8):
            tail = tails[half * 8 + n]
            rest = jnp.where(lane == n, pltpu.roll(tail, 16 * n, 1) if n else tail, rest)
        out(half, rest.astype(BF16))


def pack_left_kernel(pairs, mask, blocks, after, out):
    def step(p, carry):
        pair = jnp.transpose(blocks[:, pl.ds(2 * p, 2)], (1, 0, 2, 3)).reshape(16, 16, BS)
        wide = jnp.swapaxes(pair, 0, 1)
        rows = pl.ds(pl.multiple_of(16 * p, 16), 16)
        tails = []
        for k in range(16):
            at = SPAN * (k // 8) + 128 * (k % 8)
            out[rows, at : at + 128] = wide[k, :, :128] * mask[k]
            tails.append(widen(wide[k, :, 128:] * mask[k, :, : BS - 128]))

        def put(half, value):
            out[rows, SPAN * half + 1024 : SPAN * half + 1152] = value

        place_tails(tails, put, rows)
        return carry

    lax.fori_loop(0, pairs, step, 0)


def pack_left(half, mask, blocks, after):
    count = (14, 34)[half]
    return pl.pallas_call(
        functools.partial(pack_left_kernel, count // 2),
        grid=(ROWS[half] // 8 // count,),
        in_specs=[
            pl.BlockSpec((16, 16, 128), lambda g: (0, 0, 0)),
            pl.BlockSpec(
                (pl.Element(8), pl.Element(count), pl.Element(16), pl.Element(BS)),
                lambda g: (0, CUT[half] // 8 + count * g, 0, 0),
            ),
            pl.BlockSpec(memory_space=pl.ANY),
        ],
        out_specs=pl.BlockSpec((count * 8, WIDE), lambda g: (g, 0)),
        out_shape=pltpu.VMEM((ROWS[half], WIDE), BF16),
        compiler_params=pltpu.CompilerParams(vmem_limit_bytes=32 * MIB),
        cost_estimate=pl.CostEstimate(flops=1 << 24, bytes_accessed=7 * MIB, transcendentals=0),
        name="pack_left",
    )(mask, in_hbm(blocks), after)


def pack_right_kernel(blocks, near, rest):
    base = pl.program_id(0) % 4 * 2

    def step(n, carry):
        k = base + n
        for c in range(0, 144, 16):
            if c < 128:
                rows = pl.ds(pl.multiple_of(128 * k + c, 16), 16)
                square = blocks[n, c : c + 16]
            else:
                rows = pl.ds(pl.multiple_of(1024 + 16 * k, 16), 16)
                square = jnp.concatenate([blocks[n, 128:BS], jnp.zeros((144 - BS, 16, BS), BF16)], axis=0)
            turned = jnp.swapaxes(square, 0, 1)
            near[:, rows, :] = turned[:, :, :128]

            def put(half, value, rows=rows):
                rest[rows, 128 * half : 128 * half + 128] = value

            place_tails([widen(turned[j, :, 128:]) for j in range(16)], put, rows)
        return carry

    lax.fori_loop(0, 2, step, 0)


def pack_right(blocks):
    return pl.pallas_call(
        pack_right_kernel,
        grid=(8,),
        in_specs=[pl.BlockSpec((2, BS, 16, BS), lambda g: (g, 0, 0, 0))],
        out_specs=[
            pl.BlockSpec((16, SPAN, 128), lambda g: (0, g // 4, 0)),
            pl.BlockSpec((SPAN, 256), lambda g: (g // 4, 0)),
        ],
        out_shape=[
            pltpu.VMEM((16, WIDE, 128), BF16),
            pltpu.VMEM((WIDE, 256), BF16),
        ],
        compiler_params=pltpu.CompilerParams(vmem_limit_bytes=24 * MIB),
        cost_estimate=pl.CostEstimate(flops=1 << 24, bytes_accessed=30 * MIB, transcendentals=0),
        name="pack_right",
    )(in_hbm(blocks))


def tails_kernel(half, left, rest, swap, after, out):
    right = rest[...]
    if half == 1:
        right = jnp.dot(right, swap[...], preferred_element_type=F32).astype(BF16)
    out[...] = jnp.dot(left[...], right, preferred_element_type=F32)


def product_tails(half, left, rest, after):
    lane = np.arange(256)
    swap = np.zeros((256, 256), np.float32)
    swap[lane, lane // 16 % 4 * 64 + lane // 64 * 16 + lane % 16] = 1.0
    vmem = pl.BlockSpec(memory_space=pltpu.VMEM)
    return pl.pallas_call(
        functools.partial(tails_kernel, half),
        in_specs=[vmem] * 3 + [pl.BlockSpec(memory_space=pl.ANY)],
        out_specs=vmem,
        out_shape=jax.ShapeDtypeStruct((ROWS[half], 256), F32),
        compiler_params=pltpu.CompilerParams(vmem_limit_bytes=12 * MIB),
        cost_estimate=pl.CostEstimate(flops=2 * 560 * WIDE * 256, bytes_accessed=4 * MIB, transcendentals=0),
        name="product_tails",
    )(left, rest, jnp.asarray(swap, BF16), after)


def lanes(rows):
    return lax.broadcasted_iota(jnp.int32, (rows, 128), 1)


def scale_of(most):
    power = jnp.floor(jnp.log2(jnp.maximum(jnp.full((1, 128), most, F32), 1e-30))) + 1.0
    return power, 32000.0 * jnp.exp2(-power)


def gain_of(coded):
    power = jnp.max(jnp.where(lanes(16) % 16 == 15, coded[0:16], -1000.0))
    return jnp.exp2(jnp.full((1, 128), power, F32)) * (1.0 / 32000.0)


def code(value, gain):
    return jnp.round(value * gain).astype(jnp.int32).astype(I16)


def code_tail(value, gain, power):
    coded = jnp.where(lanes(value.shape[0]) % 16 == 15, jnp.broadcast_to(power, value.shape), jnp.round(value * gain))
    return coded.astype(jnp.int32).astype(I16)


def plain(value):
    return value.astype(jnp.int32).astype(F32)


def product_kernel(half, d, spot, left, near, tails, after, out, held):
    rows = ROWS[half]
    coded = d != 0
    group = (spot[half] + d) % 4
    which = [4 * group + n if half == 0 else 4 * n + group for n in range(4)]
    for pair in range(2):
        both = jnp.dot(
            left[...],
            jnp.concatenate([near[which[2 * pair]], near[which[2 * pair + 1]]], axis=1),
            preferred_element_type=F32,
        )
        if coded:
            held[2 * pair] = both[:, :128]
            held[2 * pair + 1] = both[:, 128:]
        else:
            out[2 * pair * rows : (2 * pair + 1) * rows, :] = both[:, :128]
            out[(2 * pair + 1) * rows : (2 * pair + 2) * rows, :] = both[:, 128:]
    tail = jnp.where(group >= 2, tails[:, 128:], tails[:, :128])
    high, low = tail[:TOP], jnp.concatenate([tail[TOP:], jnp.zeros((2 * TOP - rows, 128), F32)], axis=0)
    odd = group % 2 == 1
    folded = jnp.where(
        lanes(TOP) < 64,
        jnp.where(odd, pltpu.roll(high, 64, 1), high),
        jnp.where(odd, low, pltpu.roll(low, 64, 1)),
    )
    if coded:
        power, gain = scale_of(jnp.maximum(jnp.max(jnp.abs(held[...])), jnp.max(jnp.abs(folded))))
        for n in range(4):
            out[n * rows : (n + 1) * rows, :] = code(held[n], gain)
        out[4 * rows : 4 * rows + TOP, :] = code_tail(folded, gain, power)
    else:
        out[4 * rows : 4 * rows + TOP, :] = folded


def product_group(half, d, spot, left, near, tails, after):
    rows = ROWS[half]
    coded = d != 0
    vmem = pl.BlockSpec(memory_space=pltpu.VMEM)
    return pl.pallas_call(
        functools.partial(product_kernel, half, d),
        in_specs=[pl.BlockSpec(memory_space=pltpu.SMEM)] + [vmem] * 3 + [pl.BlockSpec(memory_space=pl.ANY)],
        out_specs=vmem,
        out_shape=jax.ShapeDtypeStruct((4 * rows + TOP, 128), I16 if coded else F32),
        scratch_shapes=[pltpu.VMEM((4, rows, 128), F32)],
        compiler_params=pltpu.CompilerParams(vmem_limit_bytes=10 * MIB),
        cost_estimate=pl.CostEstimate(flops=2 * 560 * WIDE * 512, bytes_accessed=8 * MIB, transcendentals=0),
        name="product_coded" if coded else "product_own",
    )(spot, left, near, tails, after)


def merge_kernel(half, place, own, in1, in2, in3, after, mine, out1, out2, out3, held):
    rows = ROWS[half]
    parts = (in1, in2, in3)
    tails = [plain(p[4 * rows : 4 * rows + TOP, :]) for p in parts]
    gains = [gain_of(t) for t in tails]
    for n in range(4):
        here = slice(n * rows, (n + 1) * rows)
        total = own[here, :]
        for p, g in zip(parts, gains):
            total = total + plain(p[here, :]) * g
        held[n] = total
    folded = own[4 * rows : 4 * rows + TOP, :]
    for t, g in zip(tails, gains):
        folded = folded + t * g
    last = jnp.concatenate([folded[3 * FOLD :], jnp.zeros((4 * FOLD - TOP, 128), F32)], axis=0)
    pieces = [folded[0:FOLD], folded[FOLD : 2 * FOLD], folded[2 * FOLD : 3 * FOLD], last]
    slot = lanes(FOLD) // 16 % 4
    for s in range(4):

        @pl.when(place[1 - half] == s)
        def _(s=s):
            for d, out in enumerate((mine, out1, out2, out3)):
                here = (s + d) % 4
                tail = jnp.zeros((FOLD, 128), F32)
                for q in range(4):
                    tail = jnp.where(slot == q, pltpu.roll(pieces[q], 16 * ((q - here) % 8), 1) if (q - here) % 8 else pieces[q], tail)
                main = held[here]
                if d == 0:
                    out[0:rows, :] = main
                    out[rows : rows + FOLD, :] = tail
                else:
                    tail = jnp.where(lanes(FOLD) % 16 < 10, tail, 0.0)
                    power, gain = scale_of(jnp.maximum(jnp.max(jnp.abs(main)), jnp.max(jnp.abs(tail))))
                    out[0:rows, :] = code(main, gain)
                    out[rows : rows + FOLD, :] = code_tail(tail, gain, power)


def merge(half, place, own, parts, after):
    vmem = pl.BlockSpec(memory_space=pltpu.VMEM)
    return pl.pallas_call(
        functools.partial(merge_kernel, half),
        in_specs=[pl.BlockSpec(memory_space=pltpu.SMEM)] + [vmem] * 4 + [pl.BlockSpec(memory_space=pl.ANY)],
        out_specs=[vmem] * 4,
        out_shape=[jax.ShapeDtypeStruct((ROWS[half] + FOLD, 128), t) for t in (F32, I16, I16, I16)],
        scratch_shapes=[pltpu.VMEM((4, ROWS[half], 128), F32)],
        compiler_params=pltpu.CompilerParams(vmem_limit_bytes=8 * MIB),
        cost_estimate=pl.CostEstimate(flops=1 << 22, bytes_accessed=4 * MIB, transcendentals=0),
        name="merge",
    )(place, own, *parts, after)


def turn(dy, dz):
    return [(4 * y + z, (y + dy) % 4 * 4 + (z + dz) % 4) for y in range(4) for z in range(4)]


def send(array, axis, d):
    return lax.ppermute(array, "col", turn(d, 0) if axis == 0 else turn(0, d))


def exchange_products(blocks_a, pattern, blocks_b):
    place = lax.axis_index("col").astype(jnp.int32)
    spot = jnp.stack([place // 4, place % 4])
    mask = jnp.broadcast_to(jnp.tile(pattern.T, (1, 2))[:, :, None], (16, 16, 128)).astype(BF16)
    blocks_a = jnp.transpose(blocks_a, (0, 2, 1, 3))
    near, rest = pack_right(jnp.transpose(blocks_b, (0, 2, 1, 3)))
    after = near
    parts, owns = ([], []), []
    lefts = []
    for half in range(2):
        left = pack_left(half, mask, blocks_a, after)
        tails = product_tails(half, left, rest, after)
        lefts.append((left, near, tails))
        after = tails
        for d in (2, 1, 3):
            after = product_group(half, d, spot, *lefts[half], after)
            parts[half].append(send(after, half, d))
    for half in range(2):
        after = product_group(half, 0, spot, *lefts[half], after)
        owns.append(after)

    def finish(half, after):
        mine, *outs = merge(half, spot, owns[half], parts[half], after)
        return mine, [send(outs[d - 1], 1 - half, d) for d in (2, 1, 3)]

    return finish, after


def collocate_kernel(half, keep, ids, own, in1, in2, in3, cols, rows, *rest):
    if half == 0:
        density, out, stacked, right = rest
        before = None
    else:
        before, density, out, stacked, right = rest
    count = ROWS[half]

    @pl.when(pl.program_id(0) == 0)
    def _():
        main, fold = own[0:count, :], own[count : count + FOLD, :]
        for part in (in1, in2, in3):
            extra = plain(part[count : count + FOLD, :])
            gain = gain_of(extra)
            main, fold = main + plain(part[0:count, :]) * gain, fold + extra * gain
        tails = []
        for base, total in ((0, TOP), (4, count - TOP)):
            for q in range(4):
                piece = fold[0 : min(FOLD, total - q * FOLD)]
                shift = (128 - 16 * (q + base)) % 128
                tails.append(pltpu.roll(piece, shift, 1) if shift else piece)
        tail = jnp.where(lanes(count) < BS - 128, jnp.concatenate(tails, axis=0), 0.0)
        kept = keep[...][None]
        main = (main.reshape(count // 8, 8, 128) * kept).reshape(count, 128).astype(BF16)
        tail = (tail.reshape(count // 8, 8, 128) * kept).reshape(count, 128).astype(BF16)
        stacked[:, 0:128] = main
        stacked[:, 128:256] = tail
        density[:, :, 0:128] = main.reshape(count // 8, 8, 128)
        density[:, :, 128:BS] = tail.reshape(count // 8, 8, 128)[:, :, : BS - 128]
        right[128:256, :] = jnp.zeros((128, POINTS), BF16)

    right[0:BS, :] = cols[0]
    for t in range(POINTS // 256):
        here = slice(t * 256, (t + 1) * 256)
        inner = jnp.dot(stacked[...], right[:, here], preferred_element_type=F32).reshape(count // 8, 8, 256)
        total = jnp.sum(inner * rows[:, :, here].astype(F32), axis=0)
        within = slice(t % 4 * 256, t % 4 * 256 + 256)
        if half == 1:
            total = total + before[t // 4, :, within]
        out[t // 4, :, within] = total
    if half == 1:
        for n in range(POINTS // 1024):
            out[n, :, 1024:1152] = ids[...]


def collocate(half, keep, ids, own, parts, basis_cols, basis_rows, before):
    count = ROWS[half]
    unit = pl.BlockSpec((count + FOLD, 128), lambda g: (0, 0))
    small = pl.BlockSpec((8, 128), lambda g: (0, 0))
    wide = 1152 if half else 1024
    many = count // 8
    return pl.pallas_call(
        functools.partial(collocate_kernel, half),
        grid=(16384 // POINTS,),
        in_specs=[small, small]
        + [unit] * 4
        + [
            pl.BlockSpec((1, BS, POINTS), lambda g: (0, 0, g)),
            pl.BlockSpec(
                (pl.Element(many), pl.Element(8), pl.Element(POINTS)), lambda g: (CUT[half] // 8, 0, g * POINTS)
            ),
        ]
        + [pl.BlockSpec((POINTS // 1024, 8, 1024), lambda g: (g, 0, 0))] * half,
        out_specs=[
            pl.BlockSpec((many, 8, BS), lambda g: (0, 0, 0)),
            pl.BlockSpec((POINTS // 1024, 8, wide), lambda g: (g, 0, 0)),
        ],
        scratch_shapes=[pltpu.VMEM((count, 256), BF16), pltpu.VMEM((256, POINTS), BF16)],
        out_shape=[
            jax.ShapeDtypeStruct((many, 8, BS), BF16),
            jax.ShapeDtypeStruct((16, 8, wide), F32),
        ],
        compiler_params=pltpu.CompilerParams(vmem_limit_bytes=16 * MIB),
        cost_estimate=pl.CostEstimate(
            flops=2 * count * 256 * 16384, bytes_accessed=(count + 144) * 16384 * 2, transcendentals=0
        ),
        name="collocate",
    )(keep, ids, own, *parts, in_hbm(basis_cols), in_hbm(basis_rows), *before)


def bricks_kernel(points, out):
    owners = jnp.sum(points[:, :, 1024:1152].reshape(128, 128), axis=0, keepdims=True).astype(jnp.int32)
    onehot = (owners == lax.broadcasted_iota(jnp.int32, (128, 128), 0)).astype(F32)
    held = points[:, :, 0:1024].reshape(128, 1024)
    out[...] = jnp.dot(onehot, held, precision=HIGH, preferred_element_type=F32)


def sum_bricks(points):
    return pl.pallas_call(
        bricks_kernel,
        out_shape=jax.ShapeDtypeStruct((128, 1024), F32),
        compiler_params=pltpu.CompilerParams(vmem_limit_bytes=8 * MIB),
        cost_estimate=pl.CostEstimate(flops=2 * 128 * 128 * 1024, bytes_accessed=MIB, transcendentals=0),
        name="sum_bricks",
    )(points)


def tables():
    a = np.arange(16)
    outer = 2.0 * math.pi * (np.outer(a, a) % 16) / 16
    eye = np.eye(8)
    ck, sk = np.kron(eye, np.cos(outer)), np.kron(eye, np.sin(outer))
    b = np.arange(128)
    inner = 2.0 * math.pi * (np.outer(b, b) % 128) / 128
    c, s = np.cos(inner), np.sin(inner)
    twist = 2.0 * math.pi * np.outer(np.tile(a, 8), b) / 2048
    first = np.concatenate([ck, -sk], 0)
    second = np.block([[c, -s], [s, c]])
    third = np.block([[c, s], [-s, c]])
    last = np.concatenate([ck, -sk], 1) / 2048
    return [np.asarray(t, np.float32) for t in (first, second, third, last, np.cos(twist), np.sin(twist))]


def filter_kernel(own, in1, in2, in3, kern, first, second, third, last, tc, ts, out):
    def dot(p, q):
        return jnp.dot(p, q, precision=HIGH, preferred_element_type=F32)

    grid = (own[...] + in1[...]) + (in2[...] + in3[...])
    grid = jnp.concatenate([grid[:, y * 128 : y * 128 + 128] for y in range(8)], axis=0)
    section = dot(first[...], grid)
    re, im = section[:128], section[128:]
    c, s = tc[...], ts[...]
    spec = dot(jnp.concatenate([re * c + im * s, im * c - re * s], axis=1), second[...])
    k = kern[...]
    back = dot(spec * jnp.concatenate([k, k], axis=1), third[...])
    re, im = back[:, :128], back[:, 128:]
    turned = jnp.concatenate([re * c - im * s, im * c + re * s], axis=0)
    result = dot(last[...], turned)
    for y in range(8):
        out[:, y, :] = result[y * 16 : y * 16 + 16]


def filter_rows(pieces, kern):
    return pl.pallas_call(
        filter_kernel,
        out_shape=jax.ShapeDtypeStruct((16, 8, 128), F32),
        compiler_params=pltpu.CompilerParams(vmem_limit_bytes=8 * MIB),
        cost_estimate=pl.CostEstimate(flops=1 << 26, bytes_accessed=MIB, transcendentals=0),
        name="filter_rows",
    )(*pieces, kern, *tables())


def scatter_rows(partial):
    place = lax.axis_index("row")
    x, core = place // 2, place % 2
    halves = partial.reshape(4, 2, 16, 1024)
    away = lax.dynamic_index_in_dim(halves, 1 - core, 1, keepdims=False)
    mine = lax.dynamic_index_in_dim(halves, core, 1, keepdims=False)
    mine = mine + lax.ppermute(away, "row", [(r, r ^ 1) for r in range(8)])
    pieces = [lax.dynamic_index_in_dim(mine, x, 0, keepdims=False)]
    for d in (1, 2, 3):
        part = lax.dynamic_index_in_dim(mine, (x + d) % 4, 0, keepdims=False)
        pieces.append(lax.ppermute(part, "row", [(r, (r + 2 * d) % 8) for r in range(8)]))
    return pieces


def shards(blocks_a, pattern_a, blocks_b, filter_mask, task_brick, basis_rows, basis_cols, kernel):
    kern = jnp.transpose(kernel.reshape(8, 128, 16), (0, 2, 1)).reshape(128, 128)
    lane = jnp.arange(128, dtype=jnp.int32)
    owners = jnp.where(lane // 8 == lax.axis_index("col"), jnp.tile(task_brick.reshape(8), 16), 0)
    ids = jnp.concatenate([owners.astype(F32)[None], jnp.zeros((7, 128), F32)], axis=0)
    keep = jnp.broadcast_to(filter_mask.reshape(8, 1).astype(F32), (8, 128))
    by_point = jnp.transpose(basis_rows, (1, 0, 2))
    finish, after = exchange_products(blocks_a, pattern_a, blocks_b)
    densities, before, sums = [], [], []
    for half in range(2):
        sums.append(finish(half, after))
        after = sums[-1][0]
    for half in range(2):
        own, parts = sums[half]
        density, points = collocate(half, keep, ids, own, parts, basis_cols, by_point, before)
        densities.append(density)
        before = [points]
    points = lax.all_to_all(points, "col", split_axis=0, concat_axis=0, tiled=True)
    pieces = scatter_rows(sum_bricks(points))
    filtered = filter_rows(pieces, kern)
    potential = lax.all_to_all(filtered, "col", split_axis=0, concat_axis=0, tiled=True)
    density = jnp.transpose(jnp.concatenate(densities, axis=0), (1, 0, 2))
    return density[:, None], potential.reshape(128, 128)


def solution(mesh):
    return jax.shard_map(
        shards,
        mesh=mesh,
        in_specs=(
            P("row", "col", None, None),
            P("row", "col"),
            P("col", None, None, None),
            P("row", "col"),
            P("row", "col"),
            P("row", None, None),
            P("col", None, None),
            P(("row", "col"), None),
        ),
        out_specs=(P("row", "col", None, None), P("row", "col")),
        check_vma=False,
    )
```

```python
import functools
import math

import jax
import jax.numpy as jnp
import numpy as np
from jax import lax
from jax.experimental import pallas as pl
from jax.experimental.pallas import tpu as pltpu
from jax.sharding import PartitionSpec as P

BS = 138
MIB = 1 << 20
HIGH = lax.Precision.HIGHEST
F32 = jnp.float32
BF16 = jnp.bfloat16
I16 = jnp.int16
WIDE = 2304
SPAN = 1152
ROWS = (560, 544)
CUT = (0, 560)
TOP = 288
FOLD = 80
POINTS = 2048


def in_hbm(array):
    return pltpu.with_memory_space_constraint(array, pltpu.HBM)


def widen(tail):
    return jnp.concatenate([tail.astype(F32), jnp.zeros(tail.shape[:-1] + (128 - tail.shape[-1],), F32)], axis=-1)


def place_tails(tails, out, rows):
    lane = lax.broadcasted_iota(jnp.int32, (16, 128), 1) // 16
    for half in range(2):
        rest = jnp.zeros((16, 128), F32)
        for n in range(8):
            tail = tails[half * 8 + n]
            rest = jnp.where(lane == n, pltpu.roll(tail, 16 * n, 1) if n else tail, rest)
        out(half, rest.astype(BF16))


def pack_left_kernel(pairs, mask, blocks, after, out):
    def step(p, carry):
        pair = jnp.transpose(blocks[:, pl.ds(2 * p, 2)], (1, 0, 2, 3)).reshape(16, 16, BS)
        wide = jnp.swapaxes(pair, 0, 1)
        rows = pl.ds(pl.multiple_of(16 * p, 16), 16)
        tails = []
        for k in range(16):
            at = SPAN * (k // 8) + 128 * (k % 8)
            out[rows, at : at + 128] = wide[k, :, :128] * mask[k]
            tails.append(widen(wide[k, :, 128:] * mask[k, :, : BS - 128]))

        def put(half, value):
            out[rows, SPAN * half + 1024 : SPAN * half + 1152] = value

        place_tails(tails, put, rows)
        return carry

    lax.fori_loop(0, pairs, step, 0)


def pack_left(half, mask, blocks, after):
    count = (14, 34)[half]
    return pl.pallas_call(
        functools.partial(pack_left_kernel, count // 2),
        grid=(ROWS[half] // 8 // count,),
        in_specs=[
            pl.BlockSpec((16, 16, 128), lambda g: (0, 0, 0)),
            pl.BlockSpec(
                (pl.Element(8), pl.Element(count), pl.Element(16), pl.Element(BS)),
                lambda g: (0, CUT[half] // 8 + count * g, 0, 0),
            ),
            pl.BlockSpec(memory_space=pl.ANY),
        ],
        out_specs=pl.BlockSpec((count * 8, WIDE), lambda g: (g, 0)),
        out_shape=pltpu.VMEM((ROWS[half], WIDE), BF16),
        compiler_params=pltpu.CompilerParams(vmem_limit_bytes=32 * MIB),
        cost_estimate=pl.CostEstimate(flops=1 << 24, bytes_accessed=7 * MIB, transcendentals=0),
        name="pack_left",
    )(mask, in_hbm(blocks), after)


def pack_right_kernel(blocks, *others):
    near, rest = others[-2:]
    base = pl.program_id(0) % 4 * 2

    def step(n, carry):
        k = base + n
        for c in range(0, 144, 16):
            if c < 128:
                rows = pl.ds(pl.multiple_of(128 * k + c, 16), 16)
                square = blocks[n, c : c + 16]
            else:
                rows = pl.ds(pl.multiple_of(1024 + 16 * k, 16), 16)
                square = jnp.concatenate([blocks[n, 128:BS], jnp.zeros((144 - BS, 16, BS), BF16)], axis=0)
            turned = jnp.swapaxes(square, 0, 1)
            near[:, rows, :] = turned[:, :, :128]

            def put(half, value, rows=rows):
                rest[rows, 128 * half : 128 * half + 128] = value

            place_tails([widen(turned[j, :, 128:]) for j in range(16)], put, rows)
        return carry

    lax.fori_loop(0, 2, step, 0)


def pack_right(blocks, before):
    return pl.pallas_call(
        pack_right_kernel,
        grid=(8,),
        in_specs=[pl.BlockSpec((2, BS, 16, BS), lambda g: (g, 0, 0, 0))]
        + [pl.BlockSpec(memory_space=pl.ANY)] * len(before),
        out_specs=[
            pl.BlockSpec((16, SPAN, 128), lambda g: (0, g // 4, 0)),
            pl.BlockSpec((SPAN, 256), lambda g: (g // 4, 0)),
        ],
        out_shape=[
            pltpu.VMEM((16, WIDE, 128), BF16),
            pltpu.VMEM((WIDE, 256), BF16),
        ],
        compiler_params=pltpu.CompilerParams(vmem_limit_bytes=24 * MIB),
        cost_estimate=pl.CostEstimate(flops=1 << 24, bytes_accessed=30 * MIB, transcendentals=0),
        name="pack_right",
    )(in_hbm(blocks), *before)


def tails_kernel(half, left, rest, swap, after, out):
    right = rest[...]
    if half == 1:
        right = jnp.dot(right, swap[...], preferred_element_type=F32).astype(BF16)
    out[...] = jnp.dot(left[...], right, preferred_element_type=F32)


def product_tails(half, left, rest, after):
    lane = np.arange(256)
    swap = np.zeros((256, 256), np.float32)
    swap[lane, lane // 16 % 4 * 64 + lane // 64 * 16 + lane % 16] = 1.0
    vmem = pl.BlockSpec(memory_space=pltpu.VMEM)
    return pl.pallas_call(
        functools.partial(tails_kernel, half),
        in_specs=[vmem] * 3 + [pl.BlockSpec(memory_space=pl.ANY)],
        out_specs=vmem,
        out_shape=jax.ShapeDtypeStruct((ROWS[half], 256), F32),
        compiler_params=pltpu.CompilerParams(vmem_limit_bytes=12 * MIB),
        cost_estimate=pl.CostEstimate(flops=2 * 560 * WIDE * 256, bytes_accessed=4 * MIB, transcendentals=0),
        name="product_tails",
    )(left, rest, jnp.asarray(swap, BF16), after)


def lanes(rows):
    return lax.broadcasted_iota(jnp.int32, (rows, 128), 1)


def scale_of(most):
    power = jnp.floor(jnp.log2(jnp.maximum(jnp.full((1, 128), most, F32), 1e-30))) + 1.0
    return power, 32000.0 * jnp.exp2(-power)


def gain_of(coded):
    power = jnp.max(jnp.where(lanes(16) % 16 == 15, coded[0:16], -1000.0))
    return jnp.exp2(jnp.full((1, 128), power, F32)) * (1.0 / 32000.0)


def code(value, gain):
    return jnp.round(value * gain).astype(jnp.int32).astype(I16)


def code_tail(value, gain, power):
    coded = jnp.where(lanes(value.shape[0]) % 16 == 15, jnp.broadcast_to(power, value.shape), jnp.round(value * gain))
    return coded.astype(jnp.int32).astype(I16)


def plain(value):
    return value.astype(jnp.int32).astype(F32)


def product_kernel(half, d, spot, left, near, tails, after, out, held):
    rows = ROWS[half]
    coded = d != 0
    group = (spot[half] + d) % 4
    which = [4 * group + n if half == 0 else 4 * n + group for n in range(4)]
    for pair in range(2):
        both = jnp.dot(
            left[...],
            jnp.concatenate([near[which[2 * pair]], near[which[2 * pair + 1]]], axis=1),
            preferred_element_type=F32,
        )
        if coded:
            held[2 * pair] = both[:, :128]
            held[2 * pair + 1] = both[:, 128:]
        else:
            out[2 * pair * rows : (2 * pair + 1) * rows, :] = both[:, :128]
            out[(2 * pair + 1) * rows : (2 * pair + 2) * rows, :] = both[:, 128:]
    tail = jnp.where(group >= 2, tails[:, 128:], tails[:, :128])
    high, low = tail[:TOP], jnp.concatenate([tail[TOP:], jnp.zeros((2 * TOP - rows, 128), F32)], axis=0)
    odd = group % 2 == 1
    folded = jnp.where(
        lanes(TOP) < 64,
        jnp.where(odd, pltpu.roll(high, 64, 1), high),
        jnp.where(odd, low, pltpu.roll(low, 64, 1)),
    )
    if coded:
        power, gain = scale_of(jnp.maximum(jnp.max(jnp.abs(held[...])), jnp.max(jnp.abs(folded))))
        for n in range(4):
            out[n * rows : (n + 1) * rows, :] = code(held[n], gain)
        out[4 * rows : 4 * rows + TOP, :] = code_tail(folded, gain, power)
    else:
        out[4 * rows : 4 * rows + TOP, :] = folded


def product_group(half, d, spot, left, near, tails, after):
    rows = ROWS[half]
    coded = d != 0
    vmem = pl.BlockSpec(memory_space=pltpu.VMEM)
    return pl.pallas_call(
        functools.partial(product_kernel, half, d),
        in_specs=[pl.BlockSpec(memory_space=pltpu.SMEM)] + [vmem] * 3 + [pl.BlockSpec(memory_space=pl.ANY)],
        out_specs=vmem,
        out_shape=jax.ShapeDtypeStruct((4 * rows + TOP, 128), I16 if coded else F32),
        scratch_shapes=[pltpu.VMEM((4, rows, 128), F32)],
        compiler_params=pltpu.CompilerParams(vmem_limit_bytes=10 * MIB),
        cost_estimate=pl.CostEstimate(flops=2 * 560 * WIDE * 512, bytes_accessed=8 * MIB, transcendentals=0),
        name="product_coded" if coded else "product_own",
    )(spot, left, near, tails, after)


def merge_kernel(half, place, own, in1, in2, in3, after, mine, out1, out2, out3, held):
    rows = ROWS[half]
    parts = (in1, in2, in3)
    tails = [plain(p[4 * rows : 4 * rows + TOP, :]) for p in parts]
    gains = [gain_of(t) for t in tails]
    for n in range(4):
        here = slice(n * rows, (n + 1) * rows)
        total = own[here, :]
        for p, g in zip(parts, gains):
            total = total + plain(p[here, :]) * g
        held[n] = total
    folded = own[4 * rows : 4 * rows + TOP, :]
    for t, g in zip(tails, gains):
        folded = folded + t * g
    last = jnp.concatenate([folded[3 * FOLD :], jnp.zeros((4 * FOLD - TOP, 128), F32)], axis=0)
    pieces = [folded[0:FOLD], folded[FOLD : 2 * FOLD], folded[2 * FOLD : 3 * FOLD], last]
    slot = lanes(FOLD) // 16 % 4
    for s in range(4):

        @pl.when(place[1 - half] == s)
        def _(s=s):
            for d, out in enumerate((mine, out1, out2, out3)):
                here = (s + d) % 4
                tail = jnp.zeros((FOLD, 128), F32)
                for q in range(4):
                    tail = jnp.where(slot == q, pltpu.roll(pieces[q], 16 * ((q - here) % 8), 1) if (q - here) % 8 else pieces[q], tail)
                main = held[here]
                if d == 0:
                    out[0:rows, :] = main
                    out[rows : rows + FOLD, :] = tail
                else:
                    tail = jnp.where(lanes(FOLD) % 16 < 10, tail, 0.0)
                    power, gain = scale_of(jnp.maximum(jnp.max(jnp.abs(main)), jnp.max(jnp.abs(tail))))
                    out[0:rows, :] = code(main, gain)
                    out[rows : rows + FOLD, :] = code_tail(tail, gain, power)


def merge(half, place, own, parts, after):
    vmem = pl.BlockSpec(memory_space=pltpu.VMEM)
    return pl.pallas_call(
        functools.partial(merge_kernel, half),
        in_specs=[pl.BlockSpec(memory_space=pltpu.SMEM)] + [vmem] * 4 + [pl.BlockSpec(memory_space=pl.ANY)],
        out_specs=[vmem] * 4,
        out_shape=[jax.ShapeDtypeStruct((ROWS[half] + FOLD, 128), t) for t in (F32, I16, I16, I16)],
        scratch_shapes=[pltpu.VMEM((4, ROWS[half], 128), F32)],
        compiler_params=pltpu.CompilerParams(vmem_limit_bytes=8 * MIB),
        cost_estimate=pl.CostEstimate(flops=1 << 22, bytes_accessed=4 * MIB, transcendentals=0),
        name="merge",
    )(place, own, *parts, after)


def turn(dy, dz):
    return [(4 * y + z, (y + dy) % 4 * 4 + (z + dz) % 4) for y in range(4) for z in range(4)]


def send(array, axis, d):
    return lax.ppermute(array, "col", turn(d, 0) if axis == 0 else turn(0, d))


def exchange_products(blocks_a, pattern, blocks_b, before):
    place = lax.axis_index("col").astype(jnp.int32)
    spot = jnp.stack([place // 4, place % 4])
    mask = jnp.broadcast_to(jnp.tile(pattern.T, (1, 2))[:, :, None], (16, 16, 128)).astype(BF16)
    blocks_a = jnp.transpose(blocks_a, (0, 2, 1, 3))
    near, rest = pack_right(jnp.transpose(blocks_b, (0, 2, 1, 3)), [mask, spot] + before)
    after = near
    parts, owns = ([], []), []
    lefts = []
    for half in range(2):
        left = pack_left(half, mask, blocks_a, after)
        tails = product_tails(half, left, rest, after)
        lefts.append((left, near, tails))
        after = tails
        for d in (2, 1, 3):
            after = product_group(half, d, spot, *lefts[half], after)
            parts[half].append(send(after, half, d))
    for half in range(2):
        after = product_group(half, 0, spot, *lefts[half], after)
        owns.append(after)

    def finish(half, after):
        mine, *outs = merge(half, spot, owns[half], parts[half], after)
        return mine, [send(outs[d - 1], 1 - half, d) for d in (2, 1, 3)]

    return finish, after


def collocate_kernel(half, keep, ids, own, in1, in2, in3, cols, rows, *rest):
    if half == 0:
        density, out, stacked, right = rest
        before = None
    else:
        before, density, out, stacked, right = rest
    count = ROWS[half]

    @pl.when(pl.program_id(0) == 0)
    def _():
        main, fold = own[0:count, :], own[count : count + FOLD, :]
        for part in (in1, in2, in3):
            extra = plain(part[count : count + FOLD, :])
            gain = gain_of(extra)
            main, fold = main + plain(part[0:count, :]) * gain, fold + extra * gain
        tails = []
        for base, total in ((0, TOP), (4, count - TOP)):
            for q in range(4):
                piece = fold[0 : min(FOLD, total - q * FOLD)]
                shift = (128 - 16 * (q + base)) % 128
                tails.append(pltpu.roll(piece, shift, 1) if shift else piece)
        tail = jnp.where(lanes(count) < BS - 128, jnp.concatenate(tails, axis=0), 0.0)
        kept = keep[...][None]
        main = (main.reshape(count // 8, 8, 128) * kept).reshape(count, 128).astype(BF16)
        tail = (tail.reshape(count // 8, 8, 128) * kept).reshape(count, 128).astype(BF16)
        stacked[:, 0:128] = main
        stacked[:, 128:256] = tail
        density[:, :, 0:128] = main.reshape(count // 8, 8, 128)
        density[:, :, 128:BS] = tail.reshape(count // 8, 8, 128)[:, :, : BS - 128]
        right[128:256, :] = jnp.zeros((128, POINTS), BF16)

    right[0:BS, :] = cols[0]
    for t in range(POINTS // 256):
        here = slice(t * 256, (t + 1) * 256)
        inner = jnp.dot(stacked[...], right[:, here], preferred_element_type=F32).reshape(count // 8, 8, 256)
        total = jnp.sum(inner * rows[:, :, here].astype(F32), axis=0)
        within = slice(t % 4 * 256, t % 4 * 256 + 256)
        if half == 1:
            total = total + before[t // 4, :, within]
        out[t // 4, :, within] = total
    if half == 1:
        for n in range(POINTS // 1024):
            out[n, :, 1024:1152] = ids[...]


def collocate(half, keep, ids, own, parts, basis_cols, basis_rows, before):
    count = ROWS[half]
    unit = pl.BlockSpec((count + FOLD, 128), lambda g: (0, 0))
    small = pl.BlockSpec((8, 128), lambda g: (0, 0))
    wide = 1152 if half else 1024
    many = count // 8
    return pl.pallas_call(
        functools.partial(collocate_kernel, half),
        grid=(16384 // POINTS,),
        in_specs=[small, small]
        + [unit] * 4
        + [
            pl.BlockSpec((1, BS, POINTS), lambda g: (0, 0, g)),
            pl.BlockSpec(
                (pl.Element(many), pl.Element(8), pl.Element(POINTS)), lambda g: (CUT[half] // 8, 0, g * POINTS)
            ),
        ]
        + [pl.BlockSpec((POINTS // 1024, 8, 1024), lambda g: (g, 0, 0))] * half,
        out_specs=[
            pl.BlockSpec((many, 8, BS), lambda g: (0, 0, 0)),
            pl.BlockSpec((POINTS // 1024, 8, wide), lambda g: (g, 0, 0)),
        ],
        scratch_shapes=[pltpu.VMEM((count, 256), BF16), pltpu.VMEM((256, POINTS), BF16)],
        out_shape=[
            jax.ShapeDtypeStruct((many, 8, BS), BF16),
            jax.ShapeDtypeStruct((16, 8, wide), F32),
        ],
        compiler_params=pltpu.CompilerParams(vmem_limit_bytes=16 * MIB),
        cost_estimate=pl.CostEstimate(
            flops=2 * count * 256 * 16384, bytes_accessed=(count + 144) * 16384 * 2, transcendentals=0
        ),
        name="collocate",
    )(keep, ids, own, *parts, in_hbm(basis_cols), in_hbm(basis_rows), *before)


def bricks_kernel(points, out):
    owners = jnp.sum(points[:, :, 1024:1152].reshape(128, 128), axis=0, keepdims=True).astype(jnp.int32)
    onehot = (owners == lax.broadcasted_iota(jnp.int32, (128, 128), 0)).astype(F32)
    held = points[:, :, 0:1024].reshape(128, 1024)
    out[...] = jnp.dot(onehot, held, precision=HIGH, preferred_element_type=F32)


def sum_bricks(points):
    return pl.pallas_call(
        bricks_kernel,
        out_shape=jax.ShapeDtypeStruct((128, 1024), F32),
        compiler_params=pltpu.CompilerParams(vmem_limit_bytes=8 * MIB),
        cost_estimate=pl.CostEstimate(flops=2 * 128 * 128 * 1024, bytes_accessed=MIB, transcendentals=0),
        name="sum_bricks",
    )(points)


def tables():
    a = np.arange(16)
    outer = 2.0 * math.pi * (np.outer(a, a) % 16) / 16
    eye = np.eye(8)
    ck, sk = np.kron(eye, np.cos(outer)), np.kron(eye, np.sin(outer))
    b = np.arange(128)
    inner = 2.0 * math.pi * (np.outer(b, b) % 128) / 128
    c, s = np.cos(inner), np.sin(inner)
    twist = 2.0 * math.pi * np.outer(np.tile(a, 8), b) / 2048
    first = np.concatenate([ck, -sk], 0)
    second = np.block([[c, -s], [s, c]])
    third = np.block([[c, s], [-s, c]])
    last = np.concatenate([ck, -sk], 1) / 2048
    return [np.asarray(t, np.float32) for t in (first, second, third, last, np.cos(twist), np.sin(twist))]


def filter_kernel(own, in1, in2, in3, kern, first, second, third, last, tc, ts, out):
    def dot(p, q):
        return jnp.dot(p, q, precision=HIGH, preferred_element_type=F32)

    grid = (own[...] + in1[...]) + (in2[...] + in3[...])
    grid = jnp.concatenate([grid[:, y * 128 : y * 128 + 128] for y in range(8)], axis=0)
    section = dot(first[...], grid)
    re, im = section[:128], section[128:]
    c, s = tc[...], ts[...]
    spec = dot(jnp.concatenate([re * c + im * s, im * c - re * s], axis=1), second[...])
    k = kern[...]
    back = dot(spec * jnp.concatenate([k, k], axis=1), third[...])
    re, im = back[:, :128], back[:, 128:]
    turned = jnp.concatenate([re * c - im * s, im * c + re * s], axis=0)
    result = dot(last[...], turned)
    for y in range(8):
        out[:, y, :] = result[y * 16 : y * 16 + 16]


def filter_rows(pieces, kern):
    return pl.pallas_call(
        filter_kernel,
        out_shape=jax.ShapeDtypeStruct((16, 8, 128), F32),
        compiler_params=pltpu.CompilerParams(vmem_limit_bytes=8 * MIB),
        cost_estimate=pl.CostEstimate(flops=1 << 26, bytes_accessed=MIB, transcendentals=0),
        name="filter_rows",
    )(*pieces, kern, *tables())


def scatter_rows(partial):
    place = lax.axis_index("row")
    x, core = place // 2, place % 2
    halves = partial.reshape(4, 2, 16, 1024)
    away = lax.dynamic_index_in_dim(halves, 1 - core, 1, keepdims=False)
    mine = lax.dynamic_index_in_dim(halves, core, 1, keepdims=False)
    mine = mine + lax.ppermute(away, "row", [(r, r ^ 1) for r in range(8)])
    pieces = [lax.dynamic_index_in_dim(mine, x, 0, keepdims=False)]
    for d in (1, 2, 3):
        part = lax.dynamic_index_in_dim(mine, (x + d) % 4, 0, keepdims=False)
        pieces.append(lax.ppermute(part, "row", [(r, (r + 2 * d) % 8) for r in range(8)]))
    return pieces


def shards(blocks_a, pattern_a, blocks_b, filter_mask, task_brick, basis_rows, basis_cols, kernel):
    kern = jnp.transpose(kernel.reshape(8, 128, 16), (0, 2, 1)).reshape(128, 128)
    lane = jnp.arange(128, dtype=jnp.int32)
    owners = jnp.where(lane // 8 == lax.axis_index("col"), jnp.tile(task_brick.reshape(8), 16), 0)
    ids = jnp.concatenate([owners.astype(F32)[None], jnp.zeros((7, 128), F32)], axis=0)
    keep = jnp.broadcast_to(filter_mask.reshape(8, 1).astype(F32), (8, 128))
    by_point = jnp.transpose(basis_rows, (1, 0, 2))
    finish, after = exchange_products(blocks_a, pattern_a, blocks_b, [kern, ids, keep])
    densities, before, sums = [], [], []
    for half in range(2):
        sums.append(finish(half, after))
        after = sums[-1][0]
    for half in range(2):
        own, parts = sums[half]
        density, points = collocate(half, keep, ids, own, parts, basis_cols, by_point, before)
        densities.append(density)
        before = [points]
    points = lax.all_to_all(points, "col", split_axis=0, concat_axis=0, tiled=True)
    pieces = scatter_rows(sum_bricks(points))
    filtered = filter_rows(pieces, kern)
    potential = lax.all_to_all(filtered, "col", split_axis=0, concat_axis=0, tiled=True)
    density = jnp.transpose(jnp.concatenate(densities, axis=0), (1, 0, 2))
    return density[:, None], potential.reshape(128, 128)


def solution(mesh):
    return jax.shard_map(
        shards,
        mesh=mesh,
        in_specs=(
            P("row", "col", None, None),
            P("row", "col"),
            P("col", None, None, None),
            P("row", "col"),
            P("row", "col"),
            P("row", None, None),
            P("col", None, None),
            P(("row", "col"), None),
        ),
        out_specs=(P("row", "col", None, None), P("row", "col")),
        check_vma=False,
    )
```

```python
import functools
import math

import jax
import jax.numpy as jnp
import numpy as np
from jax import lax
from jax.experimental import pallas as pl
from jax.experimental.pallas import tpu as pltpu
from jax.sharding import PartitionSpec as P

BS = 138
MIB = 1 << 20
HIGH = lax.Precision.HIGHEST
F32 = jnp.float32
BF16 = jnp.bfloat16
I16 = jnp.int16
WIDE = 2304
SPAN = 1152
ROWS = (560, 544)
CUT = (0, 560)
TOP = 288
FOLD = 80
POINTS = 2048


def in_hbm(array):
    return pltpu.with_memory_space_constraint(array, pltpu.HBM)


def widen(tail):
    return jnp.concatenate([tail.astype(F32), jnp.zeros(tail.shape[:-1] + (128 - tail.shape[-1],), F32)], axis=-1)


def place_tails(tails, out, rows):
    lane = lax.broadcasted_iota(jnp.int32, (16, 128), 1) // 16
    for half in range(2):
        rest = jnp.zeros((16, 128), F32)
        for n in range(8):
            tail = tails[half * 8 + n]
            rest = jnp.where(lane == n, pltpu.roll(tail, 16 * n, 1) if n else tail, rest)
        out(half, rest.astype(BF16))


def pack_left_kernel(pairs, mask, blocks, after, out):
    def step(p, carry):
        pair = jnp.transpose(blocks[:, pl.ds(2 * p, 2)], (1, 0, 2, 3)).reshape(16, 16, BS)
        wide = jnp.swapaxes(pair, 0, 1)
        rows = pl.ds(pl.multiple_of(16 * p, 16), 16)
        tails = []
        for k in range(16):
            at = SPAN * (k // 8) + 128 * (k % 8)
            out[rows, at : at + 128] = wide[k, :, :128] * mask[k]
            tails.append(widen(wide[k, :, 128:] * mask[k, :, : BS - 128]))

        def put(half, value):
            out[rows, SPAN * half + 1024 : SPAN * half + 1152] = value

        place_tails(tails, put, rows)
        return carry

    lax.fori_loop(0, pairs, step, 0)


def pack_left(half, mask, blocks, after):
    count = (14, 34)[half]
    return pl.pallas_call(
        functools.partial(pack_left_kernel, count // 2),
        grid=(ROWS[half] // 8 // count,),
        in_specs=[
            pl.BlockSpec((16, 16, 128), lambda g: (0, 0, 0)),
            pl.BlockSpec(
                (pl.Element(8), pl.Element(count), pl.Element(16), pl.Element(BS)),
                lambda g: (0, CUT[half] // 8 + count * g, 0, 0),
            ),
            pl.BlockSpec(memory_space=pl.ANY),
        ],
        out_specs=pl.BlockSpec((count * 8, WIDE), lambda g: (g, 0)),
        out_shape=pltpu.VMEM((ROWS[half], WIDE), BF16),
        compiler_params=pltpu.CompilerParams(vmem_limit_bytes=32 * MIB),
        cost_estimate=pl.CostEstimate(flops=1000, bytes_accessed=1000, transcendentals=0),
        name="pack_left",
    )(mask, in_hbm(blocks), after)


def pack_right_kernel(blocks, *others):
    near, rest = others[-2:]
    base = pl.program_id(0) % 4 * 2

    def step(n, carry):
        k = base + n
        for c in range(0, 144, 16):
            if c < 128:
                rows = pl.ds(pl.multiple_of(128 * k + c, 16), 16)
                square = blocks[n, c : c + 16]
            else:
                rows = pl.ds(pl.multiple_of(1024 + 16 * k, 16), 16)
                square = jnp.concatenate([blocks[n, 128:BS], jnp.zeros((144 - BS, 16, BS), BF16)], axis=0)
            turned = jnp.swapaxes(square, 0, 1)
            near[:, rows, :] = turned[:, :, :128]

            def put(half, value, rows=rows):
                rest[rows, 128 * half : 128 * half + 128] = value

            place_tails([widen(turned[j, :, 128:]) for j in range(16)], put, rows)
        return carry

    lax.fori_loop(0, 2, step, 0)


def pack_right(blocks, before):
    return pl.pallas_call(
        pack_right_kernel,
        grid=(8,),
        in_specs=[pl.BlockSpec((2, BS, 16, BS), lambda g: (g, 0, 0, 0))]
        + [pl.BlockSpec(memory_space=pl.ANY)] * len(before),
        out_specs=[
            pl.BlockSpec((16, SPAN, 128), lambda g: (0, g // 4, 0)),
            pl.BlockSpec((SPAN, 256), lambda g: (g // 4, 0)),
        ],
        out_shape=[
            pltpu.VMEM((16, WIDE, 128), BF16),
            pltpu.VMEM((WIDE, 256), BF16),
        ],
        compiler_params=pltpu.CompilerParams(vmem_limit_bytes=24 * MIB),
        cost_estimate=pl.CostEstimate(flops=1000, bytes_accessed=1000, transcendentals=0),
        name="pack_right",
    )(in_hbm(blocks), *before)


def tails_kernel(half, left, rest, swap, after, out):
    right = rest[...]
    if half == 1:
        right = jnp.dot(right, swap[...], preferred_element_type=F32).astype(BF16)
    out[...] = jnp.dot(left[...], right, preferred_element_type=F32)


def product_tails(half, left, rest, after):
    lane = np.arange(256)
    swap = np.zeros((256, 256), np.float32)
    swap[lane, lane // 16 % 4 * 64 + lane // 64 * 16 + lane % 16] = 1.0
    vmem = pl.BlockSpec(memory_space=pltpu.VMEM)
    return pl.pallas_call(
        functools.partial(tails_kernel, half),
        in_specs=[vmem] * 3 + [pl.BlockSpec(memory_space=pl.ANY)],
        out_specs=vmem,
        out_shape=jax.ShapeDtypeStruct((ROWS[half], 256), F32),
        compiler_params=pltpu.CompilerParams(vmem_limit_bytes=12 * MIB),
        cost_estimate=pl.CostEstimate(flops=1000, bytes_accessed=1000, transcendentals=0),
        name="product_tails",
    )(left, rest, jnp.asarray(swap, BF16), after)


def lanes(rows):
    return lax.broadcasted_iota(jnp.int32, (rows, 128), 1)


def scale_of(most):
    power = jnp.floor(jnp.log2(jnp.maximum(jnp.full((1, 128), most, F32), 1e-30))) + 1.0
    return power, 32000.0 * jnp.exp2(-power)


def gain_of(coded):
    power = jnp.max(jnp.where(lanes(16) % 16 == 15, coded[0:16], -1000.0))
    return jnp.exp2(jnp.full((1, 128), power, F32)) * (1.0 / 32000.0)


def code(value, gain):
    return jnp.round(value * gain).astype(jnp.int32).astype(I16)


def code_tail(value, gain, power):
    coded = jnp.where(lanes(value.shape[0]) % 16 == 15, jnp.broadcast_to(power, value.shape), jnp.round(value * gain))
    return coded.astype(jnp.int32).astype(I16)


def plain(value):
    return value.astype(jnp.int32).astype(F32)


def product_kernel(half, d, spot, left, near, tails, after, out, held):
    rows = ROWS[half]
    coded = d != 0
    group = (spot[half] + d) % 4
    which = [4 * group + n if half == 0 else 4 * n + group for n in range(4)]
    for pair in range(2):
        both = jnp.dot(
            left[...],
            jnp.concatenate([near[which[2 * pair]], near[which[2 * pair + 1]]], axis=1),
            preferred_element_type=F32,
        )
        if coded:
            held[2 * pair] = both[:, :128]
            held[2 * pair + 1] = both[:, 128:]
        else:
            out[2 * pair * rows : (2 * pair + 1) * rows, :] = both[:, :128]
            out[(2 * pair + 1) * rows : (2 * pair + 2) * rows, :] = both[:, 128:]
    tail = jnp.where(group >= 2, tails[:, 128:], tails[:, :128])
    high, low = tail[:TOP], jnp.concatenate([tail[TOP:], jnp.zeros((2 * TOP - rows, 128), F32)], axis=0)
    odd = group % 2 == 1
    folded = jnp.where(
        lanes(TOP) < 64,
        jnp.where(odd, pltpu.roll(high, 64, 1), high),
        jnp.where(odd, low, pltpu.roll(low, 64, 1)),
    )
    if coded:
        power, gain = scale_of(jnp.maximum(jnp.max(jnp.abs(held[...])), jnp.max(jnp.abs(folded))))
        for n in range(4):
            out[n * rows : (n + 1) * rows, :] = code(held[n], gain)
        out[4 * rows : 4 * rows + TOP, :] = code_tail(folded, gain, power)
    else:
        out[4 * rows : 4 * rows + TOP, :] = folded


def product_group(half, d, spot, left, near, tails, after):
    rows = ROWS[half]
    coded = d != 0
    vmem = pl.BlockSpec(memory_space=pltpu.VMEM)
    return pl.pallas_call(
        functools.partial(product_kernel, half, d),
        in_specs=[pl.BlockSpec(memory_space=pltpu.SMEM)] + [vmem] * 3 + [pl.BlockSpec(memory_space=pl.ANY)],
        out_specs=vmem,
        out_shape=jax.ShapeDtypeStruct((4 * rows + TOP, 128), I16 if coded else F32),
        scratch_shapes=[pltpu.VMEM((4, rows, 128), F32)],
        compiler_params=pltpu.CompilerParams(vmem_limit_bytes=10 * MIB),
        cost_estimate=pl.CostEstimate(flops=1000, bytes_accessed=1000, transcendentals=0),
        name="product_coded" if coded else "product_own",
    )(spot, left, near, tails, after)


def merge_kernel(half, place, own, in1, in2, in3, after, mine, out1, out2, out3, held):
    rows = ROWS[half]
    parts = (in1, in2, in3)
    tails = [plain(p[4 * rows : 4 * rows + TOP, :]) for p in parts]
    gains = [gain_of(t) for t in tails]
    for n in range(4):
        here = slice(n * rows, (n + 1) * rows)
        total = own[here, :]
        for p, g in zip(parts, gains):
            total = total + plain(p[here, :]) * g
        held[n] = total
    folded = own[4 * rows : 4 * rows + TOP, :]
    for t, g in zip(tails, gains):
        folded = folded + t * g
    last = jnp.concatenate([folded[3 * FOLD :], jnp.zeros((4 * FOLD - TOP, 128), F32)], axis=0)
    pieces = [folded[0:FOLD], folded[FOLD : 2 * FOLD], folded[2 * FOLD : 3 * FOLD], last]
    slot = lanes(FOLD) // 16 % 4
    for s in range(4):

        @pl.when(place[1 - half] == s)
        def _(s=s):
            for d, out in enumerate((mine, out1, out2, out3)):
                here = (s + d) % 4
                tail = jnp.zeros((FOLD, 128), F32)
                for q in range(4):
                    tail = jnp.where(slot == q, pltpu.roll(pieces[q], 16 * ((q - here) % 8), 1) if (q - here) % 8 else pieces[q], tail)
                main = held[here]
                if d == 0:
                    out[0:rows, :] = main
                    out[rows : rows + FOLD, :] = tail
                else:
                    tail = jnp.where(lanes(FOLD) % 16 < 10, tail, 0.0)
                    power, gain = scale_of(jnp.maximum(jnp.max(jnp.abs(main)), jnp.max(jnp.abs(tail))))
                    out[0:rows, :] = code(main, gain)
                    out[rows : rows + FOLD, :] = code_tail(tail, gain, power)


def merge(half, place, own, parts, after):
    vmem = pl.BlockSpec(memory_space=pltpu.VMEM)
    return pl.pallas_call(
        functools.partial(merge_kernel, half),
        in_specs=[pl.BlockSpec(memory_space=pltpu.SMEM)] + [vmem] * 4 + [pl.BlockSpec(memory_space=pl.ANY)],
        out_specs=[vmem] * 4,
        out_shape=[jax.ShapeDtypeStruct((ROWS[half] + FOLD, 128), t) for t in (F32, I16, I16, I16)],
        scratch_shapes=[pltpu.VMEM((4, ROWS[half], 128), F32)],
        compiler_params=pltpu.CompilerParams(vmem_limit_bytes=8 * MIB),
        cost_estimate=pl.CostEstimate(flops=1000, bytes_accessed=1000, transcendentals=0),
        name="merge",
    )(place, own, *parts, after)


def turn(dy, dz):
    return [(4 * y + z, (y + dy) % 4 * 4 + (z + dz) % 4) for y in range(4) for z in range(4)]


def send(array, axis, d):
    return lax.ppermute(array, "col", turn(d, 0) if axis == 0 else turn(0, d))


def exchange_products(blocks_a, pattern, blocks_b, before):
    place = lax.axis_index("col").astype(jnp.int32)
    spot = jnp.stack([place // 4, place % 4])
    mask = jnp.broadcast_to(jnp.tile(pattern.T, (1, 2))[:, :, None], (16, 16, 128)).astype(BF16)
    blocks_a = jnp.transpose(blocks_a, (0, 2, 1, 3))
    near, rest = pack_right(jnp.transpose(blocks_b, (0, 2, 1, 3)), [mask, spot] + before)
    after = near
    parts, owns = ([], []), []
    lefts = []
    for half in range(2):
        left = pack_left(half, mask, blocks_a, after)
        tails = product_tails(half, left, rest, after)
        lefts.append((left, near, tails))
        after = tails
        for d in (1, 2, 3):
            last = product_group(half, d, spot, *lefts[half], after)
            parts[half].append(send(last, half, d))
        after = last
    for half in range(2):
        after = product_group(half, 0, spot, *lefts[half], after)
        owns.append(after)

    def finish(half, after):
        mine, *outs = merge(half, spot, owns[half], parts[half], after)
        return mine, [send(outs[d - 1], 1 - half, d) for d in (2, 1, 3)]

    return finish, after


def collocate_kernel(half, keep, ids, own, in1, in2, in3, cols, rows, *rest):
    if half == 0:
        density, out, stacked, right, held, held_cols, sems = rest
        before = None
    else:
        before, density, out, stacked, right, held, held_cols, sems = rest
    count = ROWS[half]
    tiles = 16384 // POINTS

    def copies(g):
        spot = pl.ds(pl.multiple_of(g * POINTS, POINTS), POINTS)
        return (
            pltpu.make_async_copy(cols.at[0, :, spot], held_cols.at[g], sems.at[0, g]),
            pltpu.make_async_copy(
                rows.at[pl.ds(CUT[half] // 8, count // 8), :, spot], held.at[g], sems.at[1, g]
            ),
        )

    for g in range(tiles):
        for copy in copies(g):
            copy.start()

    def decode_density():
        main, fold = own[0:count, :], own[count : count + FOLD, :]
        for part in (in1, in2, in3):
            extra = plain(part[count : count + FOLD, :])
            gain = gain_of(extra)
            main, fold = main + plain(part[0:count, :]) * gain, fold + extra * gain
        tails = []
        for base, total in ((0, TOP), (4, count - TOP)):
            for q in range(4):
                piece = fold[0 : min(FOLD, total - q * FOLD)]
                shift = (128 - 16 * (q + base)) % 128
                tails.append(pltpu.roll(piece, shift, 1) if shift else piece)
        tail = jnp.where(lanes(count) < BS - 128, jnp.concatenate(tails, axis=0), 0.0)
        kept = keep[...][None]
        main = (main.reshape(count // 8, 8, 128) * kept).reshape(count, 128).astype(BF16)
        tail = (tail.reshape(count // 8, 8, 128) * kept).reshape(count, 128).astype(BF16)
        stacked[:, 0:128] = main
        stacked[:, 128:256] = tail
        density[:, :, 0:128] = main.reshape(count // 8, 8, 128)
        density[:, :, 128:BS] = tail.reshape(count // 8, 8, 128)[:, :, : BS - 128]
        right[128:256, :] = jnp.zeros((128, POINTS), BF16)

    decode_density()

    def step(g, carry):
        for copy in copies(g):
            copy.wait()
        right[0:BS, :] = held_cols[g]
        tile(g)
        return carry

    def tile(g):
        per = POINTS // 1024
        for t in range(POINTS // 256):
            here = slice(t * 256, (t + 1) * 256)
            inner = jnp.dot(stacked[...], right[:, here], preferred_element_type=F32).reshape(count // 8, 8, 256)
            total = jnp.sum(inner * held[g, :, :, here].astype(F32), axis=0)
            within = slice(t % 4 * 256, t % 4 * 256 + 256)
            if half == 1:
                total = total + before[per * g + t // 4, :, within]
            out[per * g + t // 4, :, within] = total
        if half == 1:
            for n in range(POINTS // 1024):
                out[per * g + n, :, 1024:1152] = ids[...]

    lax.fori_loop(0, tiles, step, 0)


def collocate(half, keep, ids, own, parts, basis_cols, basis_rows, before):
    count = ROWS[half]
    wide = 1152 if half else 1024
    vmem = pl.BlockSpec(memory_space=pltpu.VMEM)
    tiles = 16384 // POINTS
    return pl.pallas_call(
        functools.partial(collocate_kernel, half),
        in_specs=[vmem] * 6 + [pl.BlockSpec(memory_space=pltpu.HBM)] * 2 + [vmem] * half,
        out_specs=[vmem] * 2,
        scratch_shapes=[
            pltpu.VMEM((count, 256), BF16),
            pltpu.VMEM((256, POINTS), BF16),
            pltpu.VMEM((tiles, count // 8, 8, POINTS), BF16),
            pltpu.VMEM((tiles, BS, POINTS), BF16),
            pltpu.SemaphoreType.DMA((2, tiles)),
        ],
        out_shape=[
            jax.ShapeDtypeStruct((count // 8, 8, BS), BF16),
            jax.ShapeDtypeStruct((16, 8, wide), F32),
        ],
        compiler_params=pltpu.CompilerParams(vmem_limit_bytes=32 * MIB),
        cost_estimate=pl.CostEstimate(flops=1000, bytes_accessed=1000, transcendentals=0),
        name="collocate",
    )(keep, ids, own, *parts, in_hbm(basis_cols), in_hbm(basis_rows), *before)


def bricks_kernel(points, out):
    owners = jnp.sum(points[:, :, 1024:1152].reshape(128, 128), axis=0, keepdims=True).astype(jnp.int32)
    onehot = (owners == lax.broadcasted_iota(jnp.int32, (128, 128), 0)).astype(F32)
    held = points[:, :, 0:1024].reshape(128, 1024)
    out[...] = jnp.dot(onehot, held, precision=HIGH, preferred_element_type=F32)


def sum_bricks(points):
    return pl.pallas_call(
        bricks_kernel,
        out_shape=jax.ShapeDtypeStruct((128, 1024), F32),
        compiler_params=pltpu.CompilerParams(vmem_limit_bytes=8 * MIB),
        cost_estimate=pl.CostEstimate(flops=1000, bytes_accessed=1000, transcendentals=0),
        name="sum_bricks",
    )(points)


def tables():
    a = np.arange(16)
    outer = 2.0 * math.pi * (np.outer(a, a) % 16) / 16
    eye = np.eye(8)
    ck, sk = np.kron(eye, np.cos(outer)), np.kron(eye, np.sin(outer))
    b = np.arange(128)
    inner = 2.0 * math.pi * (np.outer(b, b) % 128) / 128
    c, s = np.cos(inner), np.sin(inner)
    twist = 2.0 * math.pi * np.outer(np.tile(a, 8), b) / 2048
    first = np.concatenate([ck, -sk], 0)
    second = np.block([[c, -s], [s, c]])
    third = np.block([[c, s], [-s, c]])
    last = np.concatenate([ck, -sk], 1) / 2048
    return [np.asarray(t, np.float32) for t in (first, second, third, last, np.cos(twist), np.sin(twist))]


def filter_kernel(own, in1, in2, in3, kern, first, second, third, last, tc, ts, out):
    def dot(p, q):
        return jnp.dot(p, q, precision=HIGH, preferred_element_type=F32)

    grid = (own[...] + in1[...]) + (in2[...] + in3[...])
    grid = jnp.concatenate([grid[:, y * 128 : y * 128 + 128] for y in range(8)], axis=0)
    section = dot(first[...], grid)
    re, im = section[:128], section[128:]
    c, s = tc[...], ts[...]
    spec = dot(jnp.concatenate([re * c + im * s, im * c - re * s], axis=1), second[...])
    k = kern[...]
    back = dot(spec * jnp.concatenate([k, k], axis=1), third[...])
    re, im = back[:, :128], back[:, 128:]
    turned = jnp.concatenate([re * c - im * s, im * c + re * s], axis=0)
    result = dot(last[...], turned)
    for y in range(8):
        out[:, y, :] = result[y * 16 : y * 16 + 16]


def filter_rows(pieces, kern):
    return pl.pallas_call(
        filter_kernel,
        out_shape=jax.ShapeDtypeStruct((16, 8, 128), F32),
        compiler_params=pltpu.CompilerParams(vmem_limit_bytes=8 * MIB),
        cost_estimate=pl.CostEstimate(flops=1000, bytes_accessed=1000, transcendentals=0),
        name="filter_rows",
    )(*pieces, kern, *tables())


def scatter_rows(partial):
    place = lax.axis_index("row")
    x, core = place // 2, place % 2
    halves = partial.reshape(4, 2, 16, 1024)
    away = lax.dynamic_index_in_dim(halves, 1 - core, 1, keepdims=False)
    mine = lax.dynamic_index_in_dim(halves, core, 1, keepdims=False)
    mine = mine + lax.ppermute(away, "row", [(r, r ^ 1) for r in range(8)])
    pieces = [lax.dynamic_index_in_dim(mine, x, 0, keepdims=False)]
    for d in (1, 2, 3):
        part = lax.dynamic_index_in_dim(mine, (x + d) % 4, 0, keepdims=False)
        pieces.append(lax.ppermute(part, "row", [(r, (r + 2 * d) % 8) for r in range(8)]))
    return pieces


def shards(blocks_a, pattern_a, blocks_b, filter_mask, task_brick, basis_rows, basis_cols, kernel):
    kern = jnp.transpose(kernel.reshape(8, 128, 16), (0, 2, 1)).reshape(128, 128)
    lane = jnp.arange(128, dtype=jnp.int32)
    owners = jnp.where(lane // 8 == lax.axis_index("col"), jnp.tile(task_brick.reshape(8), 16), 0)
    ids = jnp.concatenate([owners.astype(F32)[None], jnp.zeros((7, 128), F32)], axis=0)
    keep = jnp.broadcast_to(filter_mask.reshape(8, 1).astype(F32), (8, 128))
    by_point = jnp.transpose(basis_rows, (1, 0, 2))
    finish, after = exchange_products(blocks_a, pattern_a, blocks_b, [kern, ids, keep])
    densities, before = [], []
    for half in range(2):
        own, parts = finish(half, after)
        density, after = collocate(half, keep, ids, own, parts, basis_cols, by_point, before)
        densities.append(density)
        before = [after]
    points = after
    points = lax.all_to_all(points, "col", split_axis=0, concat_axis=0, tiled=True)
    pieces = scatter_rows(sum_bricks(points))
    filtered = filter_rows(pieces, kern)
    potential = lax.all_to_all(filtered, "col", split_axis=0, concat_axis=0, tiled=True)
    density = jnp.transpose(jnp.concatenate(densities, axis=0), (1, 0, 2))
    return density[:, None], potential.reshape(128, 128)


def solution(mesh):
    return jax.shard_map(
        shards,
        mesh=mesh,
        in_specs=(
            P("row", "col", None, None),
            P("row", "col"),
            P("col", None, None, None),
            P("row", "col"),
            P("row", "col"),
            P("row", None, None),
            P("col", None, None),
            P(("row", "col"), None),
        ),
        out_specs=(P("row", "col", None, None), P("row", "col")),
        check_vma=False,
    )
```

```python
import functools
import math

import jax
import jax.numpy as jnp
import numpy as np
from jax import lax
from jax.experimental import pallas as pl
from jax.experimental.pallas import tpu as pltpu
from jax.sharding import PartitionSpec as P

BS = 138
MIB = 1 << 20
HIGH = lax.Precision.HIGHEST
F32 = jnp.float32
BF16 = jnp.bfloat16
I16 = jnp.int16
WIDE = 2304
SPAN = 1152
ROWS = (720, 384)
CUT = (0, 720)
TOP = (368, 192)
FOLD = (96, 48)
STEP = (18, 24)
POINTS = 2048


def in_hbm(array):
    return pltpu.with_memory_space_constraint(array, pltpu.HBM)


def widen(tail):
    return jnp.concatenate([tail.astype(F32), jnp.zeros(tail.shape[:-1] + (128 - tail.shape[-1],), F32)], axis=-1)


def place_tails(tails, out, rows):
    lane = lax.broadcasted_iota(jnp.int32, (16, 128), 1) // 16
    for half in range(2):
        rest = jnp.zeros((16, 128), F32)
        for n in range(8):
            tail = tails[half * 8 + n]
            rest = jnp.where(lane == n, pltpu.roll(tail, 16 * n, 1) if n else tail, rest)
        out(half, rest.astype(BF16))


def pack_left_kernel(pairs, mask, blocks, after, out):
    def step(p, carry):
        pair = jnp.transpose(blocks[:, pl.ds(2 * p, 2)], (1, 0, 2, 3)).reshape(16, 16, BS)
        wide = jnp.swapaxes(pair, 0, 1)
        rows = pl.ds(pl.multiple_of(16 * p, 16), 16)
        tails = []
        for k in range(16):
            at = SPAN * (k // 8) + 128 * (k % 8)
            out[rows, at : at + 128] = wide[k, :, :128] * mask[k]
            tails.append(widen(wide[k, :, 128:] * mask[k, :, : BS - 128]))

        def put(half, value):
            out[rows, SPAN * half + 1024 : SPAN * half + 1152] = value

        place_tails(tails, put, rows)
        return carry

    lax.fori_loop(0, pairs, step, 0)


def pack_left(half, mask, blocks, after):
    count = STEP[half]
    return pl.pallas_call(
        functools.partial(pack_left_kernel, count // 2),
        grid=(ROWS[half] // 8 // count,),
        in_specs=[
            pl.BlockSpec((16, 16, 128), lambda g: (0, 0, 0)),
            pl.BlockSpec(
                (pl.Element(8), pl.Element(count), pl.Element(16), pl.Element(BS)),
                lambda g: (0, CUT[half] // 8 + count * g, 0, 0),
            ),
            pl.BlockSpec(memory_space=pl.ANY),
        ],
        out_specs=pl.BlockSpec((count * 8, WIDE), lambda g: (g, 0)),
        out_shape=pltpu.VMEM((ROWS[half], WIDE), BF16),
        compiler_params=pltpu.CompilerParams(vmem_limit_bytes=32 * MIB),
        cost_estimate=pl.CostEstimate(flops=1000, bytes_accessed=1000, transcendentals=0),
        name="pack_left",
    )(mask, in_hbm(blocks), after)


def pack_right_kernel(blocks, *others):
    near, rest = others[-2:]
    base = pl.program_id(0) % 4 * 2

    def step(n, carry):
        k = base + n
        for c in range(0, 144, 16):
            if c < 128:
                rows = pl.ds(pl.multiple_of(128 * k + c, 16), 16)
                square = blocks[n, c : c + 16]
            else:
                rows = pl.ds(pl.multiple_of(1024 + 16 * k, 16), 16)
                square = jnp.concatenate([blocks[n, 128:BS], jnp.zeros((144 - BS, 16, BS), BF16)], axis=0)
            turned = jnp.swapaxes(square, 0, 1)
            near[:, rows, :] = turned[:, :, :128]

            def put(half, value, rows=rows):
                rest[rows, 128 * half : 128 * half + 128] = value

            place_tails([widen(turned[j, :, 128:]) for j in range(16)], put, rows)
        return carry

    lax.fori_loop(0, 2, step, 0)


def pack_right(blocks, before):
    return pl.pallas_call(
        pack_right_kernel,
        grid=(8,),
        in_specs=[pl.BlockSpec((2, BS, 16, BS), lambda g: (g, 0, 0, 0))]
        + [pl.BlockSpec(memory_space=pl.ANY)] * len(before),
        out_specs=[
            pl.BlockSpec((16, SPAN, 128), lambda g: (0, g // 4, 0)),
            pl.BlockSpec((SPAN, 256), lambda g: (g // 4, 0)),
        ],
        out_shape=[
            pltpu.VMEM((16, WIDE, 128), BF16),
            pltpu.VMEM((WIDE, 256), BF16),
        ],
        compiler_params=pltpu.CompilerParams(vmem_limit_bytes=24 * MIB),
        cost_estimate=pl.CostEstimate(flops=1000, bytes_accessed=1000, transcendentals=0),
        name="pack_right",
    )(in_hbm(blocks), *before)


def tails_kernel(half, left, rest, swap, after, out):
    right = rest[...]
    if half == 1:
        right = jnp.dot(right, swap[...], preferred_element_type=F32).astype(BF16)
    out[...] = jnp.dot(left[...], right, preferred_element_type=F32)


def product_tails(half, left, rest, after):
    lane = np.arange(256)
    swap = np.zeros((256, 256), np.float32)
    swap[lane, lane // 16 % 4 * 64 + lane // 64 * 16 + lane % 16] = 1.0
    vmem = pl.BlockSpec(memory_space=pltpu.VMEM)
    return pl.pallas_call(
        functools.partial(tails_kernel, half),
        in_specs=[vmem] * 3 + [pl.BlockSpec(memory_space=pl.ANY)],
        out_specs=vmem,
        out_shape=jax.ShapeDtypeStruct((ROWS[half], 256), F32),
        compiler_params=pltpu.CompilerParams(vmem_limit_bytes=12 * MIB),
        cost_estimate=pl.CostEstimate(flops=1000, bytes_accessed=1000, transcendentals=0),
        name="product_tails",
    )(left, rest, jnp.asarray(swap, BF16), after)


def padded(value, rows):
    if value.shape[0] == rows:
        return value
    return jnp.concatenate([value, jnp.zeros((rows - value.shape[0], 128), F32)], axis=0)


def lanes(rows):
    return lax.broadcasted_iota(jnp.int32, (rows, 128), 1)


def scale_of(most):
    power = jnp.floor(jnp.log2(jnp.maximum(jnp.full((1, 128), most, F32), 1e-30))) + 1.0
    return power, 32000.0 * jnp.exp2(-power)


def gain_of(coded):
    power = jnp.max(jnp.where(lanes(16) % 16 == 15, coded[0:16], -1000.0))
    return jnp.exp2(jnp.full((1, 128), power, F32)) * (1.0 / 32000.0)


def code(value, gain):
    return jnp.round(value * gain).astype(jnp.int32).astype(I16)


def code_tail(value, gain, power):
    coded = jnp.where(lanes(value.shape[0]) % 16 == 15, jnp.broadcast_to(power, value.shape), jnp.round(value * gain))
    return coded.astype(jnp.int32).astype(I16)


def plain(value):
    return value.astype(jnp.int32).astype(F32)


def product_kernel(half, d, spot, left, near, tails, after, out, held):
    rows = ROWS[half]
    coded = d != 0
    group = (spot[half] + d) % 4
    which = [4 * group + n if half == 0 else 4 * n + group for n in range(4)]
    for pair in range(2):
        both = jnp.dot(
            left[...],
            jnp.concatenate([near[which[2 * pair]], near[which[2 * pair + 1]]], axis=1),
            preferred_element_type=F32,
        )
        if coded:
            held[2 * pair] = both[:, :128]
            held[2 * pair + 1] = both[:, 128:]
        else:
            out[2 * pair * rows : (2 * pair + 1) * rows, :] = both[:, :128]
            out[(2 * pair + 1) * rows : (2 * pair + 2) * rows, :] = both[:, 128:]
    tail = jnp.where(group >= 2, tails[:, 128:], tails[:, :128])
    top = TOP[half]
    high, low = tail[:top], padded(tail[top:], top)
    odd = group % 2 == 1
    folded = jnp.where(
        lanes(top) < 64,
        jnp.where(odd, pltpu.roll(high, 64, 1), high),
        jnp.where(odd, low, pltpu.roll(low, 64, 1)),
    )
    if coded:
        power, gain = scale_of(jnp.maximum(jnp.max(jnp.abs(held[...])), jnp.max(jnp.abs(folded))))
        for n in range(4):
            out[n * rows : (n + 1) * rows, :] = code(held[n], gain)
        out[4 * rows : 4 * rows + TOP[half], :] = code_tail(folded, gain, power)
    else:
        out[4 * rows : 4 * rows + TOP[half], :] = folded


def product_group(half, d, spot, left, near, tails, after):
    rows = ROWS[half]
    coded = d != 0
    vmem = pl.BlockSpec(memory_space=pltpu.VMEM)
    return pl.pallas_call(
        functools.partial(product_kernel, half, d),
        in_specs=[pl.BlockSpec(memory_space=pltpu.SMEM)] + [vmem] * 3 + [pl.BlockSpec(memory_space=pl.ANY)],
        out_specs=vmem,
        out_shape=jax.ShapeDtypeStruct((4 * rows + TOP[half], 128), I16 if coded else F32),
        scratch_shapes=[pltpu.VMEM((4, rows, 128), F32)],
        compiler_params=pltpu.CompilerParams(vmem_limit_bytes=10 * MIB),
        cost_estimate=pl.CostEstimate(flops=1000, bytes_accessed=1000, transcendentals=0),
        name="product_coded" if coded else "product_own",
    )(spot, left, near, tails, after)


def merge_kernel(half, spot, own, in1, in2, in3, after, mine, out, held):
    rows, top, size = ROWS[half], TOP[half], FOLD[half]
    parts = (in1, in2, in3)
    tails = [plain(p[4 * rows : 4 * rows + top, :]) for p in parts]
    gains = [gain_of(t) for t in tails]
    for n in range(4):
        here = slice(n * rows, (n + 1) * rows)
        total = own[here, :]
        for p, g in zip(parts, gains):
            total = total + plain(p[here, :]) * g
        held[n] = total
    folded = own[4 * rows : 4 * rows + top, :]
    for t, g in zip(tails, gains):
        folded = folded + t * g
    pieces = [padded(folded[q * size : min(top, (q + 1) * size)], size) for q in range(4)]
    slot = lanes(size) // 16 % 4
    place = spot[1 - half]
    for n in range(4):
        tail = jnp.zeros((size, 128), F32)
        for q in range(4):
            turned = pltpu.roll(pieces[q], 16 * ((q - n) % 8), 1) if q != n else pieces[q]
            tail = jnp.where(slot == q, turned, tail)
        tail = jnp.where(lanes(size) % 16 < 10, tail, 0.0)
        main = held[n]

        @pl.when(place == n)
        def _(main=main, tail=tail, n=n):
            mine[0:rows, :] = main
            mine[rows : rows + size, :] = tail
            out[n] = jnp.zeros((rows + size, 128), I16)

        @pl.when(place != n)
        def _(main=main, tail=tail, n=n):
            power, gain = scale_of(jnp.maximum(jnp.max(jnp.abs(main)), jnp.max(jnp.abs(tail))))
            out[n, 0:rows, :] = code(main, gain)
            out[n, rows : rows + size, :] = code_tail(tail, gain, power)


def merge(half, spot, own, parts, after):
    vmem = pl.BlockSpec(memory_space=pltpu.VMEM)
    total = ROWS[half] + FOLD[half]
    return pl.pallas_call(
        functools.partial(merge_kernel, half),
        in_specs=[pl.BlockSpec(memory_space=pltpu.SMEM)] + [vmem] * 4 + [pl.BlockSpec(memory_space=pl.ANY)],
        out_specs=[vmem] * 2,
        out_shape=[jax.ShapeDtypeStruct((total, 128), F32), jax.ShapeDtypeStruct((4, total, 128), I16)],
        scratch_shapes=[pltpu.VMEM((4, ROWS[half], 128), F32)],
        compiler_params=pltpu.CompilerParams(vmem_limit_bytes=12 * MIB),
        cost_estimate=pl.CostEstimate(flops=1000, bytes_accessed=1000, transcendentals=0),
        name="merge",
    )(spot, own, *parts, after)


def turn(dy, dz):
    return [(4 * y + z, (y + dy) % 4 * 4 + (z + dz) % 4) for y in range(4) for z in range(4)]


def send(array, axis, d):
    return lax.ppermute(array, "col", turn(d, 0) if axis == 0 else turn(0, d))


def exchange_products(blocks_a, pattern, blocks_b, before):
    place = lax.axis_index("col").astype(jnp.int32)
    spot = jnp.stack([place // 4, place % 4])
    mask = jnp.broadcast_to(jnp.tile(pattern.T, (1, 2))[:, :, None], (16, 16, 128)).astype(BF16)
    blocks_a = jnp.transpose(blocks_a, (0, 2, 1, 3))
    near, rest = pack_right(jnp.transpose(blocks_b, (0, 2, 1, 3)), [mask, spot] + before)
    after = near
    parts, owns = ([], []), []
    lefts = []
    for half in range(2):
        left = pack_left(half, mask, blocks_a, after)
        tails = product_tails(half, left, rest, after)
        lefts.append((left, near, tails))
        after = tails
        for d in (1, 2, 3):
            last = product_group(half, d, spot, *lefts[half], after)
            parts[half].append(send(last, half, d))
        after = last
    for half in range(2):
        after = product_group(half, 0, spot, *lefts[half], after)
        owns.append(after)

    def finish(half, after):
        mine, out = merge(half, spot, owns[half], parts[half], after)
        if half == 0:
            groups = [[4 * y + z for z in range(4)] for y in range(4)]
        else:
            groups = [[4 * y + z for y in range(4)] for z in range(4)]
        given = lax.all_to_all(out, "col", split_axis=0, concat_axis=0, axis_index_groups=groups, tiled=True)
        return mine, given

    return finish, after


def collocate_kernel(half, keep, ids, own, parts, cols, rows, after, *rest):
    size = FOLD[half]
    if half == 0:
        density, out, stacked, right, held, held_cols, sems = rest
        before = None
    else:
        before, density, out, stacked, right, held, held_cols, sems = rest
    count = ROWS[half]
    tiles = 16384 // POINTS

    def copies(g):
        spot = pl.ds(pl.multiple_of(g * POINTS, POINTS), POINTS)
        return (
            pltpu.make_async_copy(cols.at[0, :, spot], held_cols.at[g], sems.at[0, g]),
            pltpu.make_async_copy(
                rows.at[pl.ds(CUT[half] // 8, count // 8), :, spot], held.at[g], sems.at[1, g]
            ),
        )

    for g in range(tiles):
        for copy in copies(g):
            copy.start()

    def decode_density():
        main, fold = own[0:count, :], own[count : count + size, :]
        for n in range(4):
            extra = plain(parts[n, count : count + size, :])
            gain = gain_of(extra)
            main, fold = main + plain(parts[n, 0:count, :]) * gain, fold + extra * gain
        tails = []
        for base, total in ((0, TOP[half]), (4, count - TOP[half])):
            for q in range(4):
                piece = fold[0 : min(size, total - q * size)]
                shift = (128 - 16 * (q + base)) % 128
                tails.append(pltpu.roll(piece, shift, 1) if shift else piece)
        tail = jnp.where(lanes(count) < BS - 128, jnp.concatenate(tails, axis=0), 0.0)
        kept = keep[...][None]
        main = (main.reshape(count // 8, 8, 128) * kept).reshape(count, 128).astype(BF16)
        tail = (tail.reshape(count // 8, 8, 128) * kept).reshape(count, 128).astype(BF16)
        stacked[:, 0:128] = main
        stacked[:, 128:256] = tail
        density[:, :, 0:128] = main.reshape(count // 8, 8, 128)
        density[:, :, 128:BS] = tail.reshape(count // 8, 8, 128)[:, :, : BS - 128]
        right[128:256, :] = jnp.zeros((128, POINTS), BF16)

    decode_density()

    def step(g, carry):
        for copy in copies(g):
            copy.wait()
        right[0:BS, :] = held_cols[g]
        tile(g)
        return carry

    def tile(g):
        per = POINTS // 1024
        for t in range(POINTS // 256):
            here = slice(t * 256, (t + 1) * 256)
            inner = jnp.dot(stacked[...], right[:, here], preferred_element_type=F32).reshape(count // 8, 8, 256)
            total = jnp.sum(inner * held[g, :, :, here].astype(F32), axis=0)
            within = slice(t % 4 * 256, t % 4 * 256 + 256)
            if half == 1:
                total = total + before[per * g + t // 4, :, within]
            out[per * g + t // 4, :, within] = total
        if half == 1:
            for n in range(POINTS // 1024):
                out[per * g + n, :, 1024:1152] = ids[...]

    lax.fori_loop(0, tiles, step, 0)


def collocate(half, keep, ids, own, parts, basis_cols, basis_rows, before, after):
    count = ROWS[half]
    wide = 1152 if half else 1024
    vmem = pl.BlockSpec(memory_space=pltpu.VMEM)
    tiles = 16384 // POINTS
    return pl.pallas_call(
        functools.partial(collocate_kernel, half),
        in_specs=[vmem] * 4
        + [pl.BlockSpec(memory_space=pltpu.HBM)] * 2
        + [pl.BlockSpec(memory_space=pl.ANY)]
        + [vmem] * half,
        out_specs=[vmem] * 2,
        scratch_shapes=[
            pltpu.VMEM((count, 256), BF16),
            pltpu.VMEM((256, POINTS), BF16),
            pltpu.VMEM((tiles, count // 8, 8, POINTS), BF16),
            pltpu.VMEM((tiles, BS, POINTS), BF16),
            pltpu.SemaphoreType.DMA((2, tiles)),
        ],
        out_shape=[
            jax.ShapeDtypeStruct((count // 8, 8, BS), BF16),
            jax.ShapeDtypeStruct((16, 8, wide), F32),
        ],
        compiler_params=pltpu.CompilerParams(vmem_limit_bytes=(40, 28)[half] * MIB),
        cost_estimate=pl.CostEstimate(flops=1000, bytes_accessed=1000, transcendentals=0),
        name="collocate",
    )(keep, ids, own, parts, in_hbm(basis_cols), in_hbm(basis_rows), after, *before)


def bricks_kernel(points, out):
    owners = jnp.sum(points[:, :, 1024:1152].reshape(128, 128), axis=0, keepdims=True).astype(jnp.int32)
    onehot = (owners == lax.broadcasted_iota(jnp.int32, (128, 128), 0)).astype(F32)
    held = points[:, :, 0:1024].reshape(128, 1024)
    out[...] = jnp.dot(onehot, held, precision=HIGH, preferred_element_type=F32)


def sum_bricks(points):
    return pl.pallas_call(
        bricks_kernel,
        out_shape=jax.ShapeDtypeStruct((128, 1024), F32),
        compiler_params=pltpu.CompilerParams(vmem_limit_bytes=8 * MIB),
        cost_estimate=pl.CostEstimate(flops=1000, bytes_accessed=1000, transcendentals=0),
        name="sum_bricks",
    )(points)


def tables():
    a = np.arange(16)
    outer = 2.0 * math.pi * (np.outer(a, a) % 16) / 16
    eye = np.eye(8)
    ck, sk = np.kron(eye, np.cos(outer)), np.kron(eye, np.sin(outer))
    b = np.arange(128)
    inner = 2.0 * math.pi * (np.outer(b, b) % 128) / 128
    c, s = np.cos(inner), np.sin(inner)
    twist = 2.0 * math.pi * np.outer(np.tile(a, 8), b) / 2048
    first = np.concatenate([ck, -sk], 0)
    second = np.block([[c, -s], [s, c]])
    third = np.block([[c, s], [-s, c]])
    last = np.concatenate([ck, -sk], 1) / 2048
    return [np.asarray(t, np.float32) for t in (first, second, third, last, np.cos(twist), np.sin(twist))]


def filter_kernel(own, in1, in2, in3, kern, first, second, third, last, tc, ts, out):
    def dot(p, q):
        return jnp.dot(p, q, precision=HIGH, preferred_element_type=F32)

    grid = (own[...] + in1[...]) + (in2[...] + in3[...])
    grid = jnp.concatenate([grid[:, y * 128 : y * 128 + 128] for y in range(8)], axis=0)
    section = dot(first[...], grid)
    re, im = section[:128], section[128:]
    c, s = tc[...], ts[...]
    spec = dot(jnp.concatenate([re * c + im * s, im * c - re * s], axis=1), second[...])
    k = kern[...]
    back = dot(spec * jnp.concatenate([k, k], axis=1), third[...])
    re, im = back[:, :128], back[:, 128:]
    turned = jnp.concatenate([re * c - im * s, im * c + re * s], axis=0)
    result = dot(last[...], turned)
    for y in range(8):
        out[:, y, :] = result[y * 16 : y * 16 + 16]


def filter_rows(pieces, kern):
    return pl.pallas_call(
        filter_kernel,
        out_shape=jax.ShapeDtypeStruct((16, 8, 128), F32),
        compiler_params=pltpu.CompilerParams(vmem_limit_bytes=8 * MIB),
        cost_estimate=pl.CostEstimate(flops=1000, bytes_accessed=1000, transcendentals=0),
        name="filter_rows",
    )(*pieces, kern, *tables())


def scatter_rows(partial):
    place = lax.axis_index("row")
    x, core = place // 2, place % 2
    halves = partial.reshape(4, 2, 16, 1024)
    away = lax.dynamic_index_in_dim(halves, 1 - core, 1, keepdims=False)
    mine = lax.dynamic_index_in_dim(halves, core, 1, keepdims=False)
    mine = mine + lax.ppermute(away, "row", [(r, r ^ 1) for r in range(8)])
    pieces = [lax.dynamic_index_in_dim(mine, x, 0, keepdims=False)]
    for d in (1, 2, 3):
        part = lax.dynamic_index_in_dim(mine, (x + d) % 4, 0, keepdims=False)
        pieces.append(lax.ppermute(part, "row", [(r, (r + 2 * d) % 8) for r in range(8)]))
    return pieces


def shards(blocks_a, pattern_a, blocks_b, filter_mask, task_brick, basis_rows, basis_cols, kernel):
    kern = jnp.transpose(kernel.reshape(8, 128, 16), (0, 2, 1)).reshape(128, 128)
    lane = jnp.arange(128, dtype=jnp.int32)
    owners = jnp.where(lane // 8 == lax.axis_index("col"), jnp.tile(task_brick.reshape(8), 16), 0)
    ids = jnp.concatenate([owners.astype(F32)[None], jnp.zeros((7, 128), F32)], axis=0)
    keep = jnp.broadcast_to(filter_mask.reshape(8, 1).astype(F32), (8, 128))
    by_point = jnp.transpose(basis_rows, (1, 0, 2))
    finish, after = exchange_products(blocks_a, pattern_a, blocks_b, [kern, ids, keep])
    densities, before, sums = [], [], []
    for half in range(2):
        sums.append(finish(half, after))
        after = sums[half][0]
    for half in range(2):
        own, parts = sums[half]
        density, after = collocate(half, keep, ids, own, parts, basis_cols, by_point, before, after)
        densities.append(density)
        before = [after]
    points = after
    points = lax.all_to_all(points, "col", split_axis=0, concat_axis=0, tiled=True)
    pieces = scatter_rows(sum_bricks(points))
    filtered = filter_rows(pieces, kern)
    potential = lax.all_to_all(filtered, "col", split_axis=0, concat_axis=0, tiled=True)
    density = jnp.transpose(jnp.concatenate(densities, axis=0), (1, 0, 2))
    return density[:, None], potential.reshape(128, 128)


def solution(mesh):
    return jax.shard_map(
        shards,
        mesh=mesh,
        in_specs=(
            P("row", "col", None, None),
            P("row", "col"),
            P("col", None, None, None),
            P("row", "col"),
            P("row", "col"),
            P("row", None, None),
            P("col", None, None),
            P(("row", "col"), None),
        ),
        out_specs=(P("row", "col", None, None), P("row", "col")),
        check_vma=False,
    )
```

```python
import functools
import math

import jax
import jax.numpy as jnp
import numpy as np
from jax import lax
from jax.experimental import pallas as pl
from jax.experimental.pallas import tpu as pltpu
from jax.sharding import PartitionSpec as P

BS = 138
MIB = 1 << 20
HIGH = lax.Precision.HIGHEST
F32 = jnp.float32
BF16 = jnp.bfloat16
I16 = jnp.int16
WIDE = 2304
SPAN = 1152
ROWS = (672, 432)
CUT = (0, 672)
TOP = (336, 224)
FOLD = (96, 64)
STEP = (28, 18)
POINTS = 2048


def in_hbm(array):
    return pltpu.with_memory_space_constraint(array, pltpu.HBM)


def widen(tail):
    return jnp.concatenate([tail.astype(F32), jnp.zeros(tail.shape[:-1] + (128 - tail.shape[-1],), F32)], axis=-1)


def place_tails(tails, out, rows):
    lane = lax.broadcasted_iota(jnp.int32, (16, 128), 1) // 16
    for half in range(2):
        rest = jnp.zeros((16, 128), F32)
        for n in range(8):
            tail = tails[half * 8 + n]
            rest = jnp.where(lane == n, pltpu.roll(tail, 16 * n, 1) if n else tail, rest)
        out(half, rest.astype(BF16))


def pack_left_kernel(pairs, mask, blocks, after, out):
    def step(p, carry):
        pair = jnp.transpose(blocks[:, pl.ds(2 * p, 2)], (1, 0, 2, 3)).reshape(16, 16, BS)
        wide = jnp.swapaxes(pair, 0, 1)
        rows = pl.ds(pl.multiple_of(16 * p, 16), 16)
        tails = []
        for k in range(16):
            at = SPAN * (k // 8) + 128 * (k % 8)
            out[rows, at : at + 128] = wide[k, :, :128] * mask[k]
            tails.append(widen(wide[k, :, 128:] * mask[k, :, : BS - 128]))

        def put(half, value):
            out[rows, SPAN * half + 1024 : SPAN * half + 1152] = value

        place_tails(tails, put, rows)
        return carry

    lax.fori_loop(0, pairs, step, 0)


def pack_left(half, mask, blocks, after):
    count = STEP[half]
    return pl.pallas_call(
        functools.partial(pack_left_kernel, count // 2),
        grid=(ROWS[half] // 8 // count,),
        in_specs=[
            pl.BlockSpec((16, 16, 128), lambda g: (0, 0, 0)),
            pl.BlockSpec(
                (pl.Element(8), pl.Element(count), pl.Element(16), pl.Element(BS)),
                lambda g: (0, CUT[half] // 8 + count * g, 0, 0),
            ),
            pl.BlockSpec(memory_space=pl.ANY),
        ],
        out_specs=pl.BlockSpec((count * 8, WIDE), lambda g: (g, 0)),
        out_shape=pltpu.VMEM((ROWS[half], WIDE), BF16),
        compiler_params=pltpu.CompilerParams(vmem_limit_bytes=32 * MIB),
        cost_estimate=pl.CostEstimate(flops=1000, bytes_accessed=1000, transcendentals=0),
        name="pack_left",
    )(mask, in_hbm(blocks), after)


def pack_right_kernel(blocks, *others):
    near, rest = others[-2:]
    base = pl.program_id(0) % 4 * 2

    def step(n, carry):
        k = base + n
        for c in range(0, 144, 16):
            if c < 128:
                rows = pl.ds(pl.multiple_of(128 * k + c, 16), 16)
                square = blocks[n, c : c + 16]
            else:
                rows = pl.ds(pl.multiple_of(1024 + 16 * k, 16), 16)
                square = jnp.concatenate([blocks[n, 128:BS], jnp.zeros((144 - BS, 16, BS), BF16)], axis=0)
            turned = jnp.swapaxes(square, 0, 1)
            near[:, rows, :] = turned[:, :, :128]

            def put(half, value, rows=rows):
                rest[rows, 128 * half : 128 * half + 128] = value

            place_tails([widen(turned[j, :, 128:]) for j in range(16)], put, rows)
        return carry

    lax.fori_loop(0, 2, step, 0)


def pack_right(blocks, before):
    return pl.pallas_call(
        pack_right_kernel,
        grid=(8,),
        in_specs=[pl.BlockSpec((2, BS, 16, BS), lambda g: (g, 0, 0, 0))]
        + [pl.BlockSpec(memory_space=pl.ANY)] * len(before),
        out_specs=[
            pl.BlockSpec((16, SPAN, 128), lambda g: (0, g // 4, 0)),
            pl.BlockSpec((SPAN, 256), lambda g: (g // 4, 0)),
        ],
        out_shape=[
            pltpu.VMEM((16, WIDE, 128), BF16),
            pltpu.VMEM((WIDE, 256), BF16),
        ],
        compiler_params=pltpu.CompilerParams(vmem_limit_bytes=24 * MIB),
        cost_estimate=pl.CostEstimate(flops=1000, bytes_accessed=1000, transcendentals=0),
        name="pack_right",
    )(in_hbm(blocks), *before)


def tails_kernel(half, left, rest, swap, after, out):
    right = rest[...]
    if half == 1:
        right = jnp.dot(right, swap[...], preferred_element_type=F32).astype(BF16)
    out[...] = jnp.dot(left[...], right, preferred_element_type=F32)


def product_tails(half, left, rest, after):
    lane = np.arange(256)
    swap = np.zeros((256, 256), np.float32)
    swap[lane, lane // 16 % 4 * 64 + lane // 64 * 16 + lane % 16] = 1.0
    vmem = pl.BlockSpec(memory_space=pltpu.VMEM)
    return pl.pallas_call(
        functools.partial(tails_kernel, half),
        in_specs=[vmem] * 3 + [pl.BlockSpec(memory_space=pl.ANY)],
        out_specs=vmem,
        out_shape=jax.ShapeDtypeStruct((ROWS[half], 256), F32),
        compiler_params=pltpu.CompilerParams(vmem_limit_bytes=12 * MIB),
        cost_estimate=pl.CostEstimate(flops=1000, bytes_accessed=1000, transcendentals=0),
        name="product_tails",
    )(left, rest, jnp.asarray(swap, BF16), after)


def padded(value, rows):
    if value.shape[0] == rows:
        return value
    return jnp.concatenate([value, jnp.zeros((rows - value.shape[0], 128), F32)], axis=0)


def lanes(rows):
    return lax.broadcasted_iota(jnp.int32, (rows, 128), 1)


def scale_of(most):
    power = jnp.floor(jnp.log2(jnp.maximum(jnp.full((1, 128), most, F32), 1e-30))) + 1.0
    return power, 32000.0 * jnp.exp2(-power)


def gain_of(coded):
    power = jnp.max(jnp.where(lanes(16) % 16 == 15, coded[0:16], -1000.0))
    return jnp.exp2(jnp.full((1, 128), power, F32)) * (1.0 / 32000.0)


def code(value, gain):
    return jnp.round(value * gain).astype(jnp.int32).astype(I16)


def code_tail(value, gain, power):
    coded = jnp.where(lanes(value.shape[0]) % 16 == 15, jnp.broadcast_to(power, value.shape), jnp.round(value * gain))
    return coded.astype(jnp.int32).astype(I16)


def plain(value):
    return value.astype(jnp.int32).astype(F32)


def product_kernel(half, d, spot, left, near, tails, after, out, held):
    rows = ROWS[half]
    coded = d != 0
    group = (spot[half] + d) % 4
    which = [4 * group + n if half == 0 else 4 * n + group for n in range(4)]
    for pair in range(2):
        both = jnp.dot(
            left[...],
            jnp.concatenate([near[which[2 * pair]], near[which[2 * pair + 1]]], axis=1),
            preferred_element_type=F32,
        )
        if coded:
            held[2 * pair] = both[:, :128]
            held[2 * pair + 1] = both[:, 128:]
        else:
            out[2 * pair * rows : (2 * pair + 1) * rows, :] = both[:, :128]
            out[(2 * pair + 1) * rows : (2 * pair + 2) * rows, :] = both[:, 128:]
    tail = jnp.where(group >= 2, tails[:, 128:], tails[:, :128])
    top = TOP[half]
    high, low = tail[:top], padded(tail[top:], top)
    odd = group % 2 == 1
    folded = jnp.where(
        lanes(top) < 64,
        jnp.where(odd, pltpu.roll(high, 64, 1), high),
        jnp.where(odd, low, pltpu.roll(low, 64, 1)),
    )
    if coded:
        power, gain = scale_of(jnp.maximum(jnp.max(jnp.abs(held[...])), jnp.max(jnp.abs(folded))))
        for n in range(4):
            out[n * rows : (n + 1) * rows, :] = code(held[n], gain)
        out[4 * rows : 4 * rows + TOP[half], :] = code_tail(folded, gain, power)
    else:
        out[4 * rows : 4 * rows + TOP[half], :] = folded


def product_group(half, d, spot, left, near, tails, after):
    rows = ROWS[half]
    coded = d != 0
    vmem = pl.BlockSpec(memory_space=pltpu.VMEM)
    return pl.pallas_call(
        functools.partial(product_kernel, half, d),
        in_specs=[pl.BlockSpec(memory_space=pltpu.SMEM)] + [vmem] * 3 + [pl.BlockSpec(memory_space=pl.ANY)],
        out_specs=vmem,
        out_shape=jax.ShapeDtypeStruct((4 * rows + TOP[half], 128), I16 if coded else F32),
        scratch_shapes=[pltpu.VMEM((4, rows, 128), F32)],
        compiler_params=pltpu.CompilerParams(vmem_limit_bytes=10 * MIB),
        cost_estimate=pl.CostEstimate(flops=1000, bytes_accessed=1000, transcendentals=0),
        name="product_coded" if coded else "product_own",
    )(spot, left, near, tails, after)


def merge_kernel(half, place, own, in1, in2, in3, after, mine, out1, out2, out3, held):
    rows, top, size = ROWS[half], TOP[half], FOLD[half]
    parts = (in1, in2, in3)
    tails = [plain(p[4 * rows : 4 * rows + top, :]) for p in parts]
    gains = [gain_of(t) for t in tails]
    for n in range(4):
        here = slice(n * rows, (n + 1) * rows)
        total = own[here, :]
        for p, g in zip(parts, gains):
            total = total + plain(p[here, :]) * g
        held[n] = total
    folded = own[4 * rows : 4 * rows + top, :]
    for t, g in zip(tails, gains):
        folded = folded + t * g
    pieces = [padded(folded[q * size : min(top, (q + 1) * size)], size) for q in range(4)]
    slot = lanes(size) // 16 % 4
    for s in range(4):

        @pl.when(place[1 - half] == s)
        def _(s=s):
            for d, out in enumerate((mine, out1, out2, out3)):
                here = (s + d) % 4
                tail = jnp.zeros((size, 128), F32)
                for q in range(4):
                    tail = jnp.where(slot == q, pltpu.roll(pieces[q], 16 * ((q - here) % 8), 1) if (q - here) % 8 else pieces[q], tail)
                main = held[here]
                if d == 0:
                    out[0:rows, :] = main
                    out[rows : rows + size, :] = tail
                else:
                    tail = jnp.where(lanes(size) % 16 < 10, tail, 0.0)
                    power, gain = scale_of(jnp.maximum(jnp.max(jnp.abs(main)), jnp.max(jnp.abs(tail))))
                    out[0:rows, :] = code(main, gain)
                    out[rows : rows + size, :] = code_tail(tail, gain, power)


def merge(half, place, own, parts, after):
    vmem = pl.BlockSpec(memory_space=pltpu.VMEM)
    return pl.pallas_call(
        functools.partial(merge_kernel, half),
        in_specs=[pl.BlockSpec(memory_space=pltpu.SMEM)] + [vmem] * 4 + [pl.BlockSpec(memory_space=pl.ANY)],
        out_specs=[vmem] * 4,
        out_shape=[jax.ShapeDtypeStruct((ROWS[half] + FOLD[half], 128), t) for t in (F32, I16, I16, I16)],
        scratch_shapes=[pltpu.VMEM((4, ROWS[half], 128), F32)],
        compiler_params=pltpu.CompilerParams(vmem_limit_bytes=12 * MIB),
        cost_estimate=pl.CostEstimate(flops=1000, bytes_accessed=1000, transcendentals=0),
        name="merge",
    )(place, own, *parts, after)


def turn(dy, dz):
    return [(4 * y + z, (y + dy) % 4 * 4 + (z + dz) % 4) for y in range(4) for z in range(4)]


def send(array, axis, d):
    return lax.ppermute(array, "col", turn(d, 0) if axis == 0 else turn(0, d))


def exchange_products(blocks_a, pattern, blocks_b, before):
    place = lax.axis_index("col").astype(jnp.int32)
    spot = jnp.stack([place // 4, place % 4])
    mask = jnp.broadcast_to(jnp.tile(pattern.T, (1, 2))[:, :, None], (16, 16, 128)).astype(BF16)
    blocks_a = jnp.transpose(blocks_a, (0, 2, 1, 3))
    near, rest = pack_right(jnp.transpose(blocks_b, (0, 2, 1, 3)), [mask, spot] + before)
    after = near
    parts, owns = ([], []), []
    lefts = []
    for half in range(2):
        left = pack_left(half, mask, blocks_a, after)
        tails = product_tails(half, left, rest, after)
        lefts.append((left, near, tails))
        after = tails
        for d in (1, 2, 3):
            last = product_group(half, d, spot, *lefts[half], after)
            parts[half].append(send(last, half, d))
        after = last
    for half in range(2):
        after = product_group(half, 0, spot, *lefts[half], after)
        owns.append(after)

    def finish(half, after):
        mine, *outs = merge(half, spot, owns[half], parts[half], after)
        return mine, [send(outs[d - 1], 1 - half, d) for d in (2, 1, 3)]

    return finish, after


def collocate_kernel(half, keep, ids, own, in1, in2, in3, cols, rows, after, *rest):
    size = FOLD[half]
    if half == 0:
        density, out, stacked, right, held, held_cols, sems = rest
        before = None
    else:
        before, density, out, stacked, right, held, held_cols, sems = rest
    count = ROWS[half]
    tiles = 16384 // POINTS

    def copies(g):
        spot = pl.ds(pl.multiple_of(g * POINTS, POINTS), POINTS)
        return (
            pltpu.make_async_copy(cols.at[0, :, spot], held_cols.at[g], sems.at[0, g]),
            pltpu.make_async_copy(
                rows.at[pl.ds(CUT[half] // 8, count // 8), :, spot], held.at[g], sems.at[1, g]
            ),
        )

    for g in range(tiles):
        for copy in copies(g):
            copy.start()

    def decode_density():
        main, fold = own[0:count, :], own[count : count + size, :]
        for part in (in1, in2, in3):
            extra = plain(part[count : count + size, :])
            gain = gain_of(extra)
            main, fold = main + plain(part[0:count, :]) * gain, fold + extra * gain
        tails = []
        for base, total in ((0, TOP[half]), (4, count - TOP[half])):
            for q in range(4):
                piece = fold[0 : min(size, total - q * size)]
                shift = (128 - 16 * (q + base)) % 128
                tails.append(pltpu.roll(piece, shift, 1) if shift else piece)
        tail = jnp.where(lanes(count) < BS - 128, jnp.concatenate(tails, axis=0), 0.0)
        kept = keep[...][None]
        main = (main.reshape(count // 8, 8, 128) * kept).reshape(count, 128).astype(BF16)
        tail = (tail.reshape(count // 8, 8, 128) * kept).reshape(count, 128).astype(BF16)
        stacked[:, 0:128] = main
        stacked[:, 128:256] = tail
        density[:, :, 0:128] = main.reshape(count // 8, 8, 128)
        density[:, :, 128:BS] = tail.reshape(count // 8, 8, 128)[:, :, : BS - 128]
        right[128:256, :] = jnp.zeros((128, POINTS), BF16)

    decode_density()

    def step(g, carry):
        for copy in copies(g):
            copy.wait()
        right[0:BS, :] = held_cols[g]
        tile(g)
        return carry

    def tile(g):
        per = POINTS // 1024
        for t in range(POINTS // 256):
            here = slice(t * 256, (t + 1) * 256)
            inner = jnp.dot(stacked[...], right[:, here], preferred_element_type=F32).reshape(count // 8, 8, 256)
            total = jnp.sum(inner * held[g, :, :, here].astype(F32), axis=0)
            within = slice(t % 4 * 256, t % 4 * 256 + 256)
            if half == 1:
                total = total + before[per * g + t // 4, :, within]
            out[per * g + t // 4, :, within] = total
        if half == 1:
            for n in range(POINTS // 1024):
                out[per * g + n, :, 1024:1152] = ids[...]

    lax.fori_loop(0, tiles, step, 0)


def collocate(half, keep, ids, own, parts, basis_cols, basis_rows, before, after):
    count = ROWS[half]
    wide = 1152 if half else 1024
    vmem = pl.BlockSpec(memory_space=pltpu.VMEM)
    tiles = 16384 // POINTS
    return pl.pallas_call(
        functools.partial(collocate_kernel, half),
        in_specs=[vmem] * 6
        + [pl.BlockSpec(memory_space=pltpu.HBM)] * 2
        + [pl.BlockSpec(memory_space=pl.ANY)]
        + [vmem] * half,
        out_specs=[vmem] * 2,
        scratch_shapes=[
            pltpu.VMEM((count, 256), BF16),
            pltpu.VMEM((256, POINTS), BF16),
            pltpu.VMEM((tiles, count // 8, 8, POINTS), BF16),
            pltpu.VMEM((tiles, BS, POINTS), BF16),
            pltpu.SemaphoreType.DMA((2, tiles)),
        ],
        out_shape=[
            jax.ShapeDtypeStruct((count // 8, 8, BS), BF16),
            jax.ShapeDtypeStruct((16, 8, wide), F32),
        ],
        compiler_params=pltpu.CompilerParams(vmem_limit_bytes=(38, 28)[half] * MIB),
        cost_estimate=pl.CostEstimate(flops=1000, bytes_accessed=1000, transcendentals=0),
        name="collocate",
    )(keep, ids, own, *parts, in_hbm(basis_cols), in_hbm(basis_rows), after, *before)


def bricks_kernel(points, out):
    owners = jnp.sum(points[:, :, 1024:1152].reshape(128, 128), axis=0, keepdims=True).astype(jnp.int32)
    onehot = (owners == lax.broadcasted_iota(jnp.int32, (128, 128), 0)).astype(F32)
    held = points[:, :, 0:1024].reshape(128, 1024)
    out[...] = jnp.dot(onehot, held, precision=HIGH, preferred_element_type=F32)


def sum_bricks(points):
    return pl.pallas_call(
        bricks_kernel,
        out_shape=jax.ShapeDtypeStruct((128, 1024), F32),
        compiler_params=pltpu.CompilerParams(vmem_limit_bytes=8 * MIB),
        cost_estimate=pl.CostEstimate(flops=1000, bytes_accessed=1000, transcendentals=0),
        name="sum_bricks",
    )(points)


def tables():
    a = np.arange(16)
    outer = 2.0 * math.pi * (np.outer(a, a) % 16) / 16
    eye = np.eye(8)
    ck, sk = np.kron(eye, np.cos(outer)), np.kron(eye, np.sin(outer))
    b = np.arange(128)
    inner = 2.0 * math.pi * (np.outer(b, b) % 128) / 128
    c, s = np.cos(inner), np.sin(inner)
    twist = 2.0 * math.pi * np.outer(np.tile(a, 8), b) / 2048
    first = np.concatenate([ck, -sk], 0)
    second = np.block([[c, -s], [s, c]])
    third = np.block([[c, s], [-s, c]])
    last = np.concatenate([ck, -sk], 1) / 2048
    return [np.asarray(t, np.float32) for t in (first, second, third, last, np.cos(twist), np.sin(twist))]


def filter_kernel(own, in1, in2, in3, kern, first, second, third, last, tc, ts, out):
    def dot(p, q):
        return jnp.dot(p, q, precision=HIGH, preferred_element_type=F32)

    grid = (own[...] + in1[...]) + (in2[...] + in3[...])
    grid = jnp.concatenate([grid[:, y * 128 : y * 128 + 128] for y in range(8)], axis=0)
    section = dot(first[...], grid)
    re, im = section[:128], section[128:]
    c, s = tc[...], ts[...]
    spec = dot(jnp.concatenate([re * c + im * s, im * c - re * s], axis=1), second[...])
    k = kern[...]
    back = dot(spec * jnp.concatenate([k, k], axis=1), third[...])
    re, im = back[:, :128], back[:, 128:]
    turned = jnp.concatenate([re * c - im * s, im * c + re * s], axis=0)
    result = dot(last[...], turned)
    for y in range(8):
        out[:, y, :] = result[y * 16 : y * 16 + 16]


def filter_rows(pieces, kern):
    return pl.pallas_call(
        filter_kernel,
        out_shape=jax.ShapeDtypeStruct((16, 8, 128), F32),
        compiler_params=pltpu.CompilerParams(vmem_limit_bytes=8 * MIB),
        cost_estimate=pl.CostEstimate(flops=1000, bytes_accessed=1000, transcendentals=0),
        name="filter_rows",
    )(*pieces, kern, *tables())


def scatter_rows(partial):
    place = lax.axis_index("row")
    x, core = place // 2, place % 2
    halves = partial.reshape(4, 2, 16, 1024)
    away = lax.dynamic_index_in_dim(halves, 1 - core, 1, keepdims=False)
    mine = lax.dynamic_index_in_dim(halves, core, 1, keepdims=False)
    mine = mine + lax.ppermute(away, "row", [(r, r ^ 1) for r in range(8)])
    pieces = [lax.dynamic_index_in_dim(mine, x, 0, keepdims=False)]
    for d in (1, 2, 3):
        part = lax.dynamic_index_in_dim(mine, (x + d) % 4, 0, keepdims=False)
        pieces.append(lax.ppermute(part, "row", [(r, (r + 2 * d) % 8) for r in range(8)]))
    return pieces


def shards(blocks_a, pattern_a, blocks_b, filter_mask, task_brick, basis_rows, basis_cols, kernel):
    kern = jnp.transpose(kernel.reshape(8, 128, 16), (0, 2, 1)).reshape(128, 128)
    lane = jnp.arange(128, dtype=jnp.int32)
    owners = jnp.where(lane // 8 == lax.axis_index("col"), jnp.tile(task_brick.reshape(8), 16), 0)
    ids = jnp.concatenate([owners.astype(F32)[None], jnp.zeros((7, 128), F32)], axis=0)
    keep = jnp.broadcast_to(filter_mask.reshape(8, 1).astype(F32), (8, 128))
    by_point = jnp.transpose(basis_rows, (1, 0, 2))
    finish, after = exchange_products(blocks_a, pattern_a, blocks_b, [kern, ids, keep])
    densities, before, sums = [], [], []
    for half in range(2):
        sums.append(finish(half, after))
        after = sums[half][0]
    for half in range(2):
        own, parts = sums[half]
        density, after = collocate(half, keep, ids, own, parts, basis_cols, by_point, before, after)
        densities.append(density)
        before = [after]
    points = after
    points = lax.all_to_all(points, "col", split_axis=0, concat_axis=0, tiled=True)
    pieces = scatter_rows(sum_bricks(points))
    filtered = filter_rows(pieces, kern)
    potential = lax.all_to_all(filtered, "col", split_axis=0, concat_axis=0, tiled=True)
    density = jnp.transpose(jnp.concatenate(densities, axis=0), (1, 0, 2))
    return density[:, None], potential.reshape(128, 128)


def solution(mesh):
    return jax.shard_map(
        shards,
        mesh=mesh,
        in_specs=(
            P("row", "col", None, None),
            P("row", "col"),
            P("col", None, None, None),
            P("row", "col"),
            P("row", "col"),
            P("row", None, None),
            P("col", None, None),
            P(("row", "col"), None),
        ),
        out_specs=(P("row", "col", None, None), P("row", "col")),
        check_vma=False,
    )
```

```python
import functools
import math

import jax
import jax.numpy as jnp
import numpy as np
from jax import lax
from jax.experimental import pallas as pl
from jax.experimental.pallas import tpu as pltpu
from jax.sharding import PartitionSpec as P

BS = 138
MIB = 1 << 20
HIGH = lax.Precision.HIGHEST
F32 = jnp.float32
BF16 = jnp.bfloat16
I16 = jnp.int16
WIDE = 2304
SPAN = 1152
ROWS = (672, 432)
CUT = (0, 672)
TOP = (336, 224)
FOLD = (96, 64)
STEP = (28, 18)
POINTS = 2048
EARLY = 56


def in_hbm(array):
    return pltpu.with_memory_space_constraint(array, pltpu.HBM)


def widen(tail):
    return jnp.concatenate([tail.astype(F32), jnp.zeros(tail.shape[:-1] + (128 - tail.shape[-1],), F32)], axis=-1)


def place_tails(tails, out, rows):
    lane = lax.broadcasted_iota(jnp.int32, (16, 128), 1) // 16
    for half in range(2):
        rest = jnp.zeros((16, 128), F32)
        for n in range(8):
            tail = tails[half * 8 + n]
            rest = jnp.where(lane == n, pltpu.roll(tail, 16 * n, 1) if n else tail, rest)
        out(half, rest.astype(BF16))


def pack_left_kernel(pairs, pattern, blocks, after, out, mask):
    @pl.when(pl.program_id(0) == 0)
    def _():
        kept = pattern[...].astype(F32)
        for k in range(16):
            column = jnp.broadcast_to(kept[:, k : k + 1], (8, 128))
            mask[k] = jnp.concatenate([column, column], axis=0).astype(BF16)

    def step(p, carry):
        pair = jnp.transpose(blocks[:, pl.ds(2 * p, 2)], (1, 0, 2, 3)).reshape(16, 16, BS)
        wide = jnp.swapaxes(pair, 0, 1)
        rows = pl.ds(pl.multiple_of(16 * p, 16), 16)
        tails = []
        for k in range(16):
            at = SPAN * (k // 8) + 128 * (k % 8)
            out[rows, at : at + 128] = wide[k, :, :128] * mask[k]
            tails.append(widen(wide[k, :, 128:] * mask[k, :, : BS - 128]))

        def put(half, value):
            out[rows, SPAN * half + 1024 : SPAN * half + 1152] = value

        place_tails(tails, put, rows)
        return carry

    lax.fori_loop(0, pairs, step, 0)


def pack_left(half, pattern, blocks, after):
    count = STEP[half]
    return pl.pallas_call(
        functools.partial(pack_left_kernel, count // 2),
        grid=(ROWS[half] // 8 // count,),
        in_specs=[
            pl.BlockSpec((8, 16), lambda g: (0, 0)),
            pl.BlockSpec(
                (pl.Element(8), pl.Element(count), pl.Element(16), pl.Element(BS)),
                lambda g: (0, CUT[half] // 8 + count * g, 0, 0),
            ),
            pl.BlockSpec(memory_space=pl.ANY),
        ],
        out_specs=pl.BlockSpec((count * 8, WIDE), lambda g: (g, 0)),
        out_shape=pltpu.VMEM((ROWS[half], WIDE), BF16),
        scratch_shapes=[pltpu.VMEM((16, 16, 128), BF16)],
        compiler_params=pltpu.CompilerParams(vmem_limit_bytes=32 * MIB),
        cost_estimate=pl.CostEstimate(flops=1000, bytes_accessed=1000, transcendentals=0),
        name="pack_left",
    )(pattern, in_hbm(blocks), after)


def pack_right_kernel(blocks, *others):
    near, rest = others[-2:]
    base = pl.program_id(0) % 4 * 2

    def step(n, carry):
        k = base + n
        for c in range(0, 144, 16):
            if c < 128:
                rows = pl.ds(pl.multiple_of(128 * k + c, 16), 16)
                square = blocks[n, c : c + 16]
            else:
                rows = pl.ds(pl.multiple_of(1024 + 16 * k, 16), 16)
                square = jnp.concatenate([blocks[n, 128:BS], jnp.zeros((144 - BS, 16, BS), BF16)], axis=0)
            turned = jnp.swapaxes(square, 0, 1)
            near[:, rows, :] = turned[:, :, :128]

            def put(half, value, rows=rows):
                rest[rows, 128 * half : 128 * half + 128] = value

            place_tails([widen(turned[j, :, 128:]) for j in range(16)], put, rows)
        return carry

    lax.fori_loop(0, 2, step, 0)


def pack_right(blocks, before):
    return pl.pallas_call(
        pack_right_kernel,
        grid=(8,),
        in_specs=[pl.BlockSpec((2, BS, 16, BS), lambda g: (g, 0, 0, 0))]
        + [pl.BlockSpec(memory_space=pl.ANY)] * len(before),
        out_specs=[
            pl.BlockSpec((16, SPAN, 128), lambda g: (0, g // 4, 0)),
            pl.BlockSpec((SPAN, 256), lambda g: (g // 4, 0)),
        ],
        out_shape=[
            pltpu.VMEM((16, WIDE, 128), BF16),
            pltpu.VMEM((WIDE, 256), BF16),
        ],
        compiler_params=pltpu.CompilerParams(vmem_limit_bytes=24 * MIB),
        cost_estimate=pl.CostEstimate(flops=1000, bytes_accessed=1000, transcendentals=0),
        name="pack_right",
    )(in_hbm(blocks), *before)


def tails_kernel(half, left, rest, swap, after, out):
    right = rest[...]
    if half == 1:
        right = jnp.dot(right, swap[...], preferred_element_type=F32).astype(BF16)
    out[...] = jnp.dot(left[...], right, preferred_element_type=F32)


def product_tails(half, left, rest, after):
    lane = np.arange(256)
    swap = np.zeros((256, 256), np.float32)
    swap[lane, lane // 16 % 4 * 64 + lane // 64 * 16 + lane % 16] = 1.0
    vmem = pl.BlockSpec(memory_space=pltpu.VMEM)
    return pl.pallas_call(
        functools.partial(tails_kernel, half),
        in_specs=[vmem] * 3 + [pl.BlockSpec(memory_space=pl.ANY)],
        out_specs=vmem,
        out_shape=jax.ShapeDtypeStruct((ROWS[half], 256), F32),
        compiler_params=pltpu.CompilerParams(vmem_limit_bytes=12 * MIB),
        cost_estimate=pl.CostEstimate(flops=1000, bytes_accessed=1000, transcendentals=0),
        name="product_tails",
    )(left, rest, jnp.asarray(swap, BF16), after)


def padded(value, rows):
    if value.shape[0] == rows:
        return value
    return jnp.concatenate([value, jnp.zeros((rows - value.shape[0], 128), F32)], axis=0)


def lanes(rows):
    return lax.broadcasted_iota(jnp.int32, (rows, 128), 1)


def scale_of(most):
    power = jnp.floor(jnp.log2(jnp.maximum(jnp.full((1, 128), most, F32), 1e-30))) + 1.0
    return power, 32000.0 * jnp.exp2(-power)


def gain_of(coded):
    power = jnp.max(jnp.where(lanes(16) % 16 == 15, coded[0:16], -1000.0))
    return jnp.exp2(jnp.full((1, 128), power, F32)) * (1.0 / 32000.0)


def code(value, gain):
    return jnp.round(value * gain).astype(jnp.int32).astype(I16)


def code_tail(value, gain, power):
    coded = jnp.where(lanes(value.shape[0]) % 16 == 15, jnp.broadcast_to(power, value.shape), jnp.round(value * gain))
    return coded.astype(jnp.int32).astype(I16)


def plain(value):
    return value.astype(jnp.int32).astype(F32)


def product_kernel(half, d, spot, left, near, tails, after, out, held):
    rows = ROWS[half]
    coded = d != 0
    group = (spot[half] + d) % 4
    which = [4 * group + n if half == 0 else 4 * n + group for n in range(4)]
    for pair in range(2):
        both = jnp.dot(
            left[...],
            jnp.concatenate([near[which[2 * pair]], near[which[2 * pair + 1]]], axis=1),
            preferred_element_type=F32,
        )
        if coded:
            held[2 * pair] = both[:, :128]
            held[2 * pair + 1] = both[:, 128:]
        else:
            out[2 * pair * rows : (2 * pair + 1) * rows, :] = both[:, :128]
            out[(2 * pair + 1) * rows : (2 * pair + 2) * rows, :] = both[:, 128:]
    tail = jnp.where(group >= 2, tails[:, 128:], tails[:, :128])
    top = TOP[half]
    high, low = tail[:top], padded(tail[top:], top)
    odd = group % 2 == 1
    folded = jnp.where(
        lanes(top) < 64,
        jnp.where(odd, pltpu.roll(high, 64, 1), high),
        jnp.where(odd, low, pltpu.roll(low, 64, 1)),
    )
    if coded:
        power, gain = scale_of(jnp.maximum(jnp.max(jnp.abs(held[...])), jnp.max(jnp.abs(folded))))
        for n in range(4):
            out[n * rows : (n + 1) * rows, :] = code(held[n], gain)
        out[4 * rows : 4 * rows + TOP[half], :] = code_tail(folded, gain, power)
    else:
        out[4 * rows : 4 * rows + TOP[half], :] = folded


def product_group(half, d, spot, left, near, tails, after):
    rows = ROWS[half]
    coded = d != 0
    vmem = pl.BlockSpec(memory_space=pltpu.VMEM)
    return pl.pallas_call(
        functools.partial(product_kernel, half, d),
        in_specs=[pl.BlockSpec(memory_space=pltpu.SMEM)] + [vmem] * 3 + [pl.BlockSpec(memory_space=pl.ANY)],
        out_specs=vmem,
        out_shape=jax.ShapeDtypeStruct((4 * rows + TOP[half], 128), I16 if coded else F32),
        scratch_shapes=[pltpu.VMEM((4, rows, 128), F32)],
        compiler_params=pltpu.CompilerParams(vmem_limit_bytes=10 * MIB),
        cost_estimate=pl.CostEstimate(flops=1000, bytes_accessed=1000, transcendentals=0),
        name="product_coded" if coded else "product_own",
    )(spot, left, near, tails, after)


def merge_kernel(half, place, own, in1, in2, in3, after, mine, out1, out2, out3, held):
    rows, top, size = ROWS[half], TOP[half], FOLD[half]
    parts = (in1, in2, in3)
    tails = [plain(p[4 * rows : 4 * rows + top, :]) for p in parts]
    gains = [gain_of(t) for t in tails]
    for n in range(4):
        here = slice(n * rows, (n + 1) * rows)
        total = own[here, :]
        for p, g in zip(parts, gains):
            total = total + plain(p[here, :]) * g
        held[n] = total
    folded = own[4 * rows : 4 * rows + top, :]
    for t, g in zip(tails, gains):
        folded = folded + t * g
    pieces = [padded(folded[q * size : min(top, (q + 1) * size)], size) for q in range(4)]
    slot = lanes(size) // 16 % 4
    for s in range(4):

        @pl.when(place[1 - half] == s)
        def _(s=s):
            for d, out in enumerate((mine, out1, out2, out3)):
                here = (s + d) % 4
                tail = jnp.zeros((size, 128), F32)
                for q in range(4):
                    tail = jnp.where(slot == q, pltpu.roll(pieces[q], 16 * ((q - here) % 8), 1) if (q - here) % 8 else pieces[q], tail)
                main = held[here]
                if d == 0:
                    out[0:rows, :] = main
                    out[rows : rows + size, :] = tail
                else:
                    tail = jnp.where(lanes(size) % 16 < 10, tail, 0.0)
                    power, gain = scale_of(jnp.maximum(jnp.max(jnp.abs(main)), jnp.max(jnp.abs(tail))))
                    out[0:rows, :] = code(main, gain)
                    out[rows : rows + size, :] = code_tail(tail, gain, power)


def merge(half, place, own, parts, after):
    vmem = pl.BlockSpec(memory_space=pltpu.VMEM)
    return pl.pallas_call(
        functools.partial(merge_kernel, half),
        in_specs=[pl.BlockSpec(memory_space=pltpu.SMEM)] + [vmem] * 4 + [pl.BlockSpec(memory_space=pl.ANY)],
        out_specs=[vmem] * 4,
        out_shape=[jax.ShapeDtypeStruct((ROWS[half] + FOLD[half], 128), t) for t in (F32, I16, I16, I16)],
        scratch_shapes=[pltpu.VMEM((4, ROWS[half], 128), F32)],
        compiler_params=pltpu.CompilerParams(vmem_limit_bytes=12 * MIB),
        cost_estimate=pl.CostEstimate(flops=1000, bytes_accessed=1000, transcendentals=0),
        name="merge",
    )(place, own, *parts, after)


def turn(dy, dz):
    return [(4 * y + z, (y + dy) % 4 * 4 + (z + dz) % 4) for y in range(4) for z in range(4)]


def send(array, axis, d):
    return lax.ppermute(array, "col", turn(d, 0) if axis == 0 else turn(0, d))


def exchange_products(spot, blocks_a, pattern, blocks_b, by_point, before):
    blocks_a = jnp.transpose(blocks_a, (0, 2, 1, 3))
    near, rest = pack_right(jnp.transpose(blocks_b, (0, 2, 1, 3)), [spot] + before)
    after = near
    parts, owns = ([], []), []
    lefts = []
    for half in range(2):
        left = pack_left(half, pattern, blocks_a, after)
        tails = product_tails(half, left, rest, after)
        lefts.append((left, near, tails))
        after = tails
        for d in (1, 2, 3):
            last = product_group(half, d, spot, *lefts[half], after)
            parts[half].append(send(last, half, d))
        after = last
    for half in range(2):
        after = product_group(half, 0, spot, *lefts[half], after)
        owns.append(after)

    early, after = fetch(by_point, after)

    def finish(half, after):
        mine, *outs = merge(half, spot, owns[half], parts[half], after)
        return mine, [send(outs[d - 1], 1 - half, d) for d in (2, 1, 3)]

    return finish, early, after


def fetch_kernel(rows, after, out, done, sem):
    copy = pltpu.make_async_copy(rows.at[pl.ds(0, EARLY)], out, sem)
    copy.start()
    done[...] = jnp.zeros((8, 128), F32)
    copy.wait()


def fetch(rows, after):
    vmem = pl.BlockSpec(memory_space=pltpu.VMEM)
    return pl.pallas_call(
        fetch_kernel,
        in_specs=[pl.BlockSpec(memory_space=pltpu.HBM), pl.BlockSpec(memory_space=pl.ANY)],
        out_specs=[vmem, vmem],
        out_shape=[pltpu.VMEM((EARLY, 8, 16384), BF16), jax.ShapeDtypeStruct((8, 128), F32)],
        scratch_shapes=[pltpu.SemaphoreType.DMA],
        compiler_params=pltpu.CompilerParams(vmem_limit_bytes=20 * MIB),
        cost_estimate=pl.CostEstimate(flops=1000, bytes_accessed=1000, transcendentals=0),
        name="fetch",
    )(in_hbm(rows), after)


def collocate_kernel(half, spot, keep, ids, own, in1, in2, in3, cols, rows, after, *rest):
    size = FOLD[half]
    before, density, out, stacked, right, held, held_cols, sems = rest
    count = ROWS[half]
    first = EARLY if half == 0 else 0
    tiles = 16384 // POINTS

    def copies(g):
        span = pl.ds(pl.multiple_of(g * POINTS, POINTS), POINTS)
        return (
            pltpu.make_async_copy(cols.at[0, :, span], held_cols.at[g], sems.at[0, g]),
            pltpu.make_async_copy(
                rows.at[pl.ds(CUT[half] // 8 + first, count // 8 - first), :, span], held.at[g], sems.at[1, g]
            ),
        )

    for g in range(tiles):
        for copy in copies(g):
            copy.start()

    def decode_density():
        main, fold = own[0:count, :], own[count : count + size, :]
        for part in (in1, in2, in3):
            extra = plain(part[count : count + size, :])
            gain = gain_of(extra)
            main, fold = main + plain(part[0:count, :]) * gain, fold + extra * gain
        tails = []
        for base, total in ((0, TOP[half]), (4, count - TOP[half])):
            for q in range(4):
                piece = fold[0 : min(size, total - q * size)]
                shift = (128 - 16 * (q + base)) % 128
                tails.append(pltpu.roll(piece, shift, 1) if shift else piece)
        tail = jnp.where(lanes(count) < BS - 128, jnp.concatenate(tails, axis=0), 0.0)
        row = lax.broadcasted_iota(jnp.int32, (8, 128), 0)
        kept = jnp.zeros((8, 128), F32)
        for i in range(8):
            kept = jnp.where(row == i, keep[i].astype(F32), kept)
        kept = kept[None]
        main = (main.reshape(count // 8, 8, 128) * kept).reshape(count, 128).astype(BF16)
        tail = (tail.reshape(count // 8, 8, 128) * kept).reshape(count, 128).astype(BF16)
        stacked[:, 0:128] = main
        stacked[:, 128:256] = tail
        density[:, :, 0:128] = main.reshape(count // 8, 8, 128)
        density[:, :, 128:BS] = tail.reshape(count // 8, 8, 128)[:, :, : BS - 128]
        right[128:256, :] = jnp.zeros((128, POINTS), BF16)

    decode_density()

    def step(g, carry):
        for copy in copies(g):
            copy.wait()
        right[0:BS, :] = held_cols[g]
        tile(g)
        return carry

    def tile(g):
        per = POINTS // 1024
        for t in range(POINTS // 256):
            here = slice(t * 256, (t + 1) * 256)
            inner = jnp.dot(stacked[...], right[:, here], preferred_element_type=F32).reshape(count // 8, 8, 256)
            total = jnp.sum(inner[first:] * held[g, :, :, here].astype(F32), axis=0)
            if half == 0:
                at = pl.ds(pl.multiple_of(g * POINTS + t * 256, 256), 256)
                total = total + jnp.sum(inner[:first] * before[:, :, at].astype(F32), axis=0)
            within = slice(t % 4 * 256, t % 4 * 256 + 256)
            if half == 1:
                total = total + before[per * g + t // 4, :, within]
            out[per * g + t // 4, :, within] = total
        if half == 1:
            row = lax.broadcasted_iota(jnp.int32, (8, 128), 0)
            label = jnp.zeros((8, 128), F32)
            for i in range(8):
                here = (row == 0) & (lanes(8) == 32 * spot[0] + 8 * spot[1] + i)
                label = jnp.where(here, ids[i].astype(F32), label)
            for n in range(POINTS // 1024):
                out[per * g + n, :, 1024:1152] = label

    lax.fori_loop(0, tiles, step, 0)


def collocate(half, spot, keep, ids, own, parts, basis_cols, basis_rows, before, after):
    count = ROWS[half]
    wide = 1152 if half else 1024
    vmem = pl.BlockSpec(memory_space=pltpu.VMEM)
    first = EARLY if half == 0 else 0
    tiles = 16384 // POINTS
    return pl.pallas_call(
        functools.partial(collocate_kernel, half),
        in_specs=[pl.BlockSpec(memory_space=pltpu.SMEM)] * 3
        + [vmem] * 4
        + [pl.BlockSpec(memory_space=pltpu.HBM)] * 2
        + [pl.BlockSpec(memory_space=pl.ANY)]
        + [vmem],
        out_specs=[vmem] * 2,
        scratch_shapes=[
            pltpu.VMEM((count, 256), BF16),
            pltpu.VMEM((256, POINTS), BF16),
            pltpu.VMEM((tiles, count // 8 - first, 8, POINTS), BF16),
            pltpu.VMEM((tiles, BS, POINTS), BF16),
            pltpu.SemaphoreType.DMA((2, tiles)),
        ],
        out_shape=[
            jax.ShapeDtypeStruct((count // 8, 8, BS), BF16),
            jax.ShapeDtypeStruct((16, 8, wide), F32),
        ],
        compiler_params=pltpu.CompilerParams(vmem_limit_bytes=(24, 28)[half] * MIB),
        cost_estimate=pl.CostEstimate(flops=1000, bytes_accessed=1000, transcendentals=0),
        name="collocate",
    )(spot, keep, ids, own, *parts, in_hbm(basis_cols), in_hbm(basis_rows), after, *before)


def bricks_kernel(points, out):
    owners = jnp.sum(points[:, :, 1024:1152].reshape(128, 128), axis=0, keepdims=True).astype(jnp.int32)
    onehot = (owners == lax.broadcasted_iota(jnp.int32, (128, 128), 0)).astype(F32)
    held = points[:, :, 0:1024].reshape(128, 1024)
    out[...] = jnp.dot(onehot, held, precision=HIGH, preferred_element_type=F32)


def sum_bricks(points):
    return pl.pallas_call(
        bricks_kernel,
        out_shape=jax.ShapeDtypeStruct((128, 1024), F32),
        compiler_params=pltpu.CompilerParams(vmem_limit_bytes=8 * MIB),
        cost_estimate=pl.CostEstimate(flops=1000, bytes_accessed=1000, transcendentals=0),
        name="sum_bricks",
    )(points)


def tables():
    a = np.arange(16)
    outer = 2.0 * math.pi * (np.outer(a, a) % 16) / 16
    eye = np.eye(8)
    ck, sk = np.kron(eye, np.cos(outer)), np.kron(eye, np.sin(outer))
    b = np.arange(128)
    inner = 2.0 * math.pi * (np.outer(b, b) % 128) / 128
    c, s = np.cos(inner), np.sin(inner)
    twist = 2.0 * math.pi * np.outer(np.tile(a, 8), b) / 2048
    first = np.concatenate([ck, -sk], 0)
    second = np.block([[c, -s], [s, c]])
    third = np.block([[c, s], [-s, c]])
    last = np.concatenate([ck, -sk], 1) / 2048
    return [np.asarray(t, np.float32) for t in (first, second, third, last, np.cos(twist), np.sin(twist))]


def filter_kernel(own, in1, in2, in3, kern, first, second, third, last, tc, ts, out):
    def dot(p, q):
        return jnp.dot(p, q, precision=HIGH, preferred_element_type=F32)

    grid = (own[...] + in1[...]) + (in2[...] + in3[...])
    grid = jnp.concatenate([grid[:, y * 128 : y * 128 + 128] for y in range(8)], axis=0)
    section = dot(first[...], grid)
    re, im = section[:128], section[128:]
    c, s = tc[...], ts[...]
    spec = dot(jnp.concatenate([re * c + im * s, im * c - re * s], axis=1), second[...])
    k = kern[...]
    back = dot(spec * jnp.concatenate([k, k], axis=1), third[...])
    re, im = back[:, :128], back[:, 128:]
    turned = jnp.concatenate([re * c - im * s, im * c + re * s], axis=0)
    result = dot(last[...], turned)
    for y in range(8):
        out[:, y, :] = result[y * 16 : y * 16 + 16]


def filter_rows(pieces, kern):
    return pl.pallas_call(
        filter_kernel,
        out_shape=jax.ShapeDtypeStruct((16, 8, 128), F32),
        compiler_params=pltpu.CompilerParams(vmem_limit_bytes=8 * MIB),
        cost_estimate=pl.CostEstimate(flops=1000, bytes_accessed=1000, transcendentals=0),
        name="filter_rows",
    )(*pieces, kern, *tables())


def scatter_rows(partial):
    place = lax.axis_index("row")
    x, core = place // 2, place % 2
    halves = partial.reshape(4, 2, 16, 1024)
    away = lax.dynamic_index_in_dim(halves, 1 - core, 1, keepdims=False)
    mine = lax.dynamic_index_in_dim(halves, core, 1, keepdims=False)
    mine = mine + lax.ppermute(away, "row", [(r, r ^ 1) for r in range(8)])
    pieces = [lax.dynamic_index_in_dim(mine, x, 0, keepdims=False)]
    for d in (1, 2, 3):
        part = lax.dynamic_index_in_dim(mine, (x + d) % 4, 0, keepdims=False)
        pieces.append(lax.ppermute(part, "row", [(r, (r + 2 * d) % 8) for r in range(8)]))
    return pieces


def shards(blocks_a, pattern_a, blocks_b, filter_mask, task_brick, basis_rows, basis_cols, kernel):
    kern = jnp.transpose(kernel.reshape(8, 128, 16), (0, 2, 1)).reshape(128, 128)
    place = lax.axis_index("col").astype(jnp.int32)
    spot = jnp.stack([place // 4, place % 4])
    keep, ids = filter_mask.reshape(8), task_brick.reshape(8)
    by_point = jnp.transpose(basis_rows, (1, 0, 2))
    finish, early, after = exchange_products(spot, blocks_a, pattern_a, blocks_b, by_point, [kern])
    densities, before, sums = [], [], []
    for half in range(2):
        sums.append(finish(half, after))
        after = sums[half][0]
    for half in range(2):
        own, parts = sums[half]
        density, after = collocate(
            half, spot, keep, ids, own, parts, basis_cols, by_point, [early] if half == 0 else before, after
        )
        densities.append(density)
        before = [after]
    points = after
    points = lax.all_to_all(points, "col", split_axis=0, concat_axis=0, tiled=True)
    pieces = scatter_rows(sum_bricks(points))
    filtered = filter_rows(pieces, kern)
    potential = lax.all_to_all(filtered, "col", split_axis=0, concat_axis=0, tiled=True)
    density = jnp.transpose(jnp.concatenate(densities, axis=0), (1, 0, 2))
    return density[:, None], potential.reshape(128, 128)


def solution(mesh):
    return jax.shard_map(
        shards,
        mesh=mesh,
        in_specs=(
            P("row", "col", None, None),
            P("row", "col"),
            P("col", None, None, None),
            P("row", "col"),
            P("row", "col"),
            P("row", None, None),
            P("col", None, None),
            P(("row", "col"), None),
        ),
        out_specs=(P("row", "col", None, None), P("row", "col")),
        check_vma=False,
    )
```

```python
import functools
import math

import jax
import jax.numpy as jnp
import numpy as np
from jax import lax
from jax.experimental import pallas as pl
from jax.experimental.pallas import tpu as pltpu
from jax.sharding import PartitionSpec as P

BS = 138
MIB = 1 << 20
HIGH = lax.Precision.HIGHEST
F32 = jnp.float32
BF16 = jnp.bfloat16
I16 = jnp.int16
WIDE = 2304
SPAN = 1152
ROWS = (672, 432)
CUT = (0, 672)
TOP = (336, 224)
FOLD = (96, 64)
STEP = (28, 18)
POINTS = 2048


def in_hbm(array):
    return pltpu.with_memory_space_constraint(array, pltpu.HBM)


def widen(tail):
    return jnp.concatenate([tail.astype(F32), jnp.zeros(tail.shape[:-1] + (128 - tail.shape[-1],), F32)], axis=-1)


def place_tails(tails, out, rows):
    lane = lax.broadcasted_iota(jnp.int32, (16, 128), 1) // 16
    for half in range(2):
        rest = jnp.zeros((16, 128), F32)
        for n in range(8):
            tail = tails[half * 8 + n]
            rest = jnp.where(lane == n, pltpu.roll(tail, 16 * n, 1) if n else tail, rest)
        out(half, rest.astype(BF16))


def pack_left_kernel(pairs, pattern, blocks, after, out, mask):
    @pl.when(pl.program_id(0) == 0)
    def _():
        kept = pattern[...].astype(F32)
        for k in range(16):
            column = jnp.broadcast_to(kept[:, k : k + 1], (8, 128))
            mask[k] = jnp.concatenate([column, column], axis=0).astype(BF16)

    def step(p, carry):
        pair = jnp.transpose(blocks[:, pl.ds(2 * p, 2)], (1, 0, 2, 3)).reshape(16, 16, BS)
        wide = jnp.swapaxes(pair, 0, 1)
        rows = pl.ds(pl.multiple_of(16 * p, 16), 16)
        tails = []
        for k in range(16):
            at = SPAN * (k // 8) + 128 * (k % 8)
            out[rows, at : at + 128] = wide[k, :, :128] * mask[k]
            tails.append(widen(wide[k, :, 128:] * mask[k, :, : BS - 128]))

        def put(half, value):
            out[rows, SPAN * half + 1024 : SPAN * half + 1152] = value

        place_tails(tails, put, rows)
        return carry

    lax.fori_loop(0, pairs, step, 0)


def pack_left(half, pattern, blocks, after):
    count = STEP[half]
    return pl.pallas_call(
        functools.partial(pack_left_kernel, count // 2),
        grid=(ROWS[half] // 8 // count,),
        in_specs=[
            pl.BlockSpec((8, 16), lambda g: (0, 0)),
            pl.BlockSpec(
                (pl.Element(8), pl.Element(count), pl.Element(16), pl.Element(BS)),
                lambda g: (0, CUT[half] // 8 + count * g, 0, 0),
            ),
            pl.BlockSpec(memory_space=pl.ANY),
        ],
        out_specs=pl.BlockSpec((count * 8, WIDE), lambda g: (g, 0)),
        out_shape=pltpu.VMEM((ROWS[half], WIDE), BF16),
        scratch_shapes=[pltpu.VMEM((16, 16, 128), BF16)],
        compiler_params=pltpu.CompilerParams(vmem_limit_bytes=32 * MIB),
        cost_estimate=pl.CostEstimate(flops=1000, bytes_accessed=1000, transcendentals=0),
        name="pack_left",
    )(pattern, in_hbm(blocks), after)


def pack_right_kernel(blocks, *others):
    near, rest = others[-2:]
    base = pl.program_id(0) % 4 * 2

    def step(n, carry):
        k = base + n
        for c in range(0, 144, 16):
            if c < 128:
                rows = pl.ds(pl.multiple_of(128 * k + c, 16), 16)
                square = blocks[n, c : c + 16]
            else:
                rows = pl.ds(pl.multiple_of(1024 + 16 * k, 16), 16)
                square = jnp.concatenate([blocks[n, 128:BS], jnp.zeros((144 - BS, 16, BS), BF16)], axis=0)
            turned = jnp.swapaxes(square, 0, 1)
            near[:, rows, :] = turned[:, :, :128]

            def put(half, value, rows=rows):
                rest[rows, 128 * half : 128 * half + 128] = value

            place_tails([widen(turned[j, :, 128:]) for j in range(16)], put, rows)
        return carry

    lax.fori_loop(0, 2, step, 0)


def pack_right(blocks, before):
    return pl.pallas_call(
        pack_right_kernel,
        grid=(8,),
        in_specs=[pl.BlockSpec((2, BS, 16, BS), lambda g: (g, 0, 0, 0))]
        + [pl.BlockSpec(memory_space=pl.ANY)] * len(before),
        out_specs=[
            pl.BlockSpec((16, SPAN, 128), lambda g: (0, g // 4, 0)),
            pl.BlockSpec((SPAN, 256), lambda g: (g // 4, 0)),
        ],
        out_shape=[
            pltpu.VMEM((16, WIDE, 128), BF16),
            pltpu.VMEM((WIDE, 256), BF16),
        ],
        compiler_params=pltpu.CompilerParams(vmem_limit_bytes=24 * MIB),
        cost_estimate=pl.CostEstimate(flops=1000, bytes_accessed=1000, transcendentals=0),
        name="pack_right",
    )(in_hbm(blocks), *before)


def tails_kernel(half, left, rest, swap, after, out):
    right = rest[...]
    if half == 1:
        right = jnp.dot(right, swap[...], preferred_element_type=F32).astype(BF16)
    out[...] = jnp.dot(left[...], right, preferred_element_type=F32)


def product_tails(half, left, rest, after):
    lane = np.arange(256)
    swap = np.zeros((256, 256), np.float32)
    swap[lane, lane // 16 % 4 * 64 + lane // 64 * 16 + lane % 16] = 1.0
    vmem = pl.BlockSpec(memory_space=pltpu.VMEM)
    return pl.pallas_call(
        functools.partial(tails_kernel, half),
        in_specs=[vmem] * 3 + [pl.BlockSpec(memory_space=pl.ANY)],
        out_specs=vmem,
        out_shape=jax.ShapeDtypeStruct((ROWS[half], 256), F32),
        compiler_params=pltpu.CompilerParams(vmem_limit_bytes=12 * MIB),
        cost_estimate=pl.CostEstimate(flops=1000, bytes_accessed=1000, transcendentals=0),
        name="product_tails",
    )(left, rest, jnp.asarray(swap, BF16), after)


def padded(value, rows):
    if value.shape[0] == rows:
        return value
    return jnp.concatenate([value, jnp.zeros((rows - value.shape[0], 128), F32)], axis=0)


def lanes(rows):
    return lax.broadcasted_iota(jnp.int32, (rows, 128), 1)


def scale_of(most):
    power = jnp.floor(jnp.log2(jnp.maximum(jnp.full((1, 128), most, F32), 1e-30))) + 1.0
    return power, 32000.0 * jnp.exp2(-power)


def gain_of(coded):
    power = jnp.max(jnp.where(lanes(16) % 16 == 15, coded[0:16], -1000.0))
    return jnp.exp2(jnp.full((1, 128), power, F32)) * (1.0 / 32000.0)


def code(value, gain):
    return jnp.round(value * gain).astype(jnp.int32).astype(I16)


def code_tail(value, gain, power):
    coded = jnp.where(lanes(value.shape[0]) % 16 == 15, jnp.broadcast_to(power, value.shape), jnp.round(value * gain))
    return coded.astype(jnp.int32).astype(I16)


def plain(value):
    return value.astype(jnp.int32).astype(F32)


def product_kernel(half, d, spot, left, near, tails, after, out, held):
    rows = ROWS[half]
    coded = d != 0
    group = (spot[half] + d) % 4
    which = [4 * group + n if half == 0 else 4 * n + group for n in range(4)]
    for pair in range(2):
        both = jnp.dot(
            left[...],
            jnp.concatenate([near[which[2 * pair]], near[which[2 * pair + 1]]], axis=1),
            preferred_element_type=F32,
        )
        if coded:
            held[2 * pair] = both[:, :128]
            held[2 * pair + 1] = both[:, 128:]
        else:
            out[2 * pair * rows : (2 * pair + 1) * rows, :] = both[:, :128]
            out[(2 * pair + 1) * rows : (2 * pair + 2) * rows, :] = both[:, 128:]
    tail = jnp.where(group >= 2, tails[:, 128:], tails[:, :128])
    top = TOP[half]
    high, low = tail[:top], padded(tail[top:], top)
    odd = group % 2 == 1
    folded = jnp.where(
        lanes(top) < 64,
        jnp.where(odd, pltpu.roll(high, 64, 1), high),
        jnp.where(odd, low, pltpu.roll(low, 64, 1)),
    )
    if coded:
        power, gain = scale_of(jnp.maximum(jnp.max(jnp.abs(held[...])), jnp.max(jnp.abs(folded))))
        for n in range(4):
            out[n * rows : (n + 1) * rows, :] = code(held[n], gain)
        out[4 * rows : 4 * rows + TOP[half], :] = code_tail(folded, gain, power)
    else:
        out[4 * rows : 4 * rows + TOP[half], :] = folded


def product_group(half, d, spot, left, near, tails, after):
    rows = ROWS[half]
    coded = d != 0
    vmem = pl.BlockSpec(memory_space=pltpu.VMEM)
    return pl.pallas_call(
        functools.partial(product_kernel, half, d),
        in_specs=[pl.BlockSpec(memory_space=pltpu.SMEM)] + [vmem] * 3 + [pl.BlockSpec(memory_space=pl.ANY)],
        out_specs=vmem,
        out_shape=jax.ShapeDtypeStruct((4 * rows + TOP[half], 128), I16 if coded else F32),
        scratch_shapes=[pltpu.VMEM((4, rows, 128), F32)],
        compiler_params=pltpu.CompilerParams(vmem_limit_bytes=10 * MIB),
        cost_estimate=pl.CostEstimate(flops=1000, bytes_accessed=1000, transcendentals=0),
        name="product_coded" if coded else "product_own",
    )(spot, left, near, tails, after)


def merge_kernel(half, place, own, in1, in2, in3, after, mine, out1, out2, out3, held):
    rows, top, size = ROWS[half], TOP[half], FOLD[half]
    parts = (in1, in2, in3)
    tails = [plain(p[4 * rows : 4 * rows + top, :]) for p in parts]
    gains = [gain_of(t) for t in tails]
    for n in range(4):
        here = slice(n * rows, (n + 1) * rows)
        total = own[here, :]
        for p, g in zip(parts, gains):
            total = total + plain(p[here, :]) * g
        held[n] = total
    folded = own[4 * rows : 4 * rows + top, :]
    for t, g in zip(tails, gains):
        folded = folded + t * g
    pieces = [padded(folded[q * size : min(top, (q + 1) * size)], size) for q in range(4)]
    slot = lanes(size) // 16 % 4
    for s in range(4):

        @pl.when(place[1 - half] == s)
        def _(s=s):
            for d, out in enumerate((mine, out1, out2, out3)):
                here = (s + d) % 4
                tail = jnp.zeros((size, 128), F32)
                for q in range(4):
                    tail = jnp.where(slot == q, pltpu.roll(pieces[q], 16 * ((q - here) % 8), 1) if (q - here) % 8 else pieces[q], tail)
                main = held[here]
                if d == 0:
                    out[0:rows, :] = main
                    out[rows : rows + size, :] = tail
                else:
                    tail = jnp.where(lanes(size) % 16 < 10, tail, 0.0)
                    power, gain = scale_of(jnp.maximum(jnp.max(jnp.abs(main)), jnp.max(jnp.abs(tail))))
                    out[0:rows, :] = code(main, gain)
                    out[rows : rows + size, :] = code_tail(tail, gain, power)


def merge(half, place, own, parts, after):
    vmem = pl.BlockSpec(memory_space=pltpu.VMEM)
    return pl.pallas_call(
        functools.partial(merge_kernel, half),
        in_specs=[pl.BlockSpec(memory_space=pltpu.SMEM)] + [vmem] * 4 + [pl.BlockSpec(memory_space=pl.ANY)],
        out_specs=[vmem] * 4,
        out_shape=[jax.ShapeDtypeStruct((ROWS[half] + FOLD[half], 128), t) for t in (F32, I16, I16, I16)],
        scratch_shapes=[pltpu.VMEM((4, ROWS[half], 128), F32)],
        compiler_params=pltpu.CompilerParams(vmem_limit_bytes=12 * MIB),
        cost_estimate=pl.CostEstimate(flops=1000, bytes_accessed=1000, transcendentals=0),
        name="merge",
    )(place, own, *parts, after)


def turn(dy, dz):
    return [(4 * y + z, (y + dy) % 4 * 4 + (z + dz) % 4) for y in range(4) for z in range(4)]


def send(array, axis, d):
    return lax.ppermute(array, "col", turn(d, 0) if axis == 0 else turn(0, d))


def exchange_products(spot, blocks_a, pattern, blocks_b, before):
    blocks_a = jnp.transpose(blocks_a, (0, 2, 1, 3))
    near, rest = pack_right(jnp.transpose(blocks_b, (0, 2, 1, 3)), [spot] + before)
    after = near
    parts, owns = ([], []), []
    lefts = []
    for half in range(2):
        left = pack_left(half, pattern, blocks_a, after)
        tails = product_tails(half, left, rest, after)
        lefts.append((left, near, tails))
        after = tails
        for d in (1, 2, 3):
            last = product_group(half, d, spot, *lefts[half], after)
            parts[half].append(send(last, half, d))
        after = last
    for half in range(2):
        after = product_group(half, 0, spot, *lefts[half], after)
        owns.append(after)

    def finish(half, after):
        mine, *outs = merge(half, spot, owns[half], parts[half], after)
        return mine, [send(outs[d - 1], 1 - half, d) for d in (2, 1, 3)]

    return finish, after


def collocate_kernel(half, spot, keep, ids, own, in1, in2, in3, cols, rows, after, *rest):
    size = FOLD[half]
    before = rest[0] if half else None
    density, out, stacked, right, held, held_cols, sems = rest[half:]
    count = ROWS[half]
    tiles = 16384 // POINTS

    def copies(g):
        span = pl.ds(pl.multiple_of(g * POINTS, POINTS), POINTS)
        return (
            pltpu.make_async_copy(cols.at[0, :, span], held_cols.at[g], sems.at[0, g]),
            pltpu.make_async_copy(
                rows.at[pl.ds(CUT[half] // 8, count // 8), :, span], held.at[g], sems.at[1, g]
            ),
        )

    for g in range(tiles):
        for copy in copies(g):
            copy.start()

    def decode_density():
        main, fold = own[0:count, :], own[count : count + size, :]
        for part in (in1, in2, in3):
            extra = plain(part[count : count + size, :])
            gain = gain_of(extra)
            main, fold = main + plain(part[0:count, :]) * gain, fold + extra * gain
        tails = []
        for base, total in ((0, TOP[half]), (4, count - TOP[half])):
            for q in range(4):
                piece = fold[0 : min(size, total - q * size)]
                shift = (128 - 16 * (q + base)) % 128
                tails.append(pltpu.roll(piece, shift, 1) if shift else piece)
        tail = jnp.where(lanes(count) < BS - 128, jnp.concatenate(tails, axis=0), 0.0)
        row = lax.broadcasted_iota(jnp.int32, (8, 128), 0)
        kept = jnp.zeros((8, 128), F32)
        for i in range(8):
            kept = jnp.where(row == i, keep[i].astype(F32), kept)
        kept = kept[None]
        main = (main.reshape(count // 8, 8, 128) * kept).reshape(count, 128).astype(BF16)
        tail = (tail.reshape(count // 8, 8, 128) * kept).reshape(count, 128).astype(BF16)
        stacked[:, 0:128] = main
        stacked[:, 128:256] = tail
        density[:, :, 0:128] = main.reshape(count // 8, 8, 128)
        density[:, :, 128:BS] = tail.reshape(count // 8, 8, 128)[:, :, : BS - 128]
        right[128:256, :] = jnp.zeros((128, POINTS), BF16)

    decode_density()

    def step(g, carry):
        for copy in copies(g):
            copy.wait()
        right[0:BS, :] = held_cols[g]
        tile(g)
        return carry

    def tile(g):
        per = POINTS // 1024
        for t in range(POINTS // 256):
            here = slice(t * 256, (t + 1) * 256)
            inner = jnp.dot(stacked[...], right[:, here], preferred_element_type=F32).reshape(count // 8, 8, 256)
            total = jnp.sum(inner * held[g, :, :, here].astype(F32), axis=0)
            within = slice(t % 4 * 256, t % 4 * 256 + 256)
            if half == 1:
                total = total + before[per * g + t // 4, :, within]
            out[per * g + t // 4, :, within] = total
        if half == 1:
            row = lax.broadcasted_iota(jnp.int32, (8, 128), 0)
            label = jnp.zeros((8, 128), F32)
            for i in range(8):
                here = (row == 0) & (lanes(8) == 32 * spot[0] + 8 * spot[1] + i)
                label = jnp.where(here, ids[i].astype(F32), label)
            for n in range(POINTS // 1024):
                out[per * g + n, :, 1024:1152] = label

    lax.fori_loop(0, tiles, step, 0)


def collocate(half, spot, keep, ids, own, parts, basis_cols, basis_rows, before, after):
    count = ROWS[half]
    wide = 1152 if half else 1024
    vmem = pl.BlockSpec(memory_space=pltpu.VMEM)
    tiles = 16384 // POINTS
    return pl.pallas_call(
        functools.partial(collocate_kernel, half),
        in_specs=[pl.BlockSpec(memory_space=pltpu.SMEM)] * 3
        + [vmem] * 4
        + [pl.BlockSpec(memory_space=pltpu.HBM)] * 2
        + [pl.BlockSpec(memory_space=pl.ANY)]
        + [vmem] * half,
        out_specs=[vmem] * 2,
        scratch_shapes=[
            pltpu.VMEM((count, 256), BF16),
            pltpu.VMEM((256, POINTS), BF16),
            pltpu.VMEM((tiles, count // 8, 8, POINTS), BF16),
            pltpu.VMEM((tiles, BS, POINTS), BF16),
            pltpu.SemaphoreType.DMA((2, tiles)),
        ],
        out_shape=[
            jax.ShapeDtypeStruct((count // 8, 8, BS), BF16),
            jax.ShapeDtypeStruct((16, 8, wide), F32),
        ],
        compiler_params=pltpu.CompilerParams(vmem_limit_bytes=(38, 28)[half] * MIB),
        cost_estimate=pl.CostEstimate(flops=1000, bytes_accessed=1000, transcendentals=0),
        name="collocate",
    )(spot, keep, ids, own, *parts, in_hbm(basis_cols), in_hbm(basis_rows), after, *before)


def bricks_kernel(points, out):
    owners = jnp.sum(points[:, :, 1024:1152].reshape(128, 128), axis=0, keepdims=True).astype(jnp.int32)
    onehot = (owners == lax.broadcasted_iota(jnp.int32, (128, 128), 0)).astype(F32)
    held = points[:, :, 0:1024].reshape(128, 1024)
    out[...] = jnp.dot(onehot, held, precision=HIGH, preferred_element_type=F32)


def sum_bricks(points):
    return pl.pallas_call(
        bricks_kernel,
        out_shape=jax.ShapeDtypeStruct((128, 1024), F32),
        compiler_params=pltpu.CompilerParams(vmem_limit_bytes=8 * MIB),
        cost_estimate=pl.CostEstimate(flops=1000, bytes_accessed=1000, transcendentals=0),
        name="sum_bricks",
    )(points)


def tables():
    a = np.arange(16)
    outer = 2.0 * math.pi * (np.outer(a, a) % 16) / 16
    eye = np.eye(8)
    ck, sk = np.kron(eye, np.cos(outer)), np.kron(eye, np.sin(outer))
    b = np.arange(128)
    inner = 2.0 * math.pi * (np.outer(b, b) % 128) / 128
    c, s = np.cos(inner), np.sin(inner)
    twist = 2.0 * math.pi * np.outer(np.tile(a, 8), b) / 2048
    first = np.concatenate([ck, -sk], 0)
    second = np.block([[c, -s], [s, c]])
    third = np.block([[c, s], [-s, c]])
    last = np.concatenate([ck, -sk], 1) / 2048
    return [np.asarray(t, np.float32) for t in (first, second, third, last, np.cos(twist), np.sin(twist))]


def filter_kernel(own, in1, in2, in3, kern, first, second, third, last, tc, ts, out):
    def dot(p, q):
        return jnp.dot(p, q, precision=HIGH, preferred_element_type=F32)

    grid = (own[...] + in1[...]) + (in2[...] + in3[...])
    grid = jnp.concatenate([grid[:, y * 128 : y * 128 + 128] for y in range(8)], axis=0)
    section = dot(first[...], grid)
    re, im = section[:128], section[128:]
    c, s = tc[...], ts[...]
    spec = dot(jnp.concatenate([re * c + im * s, im * c - re * s], axis=1), second[...])
    k = kern[...]
    back = dot(spec * jnp.concatenate([k, k], axis=1), third[...])
    re, im = back[:, :128], back[:, 128:]
    turned = jnp.concatenate([re * c - im * s, im * c + re * s], axis=0)
    result = dot(last[...], turned)
    for y in range(8):
        out[:, y, :] = result[y * 16 : y * 16 + 16]


def filter_rows(pieces, kern):
    return pl.pallas_call(
        filter_kernel,
        out_shape=jax.ShapeDtypeStruct((16, 8, 128), F32),
        compiler_params=pltpu.CompilerParams(vmem_limit_bytes=8 * MIB),
        cost_estimate=pl.CostEstimate(flops=1000, bytes_accessed=1000, transcendentals=0),
        name="filter_rows",
    )(*pieces, kern, *tables())


def scatter_rows(partial):
    place = lax.axis_index("row")
    x, core = place // 2, place % 2
    halves = partial.reshape(4, 2, 16, 1024)
    away = lax.dynamic_index_in_dim(halves, 1 - core, 1, keepdims=False)
    mine = lax.dynamic_index_in_dim(halves, core, 1, keepdims=False)
    mine = mine + lax.ppermute(away, "row", [(r, r ^ 1) for r in range(8)])
    pieces = [lax.dynamic_index_in_dim(mine, x, 0, keepdims=False)]
    for d in (1, 2, 3):
        part = lax.dynamic_index_in_dim(mine, (x + d) % 4, 0, keepdims=False)
        pieces.append(lax.ppermute(part, "row", [(r, (r + 2 * d) % 8) for r in range(8)]))
    return pieces


def shards(blocks_a, pattern_a, blocks_b, filter_mask, task_brick, basis_rows, basis_cols, kernel):
    kern = jnp.transpose(kernel.reshape(8, 128, 16), (0, 2, 1)).reshape(128, 128)
    place = lax.axis_index("col").astype(jnp.int32)
    spot = jnp.stack([place // 4, place % 4])
    keep, ids = filter_mask.reshape(8), task_brick.reshape(8)
    by_point = jnp.transpose(basis_rows, (1, 0, 2))
    finish, after = exchange_products(spot, blocks_a, pattern_a, blocks_b, [kern])
    densities, before, sums = [], [], []
    for half in range(2):
        sums.append(finish(half, after))
        after = sums[half][0]
    for half in range(2):
        own, parts = sums[half]
        density, after = collocate(
            half, spot, keep, ids, own, parts, basis_cols, by_point, before, after
        )
        densities.append(density)
        before = [after]
    points = after
    points = lax.all_to_all(points, "col", split_axis=0, concat_axis=0, tiled=True)
    pieces = scatter_rows(sum_bricks(points))
    filtered = filter_rows(pieces, kern)
    potential = lax.all_to_all(filtered, "col", split_axis=0, concat_axis=0, tiled=True)
    density = jnp.transpose(jnp.concatenate(densities, axis=0), (1, 0, 2))
    return density[:, None], potential.reshape(128, 128)


def solution(mesh):
    return jax.shard_map(
        shards,
        mesh=mesh,
        in_specs=(
            P("row", "col", None, None),
            P("row", "col"),
            P("col", None, None, None),
            P("row", "col"),
            P("row", "col"),
            P("row", None, None),
            P("col", None, None),
            P(("row", "col"), None),
        ),
        out_specs=(P("row", "col", None, None), P("row", "col")),
        check_vma=False,
    )
```

```python
import functools
import math

import jax
import jax.numpy as jnp
import numpy as np
from jax import lax
from jax.experimental import pallas as pl
from jax.experimental.pallas import tpu as pltpu
from jax.sharding import PartitionSpec as P

BS = 138
MIB = 1 << 20
HIGH = lax.Precision.HIGHEST
F32 = jnp.float32
BF16 = jnp.bfloat16
I16 = jnp.int16
WIDE = 2304
SPAN = 1152
ROWS = (672, 432)
CUT = (0, 672)
TOP = (336, 224)
FOLD = (96, 64)
STEP = (28, 18)
POINTS = 2048


def in_hbm(array):
    return pltpu.with_memory_space_constraint(array, pltpu.HBM)


def widen(tail):
    return jnp.concatenate([tail.astype(F32), jnp.zeros(tail.shape[:-1] + (128 - tail.shape[-1],), F32)], axis=-1)


def place_tails(tails, out, rows):
    lane = lax.broadcasted_iota(jnp.int32, (16, 128), 1) // 16
    for half in range(2):
        rest = jnp.zeros((16, 128), F32)
        for n in range(8):
            tail = tails[half * 8 + n]
            rest = jnp.where(lane == n, pltpu.roll(tail, 16 * n, 1) if n else tail, rest)
        out(half, rest.astype(BF16))


def pack_left_kernel(pairs, pattern, blocks, after, out, mask):
    @pl.when(pl.program_id(0) == 0)
    def _():
        kept = pattern[...].astype(F32)
        for k in range(16):
            column = jnp.broadcast_to(kept[:, k : k + 1], (8, 128))
            mask[k] = jnp.concatenate([column, column], axis=0).astype(BF16)

    def step(p, carry):
        pair = jnp.transpose(blocks[:, pl.ds(2 * p, 2)], (1, 0, 2, 3)).reshape(16, 16, BS)
        wide = jnp.swapaxes(pair, 0, 1)
        rows = pl.ds(pl.multiple_of(16 * p, 16), 16)
        tails = []
        for k in range(16):
            at = SPAN * (k // 8) + 128 * (k % 8)
            out[rows, at : at + 128] = wide[k, :, :128] * mask[k]
            tails.append(widen(wide[k, :, 128:] * mask[k, :, : BS - 128]))

        def put(half, value):
            out[rows, SPAN * half + 1024 : SPAN * half + 1152] = value

        place_tails(tails, put, rows)
        return carry

    lax.fori_loop(0, pairs, step, 0)


def pack_left(half, pattern, blocks, after):
    count = STEP[half]
    return pl.pallas_call(
        functools.partial(pack_left_kernel, count // 2),
        grid=(ROWS[half] // 8 // count,),
        in_specs=[
            pl.BlockSpec((8, 16), lambda g: (0, 0)),
            pl.BlockSpec(
                (pl.Element(8), pl.Element(count), pl.Element(16), pl.Element(BS)),
                lambda g: (0, CUT[half] // 8 + count * g, 0, 0),
            ),
            pl.BlockSpec(memory_space=pl.ANY),
        ],
        out_specs=pl.BlockSpec((count * 8, WIDE), lambda g: (g, 0)),
        out_shape=pltpu.VMEM((ROWS[half], WIDE), BF16),
        scratch_shapes=[pltpu.VMEM((16, 16, 128), BF16)],
        compiler_params=pltpu.CompilerParams(vmem_limit_bytes=32 * MIB),
        cost_estimate=pl.CostEstimate(flops=1000, bytes_accessed=1000, transcendentals=0),
        name="pack_left",
    )(pattern, in_hbm(blocks), after)


def pack_right_kernel(blocks, *others):
    near, rest = others[-2:]
    base = pl.program_id(0) % 4 * 2

    def step(n, carry):
        k = base + n
        for c in range(0, 144, 16):
            if c < 128:
                rows = pl.ds(pl.multiple_of(128 * k + c, 16), 16)
                square = blocks[n, c : c + 16]
            else:
                rows = pl.ds(pl.multiple_of(1024 + 16 * k, 16), 16)
                square = jnp.concatenate([blocks[n, 128:BS], jnp.zeros((144 - BS, 16, BS), BF16)], axis=0)
            turned = jnp.swapaxes(square, 0, 1)
            near[:, rows, :] = turned[:, :, :128]

            def put(half, value, rows=rows):
                rest[rows, 128 * half : 128 * half + 128] = value

            place_tails([widen(turned[j, :, 128:]) for j in range(16)], put, rows)
        return carry

    lax.fori_loop(0, 2, step, 0)


def pack_right(blocks, before):
    return pl.pallas_call(
        pack_right_kernel,
        grid=(8,),
        in_specs=[pl.BlockSpec((2, BS, 16, BS), lambda g: (g, 0, 0, 0))]
        + [pl.BlockSpec(memory_space=pl.ANY)] * len(before),
        out_specs=[
            pl.BlockSpec((16, SPAN, 128), lambda g: (0, g // 4, 0)),
            pl.BlockSpec((SPAN, 256), lambda g: (g // 4, 0)),
        ],
        out_shape=[
            pltpu.VMEM((16, WIDE, 128), BF16),
            pltpu.VMEM((WIDE, 256), BF16),
        ],
        compiler_params=pltpu.CompilerParams(vmem_limit_bytes=24 * MIB),
        cost_estimate=pl.CostEstimate(flops=1000, bytes_accessed=1000, transcendentals=0),
        name="pack_right",
    )(in_hbm(blocks), *before)


def tails_kernel(half, left, rest, swap, after, out):
    right = rest[...]
    if half == 1:
        right = jnp.dot(right, swap[...], preferred_element_type=F32).astype(BF16)
    out[...] = jnp.dot(left[...], right, preferred_element_type=F32)


def product_tails(half, left, rest, after):
    lane = np.arange(256)
    swap = np.zeros((256, 256), np.float32)
    swap[lane, lane // 16 % 4 * 64 + lane // 64 * 16 + lane % 16] = 1.0
    vmem = pl.BlockSpec(memory_space=pltpu.VMEM)
    return pl.pallas_call(
        functools.partial(tails_kernel, half),
        in_specs=[vmem] * 3 + [pl.BlockSpec(memory_space=pl.ANY)],
        out_specs=vmem,
        out_shape=jax.ShapeDtypeStruct((ROWS[half], 256), F32),
        compiler_params=pltpu.CompilerParams(vmem_limit_bytes=12 * MIB),
        cost_estimate=pl.CostEstimate(flops=1000, bytes_accessed=1000, transcendentals=0),
        name="product_tails",
    )(left, rest, jnp.asarray(swap, BF16), after)


def padded(value, rows):
    if value.shape[0] == rows:
        return value
    return jnp.concatenate([value, jnp.zeros((rows - value.shape[0], 128), F32)], axis=0)


def lanes(rows):
    return lax.broadcasted_iota(jnp.int32, (rows, 128), 1)


def scale_of(most):
    power = jnp.floor(jnp.log2(jnp.maximum(jnp.full((1, 128), most, F32), 1e-30))) + 1.0
    return power, 32000.0 * jnp.exp2(-power)


def gain_of(coded):
    power = jnp.max(jnp.where(lanes(16) % 16 == 15, coded[0:16], -1000.0))
    return jnp.exp2(jnp.full((1, 128), power, F32)) * (1.0 / 32000.0)


def code(value, gain):
    return jnp.round(value * gain).astype(jnp.int32).astype(I16)


def code_tail(value, gain, power):
    coded = jnp.where(lanes(value.shape[0]) % 16 == 15, jnp.broadcast_to(power, value.shape), jnp.round(value * gain))
    return coded.astype(jnp.int32).astype(I16)


def plain(value):
    return value.astype(jnp.int32).astype(F32)


def product_kernel(half, d, spot, left, near, tails, after, out, held):
    rows = ROWS[half]
    coded = d != 0
    group = (spot[half] + d) % 4
    which = [4 * group + n if half == 0 else 4 * n + group for n in range(4)]
    for pair in range(2):
        both = jnp.dot(
            left[...],
            jnp.concatenate([near[which[2 * pair]], near[which[2 * pair + 1]]], axis=1),
            preferred_element_type=F32,
        )
        if coded:
            held[2 * pair] = both[:, :128]
            held[2 * pair + 1] = both[:, 128:]
        else:
            out[2 * pair * rows : (2 * pair + 1) * rows, :] = both[:, :128]
            out[(2 * pair + 1) * rows : (2 * pair + 2) * rows, :] = both[:, 128:]
    tail = jnp.where(group >= 2, tails[:, 128:], tails[:, :128])
    top = TOP[half]
    high, low = tail[:top], padded(tail[top:], top)
    odd = group % 2 == 1
    folded = jnp.where(
        lanes(top) < 64,
        jnp.where(odd, pltpu.roll(high, 64, 1), high),
        jnp.where(odd, low, pltpu.roll(low, 64, 1)),
    )
    if coded:
        power, gain = scale_of(jnp.maximum(jnp.max(jnp.abs(held[...])), jnp.max(jnp.abs(folded))))
        for n in range(4):
            out[n * rows : (n + 1) * rows, :] = code(held[n], gain)
        out[4 * rows : 4 * rows + TOP[half], :] = code_tail(folded, gain, power)
    else:
        out[4 * rows : 4 * rows + TOP[half], :] = folded


def product_group(half, d, spot, left, near, tails, after):
    rows = ROWS[half]
    coded = d != 0
    vmem = pl.BlockSpec(memory_space=pltpu.VMEM)
    return pl.pallas_call(
        functools.partial(product_kernel, half, d),
        in_specs=[pl.BlockSpec(memory_space=pltpu.SMEM)] + [vmem] * 3 + [pl.BlockSpec(memory_space=pl.ANY)],
        out_specs=vmem,
        out_shape=jax.ShapeDtypeStruct((4 * rows + TOP[half], 128), I16 if coded else F32),
        scratch_shapes=[pltpu.VMEM((4, rows, 128), F32)],
        compiler_params=pltpu.CompilerParams(vmem_limit_bytes=10 * MIB),
        cost_estimate=pl.CostEstimate(flops=1000, bytes_accessed=1000, transcendentals=0),
        name="product_coded" if coded else "product_own",
    )(spot, left, near, tails, after)


def merge_kernel(half, place, own, in1, in2, in3, after, mine, out1, out2, out3, held):
    rows, top, size = ROWS[half], TOP[half], FOLD[half]
    parts = (in1, in2, in3)
    tails = [plain(p[4 * rows : 4 * rows + top, :]) for p in parts]
    gains = [gain_of(t) for t in tails]
    for n in range(4):
        here = slice(n * rows, (n + 1) * rows)
        total = own[here, :]
        for p, g in zip(parts, gains):
            total = total + plain(p[here, :]) * g
        held[n] = total
    folded = own[4 * rows : 4 * rows + top, :]
    for t, g in zip(tails, gains):
        folded = folded + t * g
    pieces = [padded(folded[q * size : min(top, (q + 1) * size)], size) for q in range(4)]
    slot = lanes(size) // 16 % 4
    for s in range(4):

        @pl.when(place[1 - half] == s)
        def _(s=s):
            for d, out in enumerate((mine, out1, out2, out3)):
                here = (s + d) % 4
                tail = jnp.zeros((size, 128), F32)
                for q in range(4):
                    tail = jnp.where(slot == q, pltpu.roll(pieces[q], 16 * ((q - here) % 8), 1) if (q - here) % 8 else pieces[q], tail)
                main = held[here]
                if d == 0:
                    out[0:rows, :] = main
                    out[rows : rows + size, :] = tail
                else:
                    tail = jnp.where(lanes(size) % 16 < 10, tail, 0.0)
                    power, gain = scale_of(jnp.maximum(jnp.max(jnp.abs(main)), jnp.max(jnp.abs(tail))))
                    out[0:rows, :] = code(main, gain)
                    out[rows : rows + size, :] = code_tail(tail, gain, power)


def merge(half, place, own, parts, after):
    vmem = pl.BlockSpec(memory_space=pltpu.VMEM)
    return pl.pallas_call(
        functools.partial(merge_kernel, half),
        in_specs=[pl.BlockSpec(memory_space=pltpu.SMEM)] + [vmem] * 4 + [pl.BlockSpec(memory_space=pl.ANY)],
        out_specs=[vmem] * 4,
        out_shape=[jax.ShapeDtypeStruct((ROWS[half] + FOLD[half], 128), t) for t in (F32, I16, I16, I16)],
        scratch_shapes=[pltpu.VMEM((4, ROWS[half], 128), F32)],
        compiler_params=pltpu.CompilerParams(vmem_limit_bytes=12 * MIB),
        cost_estimate=pl.CostEstimate(flops=1000, bytes_accessed=1000, transcendentals=0),
        name="merge",
    )(place, own, *parts, after)


def turn(dy, dz):
    return [(4 * y + z, (y + dy) % 4 * 4 + (z + dz) % 4) for y in range(4) for z in range(4)]


def send(array, axis, d):
    return lax.ppermute(array, "col", turn(d, 0) if axis == 0 else turn(0, d))


def exchange_products(spot, blocks_a, pattern, blocks_b, before):
    blocks_a = jnp.transpose(blocks_a, (0, 2, 1, 3))
    near, rest = pack_right(jnp.transpose(blocks_b, (0, 2, 1, 3)), [spot] + before)
    after = near
    parts, owns = ([], []), []
    lefts = []
    for half in range(2):
        left = pack_left(half, pattern, blocks_a, after)
        tails = product_tails(half, left, rest, after)
        lefts.append((left, near, tails))
        after = tails
        for d in (1, 2, 3):
            last = product_group(half, d, spot, *lefts[half], after)
            parts[half].append(send(last, half, d))
        after = last
    for half in range(2):
        after = product_group(half, 0, spot, *lefts[half], after)
        owns.append(after)

    def finish(half, after):
        mine, *outs = merge(half, spot, owns[half], parts[half], after)
        return mine, [send(outs[d - 1], 1 - half, d) for d in (2, 1, 3)]

    return finish, after


def collocate_kernel(half, spot, keep, ids, own, in1, in2, in3, cols, rows, after, *rest):
    size = FOLD[half]
    if half == 0:
        density, out, held_cols, stacked, right, held, sems = rest
    else:
        before, held_cols, density, out, stacked, right, held, sems = rest
    count = ROWS[half]
    tiles = 16384 // POINTS

    def copies(g):
        span = pl.ds(pl.multiple_of(g * POINTS, POINTS), POINTS)
        planes = rows.at[pl.ds(CUT[half] // 8, count // 8), :, span]
        fetched = [pltpu.make_async_copy(planes, held.at[g], sems.at[1, g])]
        if half == 0:
            fetched.append(pltpu.make_async_copy(cols.at[0, :, span], held_cols.at[g], sems.at[0, g]))
        return fetched

    for g in range(tiles):
        for copy in copies(g):
            copy.start()

    def decode_density():
        main, fold = own[0:count, :], own[count : count + size, :]
        for part in (in1, in2, in3):
            extra = plain(part[count : count + size, :])
            gain = gain_of(extra)
            main, fold = main + plain(part[0:count, :]) * gain, fold + extra * gain
        tails = []
        for base, total in ((0, TOP[half]), (4, count - TOP[half])):
            for q in range(4):
                piece = fold[0 : min(size, total - q * size)]
                shift = (128 - 16 * (q + base)) % 128
                tails.append(pltpu.roll(piece, shift, 1) if shift else piece)
        tail = jnp.where(lanes(count) < BS - 128, jnp.concatenate(tails, axis=0), 0.0)
        row = lax.broadcasted_iota(jnp.int32, (8, 128), 0)
        kept = jnp.zeros((8, 128), F32)
        for i in range(8):
            kept = jnp.where(row == i, keep[i].astype(F32), kept)
        kept = kept[None]
        main = (main.reshape(count // 8, 8, 128) * kept).reshape(count, 128).astype(BF16)
        tail = (tail.reshape(count // 8, 8, 128) * kept).reshape(count, 128).astype(BF16)
        stacked[:, 0:128] = main
        stacked[:, 128:256] = tail
        density[:, :, 0:128] = main.reshape(count // 8, 8, 128)
        density[:, :, 128:BS] = tail.reshape(count // 8, 8, 128)[:, :, : BS - 128]
        right[128:256, :] = jnp.zeros((128, POINTS), BF16)

    decode_density()

    def step(g, carry):
        for copy in copies(g):
            copy.wait()
        right[0:BS, :] = held_cols[g]
        tile(g)
        return carry

    def tile(g):
        per = POINTS // 1024
        for t in range(POINTS // 256):
            here = slice(t * 256, (t + 1) * 256)
            inner = jnp.dot(stacked[...], right[:, here], preferred_element_type=F32).reshape(count // 8, 8, 256)
            total = jnp.sum(inner * held[g, :, :, here].astype(F32), axis=0)
            within = slice(t % 4 * 256, t % 4 * 256 + 256)
            if half == 1:
                total = total + before[per * g + t // 4, :, within]
            out[per * g + t // 4, :, within] = total
        if half == 1:
            row = lax.broadcasted_iota(jnp.int32, (8, 128), 0)
            label = jnp.zeros((8, 128), F32)
            for i in range(8):
                here = (row == 0) & (lanes(8) == 32 * spot[0] + 8 * spot[1] + i)
                label = jnp.where(here, ids[i].astype(F32), label)
            for n in range(POINTS // 1024):
                out[per * g + n, :, 1024:1152] = label

    lax.fori_loop(0, tiles, step, 0)


def collocate(half, spot, keep, ids, own, parts, basis_cols, basis_rows, before, after):
    count = ROWS[half]
    wide = 1152 if half else 1024
    vmem = pl.BlockSpec(memory_space=pltpu.VMEM)
    tiles = 16384 // POINTS
    return pl.pallas_call(
        functools.partial(collocate_kernel, half),
        in_specs=[pl.BlockSpec(memory_space=pltpu.SMEM)] * 3
        + [vmem] * 4
        + [pl.BlockSpec(memory_space=pltpu.HBM)] * 2
        + [pl.BlockSpec(memory_space=pl.ANY)]
        + [vmem] * (2 * half),
        out_specs=[vmem] * (3 - half),
        scratch_shapes=[
            pltpu.VMEM((count, 256), BF16),
            pltpu.VMEM((256, POINTS), BF16),
            pltpu.VMEM((tiles, count // 8, 8, POINTS), BF16),
            pltpu.SemaphoreType.DMA((2, tiles)),
        ],
        out_shape=[
            jax.ShapeDtypeStruct((count // 8, 8, BS), BF16),
            jax.ShapeDtypeStruct((16, 8, wide), F32),
        ]
        + [pltpu.VMEM((tiles, BS, POINTS), BF16)] * (1 - half),
        compiler_params=pltpu.CompilerParams(vmem_limit_bytes=(38, 28)[half] * MIB),
        cost_estimate=pl.CostEstimate(flops=1000, bytes_accessed=1000, transcendentals=0),
        name="collocate",
    )(spot, keep, ids, own, *parts, in_hbm(basis_cols), in_hbm(basis_rows), after, *before)


def bricks_kernel(points, out):
    owners = jnp.sum(points[:, :, 1024:1152].reshape(128, 128), axis=0, keepdims=True).astype(jnp.int32)
    onehot = (owners == lax.broadcasted_iota(jnp.int32, (128, 128), 0)).astype(F32)
    held = points[:, :, 0:1024].reshape(128, 1024)
    out[...] = jnp.dot(onehot, held, precision=HIGH, preferred_element_type=F32)


def sum_bricks(points):
    return pl.pallas_call(
        bricks_kernel,
        out_shape=jax.ShapeDtypeStruct((128, 1024), F32),
        compiler_params=pltpu.CompilerParams(vmem_limit_bytes=8 * MIB),
        cost_estimate=pl.CostEstimate(flops=1000, bytes_accessed=1000, transcendentals=0),
        name="sum_bricks",
    )(points)


def tables():
    a = np.arange(16)
    outer = 2.0 * math.pi * (np.outer(a, a) % 16) / 16
    eye = np.eye(8)
    ck, sk = np.kron(eye, np.cos(outer)), np.kron(eye, np.sin(outer))
    b = np.arange(128)
    inner = 2.0 * math.pi * (np.outer(b, b) % 128) / 128
    c, s = np.cos(inner), np.sin(inner)
    twist = 2.0 * math.pi * np.outer(np.tile(a, 8), b) / 2048
    first = np.concatenate([ck, -sk], 0)
    second = np.block([[c, -s], [s, c]])
    third = np.block([[c, s], [-s, c]])
    last = np.concatenate([ck, -sk], 1) / 2048
    return [np.asarray(t, np.float32) for t in (first, second, third, last, np.cos(twist), np.sin(twist))]


def filter_kernel(own, in1, in2, in3, kern, first, second, third, last, tc, ts, out):
    def dot(p, q):
        return jnp.dot(p, q, precision=HIGH, preferred_element_type=F32)

    grid = (own[...] + in1[...]) + (in2[...] + in3[...])
    grid = jnp.concatenate([grid[:, y * 128 : y * 128 + 128] for y in range(8)], axis=0)
    section = dot(first[...], grid)
    re, im = section[:128], section[128:]
    c, s = tc[...], ts[...]
    spec = dot(jnp.concatenate([re * c + im * s, im * c - re * s], axis=1), second[...])
    k = kern[...]
    back = dot(spec * jnp.concatenate([k, k], axis=1), third[...])
    re, im = back[:, :128], back[:, 128:]
    turned = jnp.concatenate([re * c - im * s, im * c + re * s], axis=0)
    result = dot(last[...], turned)
    for y in range(8):
        out[:, y, :] = result[y * 16 : y * 16 + 16]


def filter_rows(pieces, kern):
    return pl.pallas_call(
        filter_kernel,
        out_shape=jax.ShapeDtypeStruct((16, 8, 128), F32),
        compiler_params=pltpu.CompilerParams(vmem_limit_bytes=8 * MIB),
        cost_estimate=pl.CostEstimate(flops=1000, bytes_accessed=1000, transcendentals=0),
        name="filter_rows",
    )(*pieces, kern, *tables())


def scatter_rows(partial):
    place = lax.axis_index("row")
    x, core = place // 2, place % 2
    halves = partial.reshape(4, 2, 16, 1024)
    away = lax.dynamic_index_in_dim(halves, 1 - core, 1, keepdims=False)
    mine = lax.dynamic_index_in_dim(halves, core, 1, keepdims=False)
    mine = mine + lax.ppermute(away, "row", [(r, r ^ 1) for r in range(8)])
    pieces = [lax.dynamic_index_in_dim(mine, x, 0, keepdims=False)]
    for d in (1, 2, 3):
        part = lax.dynamic_index_in_dim(mine, (x + d) % 4, 0, keepdims=False)
        pieces.append(lax.ppermute(part, "row", [(r, (r + 2 * d) % 8) for r in range(8)]))
    return pieces


def shards(blocks_a, pattern_a, blocks_b, filter_mask, task_brick, basis_rows, basis_cols, kernel):
    kern = jnp.transpose(kernel.reshape(8, 128, 16), (0, 2, 1)).reshape(128, 128)
    place = lax.axis_index("col").astype(jnp.int32)
    spot = jnp.stack([place // 4, place % 4])
    keep, ids = filter_mask.reshape(8), task_brick.reshape(8)
    by_point = jnp.transpose(basis_rows, (1, 0, 2))
    finish, after = exchange_products(spot, blocks_a, pattern_a, blocks_b, [kern])
    densities, before, sums = [], [], []
    for half in range(2):
        sums.append(finish(half, after))
        after = sums[half][0]
    for half in range(2):
        own, parts = sums[half]
        density, after, *held = collocate(
            half, spot, keep, ids, own, parts, basis_cols, by_point, before, after
        )
        densities.append(density)
        before = [after] + held
    points = after
    points = lax.all_to_all(points, "col", split_axis=0, concat_axis=0, tiled=True)
    pieces = scatter_rows(sum_bricks(points))
    filtered = filter_rows(pieces, kern)
    potential = lax.all_to_all(filtered, "col", split_axis=0, concat_axis=0, tiled=True)
    density = jnp.transpose(jnp.concatenate(densities, axis=0), (1, 0, 2))
    return density[:, None], potential.reshape(128, 128)


def solution(mesh):
    return jax.shard_map(
        shards,
        mesh=mesh,
        in_specs=(
            P("row", "col", None, None),
            P("row", "col"),
            P("col", None, None, None),
            P("row", "col"),
            P("row", "col"),
            P("row", None, None),
            P("col", None, None),
            P(("row", "col"), None),
        ),
        out_specs=(P("row", "col", None, None), P("row", "col")),
        check_vma=False,
    )
```
